32 devices in a mesh: groups: 2 (over x), owner: 8 (over z, y), slab: 2 (over core).
Axes of the slice: x: 2, y: 2, z: 4, core: 2. Of those that a mesh axis runs over, the one named last changes fastest.
Arguments:
- queries: bfloat16 [16, 4, 112, 2560], P(('groups', 'owner'), 'slab'), parts along dimension 0, may hold values from -40 to 40
- key_value: bfloat16 [2, 16, 4, 112, 2560], P(None, ('groups', 'owner'), 'slab'), parts along dimension 1, may hold values from -8 to 8
- keep: int32 [8], P('groups'), parts along dimension 0, may hold values 0 or 1
- windows: int32 [8, 3], P('groups'), parts along dimension 0, may hold values from 0 to 7, as said below
- gate: float32 [8, 5120], P('groups'), parts along dimension 0, may hold values from -1.5 to 1.5
- out_weight: bfloat16 [2560, 5120], P('owner'), may hold values from -0.125 to 0.125
Outputs:
- output: bfloat16 [16, 4, 112, 5120], P(('groups', 'owner'), 'slab'), parts along dimension 0
The draws below stay inside these ranges and needn't reach their ends.
There are 2 independent parts, one for each index of `groups`. The reference program is written for one: setup_inputs(seed, part) draws one part's arguments, and reference() takes and returns one part's arrays. A program takes and returns all parts, laid end to end along the dimension named above; an argument that names none is the same for every part. Nothing has to cross between parts.
Inputs may be any that keep to these rules, and one draw needn't show every extreme that they name: `windows`: column 0 runs from 0 to 1, column 1 from 1 to 4, column 2 from 1 to 7; the first request takes the largest value of each column.
All inputs are finite; a program needn't handle non-finite values.
Results may differ from the reference program's by a relative error of at most 0.0057.
Values may be sent and summed in bfloat16 or wider, within the bound.
No kernel may reach another device: no remote copies, remote signals or barrier semaphores. Data moves between devices by JAX's collectives and lax.ppermute only.
A program may use at most 128 MiB of HBM per device.

```python
import math
import jax
import jax.numpy as jnp
from jax import lax

D = 5120
HEADS = 20
HEAD_DIM = 128
HH = 2560
HB = 8
WB = 14
HALO = 1
SP = 112
FRAMES = 4
STREAMS = 8
REQUESTS = 4


def key_base(key):
    shape = (STREAMS, FRAMES, SP, HH)
    base_key = jax.random.fold_in(key, 11)
    raw = jnp.clip(jax.random.normal(base_key, shape, jnp.float32), -6.0, 6.0)
    return raw


def draw_key_value(key, part):
    shape = (STREAMS, FRAMES, SP, HH)
    raw = key_base(key)
    keys = raw
    values = jnp.clip(jax.random.normal(jax.random.fold_in(key, 13), shape, jnp.float32), -6.0, 6.0)
    return jnp.stack([keys, values], axis=0).astype(jnp.bfloat16)


def draw_queries(key, part):
    shape = (STREAMS, FRAMES, SP, HH)
    result = jnp.clip(jax.random.normal(jax.random.fold_in(key, 14), shape, jnp.float32), -6.0, 6.0)
    return result.astype(jnp.bfloat16)


def draw_windows(key, part):
    depth = jax.random.randint(jax.random.fold_in(key, 21), (REQUESTS,), 0, HALO + 1)
    height = jax.random.randint(jax.random.fold_in(key, 22), (REQUESTS,), 1, HB // 2 + 1)
    breadth = jax.random.randint(jax.random.fold_in(key, 23), (REQUESTS,), 1, WB // 2 + 1)
    leading = jnp.arange(REQUESTS, dtype=jnp.int32) == 0
    depth = jnp.where(leading, HALO, depth)
    height = jnp.where(leading, HB // 2, height)
    breadth = jnp.where(leading, WB // 2, breadth)
    return jnp.stack([depth, height, breadth], axis=1).astype(jnp.int32)


def set_ends(entries, rng, smallest, top_value):
    longest = entries.shape.index(max(entries.shape))
    spots = []
    for shift in (0, 1):
        where = [jax.random.randint(jax.random.fold_in(rng, axis), (), 0, length) for axis, length in enumerate(entries.shape)]
        where[longest] = (where[longest] + shift) % entries.shape[longest]
        spots.append(tuple(where))
    return entries.at[spots[0]].set(smallest).at[spots[1]].set(top_value)


def levels(own_key, extent, shards, smallest, high):
    def one(axis_at, shards_of):
        heights = jax.random.uniform(jax.random.fold_in(jax.random.fold_in(own_key, 6), axis_at), (shards_of,), jnp.float32, smallest / len(shards), high / len(shards))
        return jnp.repeat(jnp.exp(heights), extent[axis_at] // shards_of).reshape((-1,) + (1,) * (len(extent) - axis_at - 1))

    level = one(*shards[0])
    for cut in shards[1:]:
        level = level * one(*cut)
    return level


def bell_draw(own_key, shape, scale, most, pieces=(), held_as=jnp.bfloat16):
    factor_of = levels(own_key, shape, pieces, -0.22, 0.18) if pieces else 1.0
    values = jax.random.normal(own_key, shape, jnp.float32) * scale * factor_of
    return jnp.minimum(jnp.maximum(values, -most), most).astype(held_as)


def setup_inputs(seed: int = 0, part: int = 0) -> dict:
    key_of = jax.random.split(jax.random.key(seed), 7)
    part_splits = jax.random.split(jax.random.fold_in(key_of[6], part), 7)
    queries = draw_queries(jax.random.fold_in(jax.random.fold_in(key_of[6], part), 71), part)
    key_value = draw_key_value(jax.random.fold_in(jax.random.fold_in(key_of[6], part), 71), part)
    keep = set_ends((jax.random.randint(part_splits[2], (REQUESTS,), 0, 2) < 1).astype(jnp.int32), jax.random.fold_in(part_splits[2], 1), 0, 1)
    windows = draw_windows(jax.random.fold_in(jax.random.fold_in(key_of[6], part), 71), part)
    gate = jnp.clip(jax.random.uniform(part_splits[4], (REQUESTS, D), jnp.float32, -1.5, 1.5), -1.5, 1.5)
    out_weight = bell_draw(key_of[5], (HH, D), HH ** -0.5, 0.125, ((0, 8),))
    return dict(queries=queries, key_value=key_value, keep=keep, windows=windows, gate=gate, out_weight=out_weight)


NEG_LARGE = -1e+30

def attend(query_rows, key_rows, value_rows, allowed):
    query_count = query_rows.shape[0]
    key_count = key_rows.shape[0]
    query_heads = query_rows.astype(jnp.float32).reshape(query_count, HEADS, HEAD_DIM)
    key_heads = key_rows.astype(jnp.float32).reshape(key_count, HEADS, HEAD_DIM)
    value_heads = value_rows.astype(jnp.float32).reshape(key_count, HEADS, HEAD_DIM)
    scores = jnp.einsum('qhd,khd->hqk', query_heads, key_heads) * (1.0 / math.sqrt(HEAD_DIM))
    scores = jnp.where(allowed[None], scores, NEG_LARGE)
    highest = lax.optimization_barrier(jnp.max(scores, axis=-1, keepdims=True))
    exponent = jnp.exp(scores - highest)
    totals = lax.optimization_barrier(jnp.sum(exponent, axis=-1, keepdims=True))
    weights = (exponent / totals).astype(jnp.bfloat16)
    mixture = jnp.einsum('hqk,khd->qhd', weights.astype(jnp.float32), value_heads)
    return mixture.astype(jnp.bfloat16).reshape(query_count, HEADS * HEAD_DIM)

def reference(queries, key_value, keep, windows, gate, out_weight):
    tokens = FRAMES * SP
    token_ids = jnp.arange(tokens, dtype=jnp.int32)
    frame_of = token_ids // SP
    row_of = token_ids % SP // WB
    column_of = token_ids % SP % WB

    def one_stream(index):
        request = index // 2
        branch = index % 2
        window = windows[request]
        allowed = jnp.abs(frame_of[:, None] - frame_of[None, :]) <= window[0]
        allowed = allowed & (jnp.abs(row_of[:, None] - row_of[None, :]) <= window[1])
        allowed = allowed & (jnp.abs(column_of[:, None] - column_of[None, :]) <= window[2])
        query_rows = queries[index].reshape(tokens, HH)
        key_rows = key_value[0, index].reshape(tokens, HH)
        value_rows = key_value[1, index].reshape(tokens, HH)
        attended = attend(query_rows, key_rows, value_rows, allowed)
        product = jnp.dot(attended, out_weight, preferred_element_type=jnp.float32)
        factor = jnp.where(branch == 1, keep[request], 1).astype(jnp.float32)
        result = product * gate[request][None, :] * factor
        return result.astype(jnp.bfloat16).reshape(FRAMES, SP, D)
    return lax.map(one_stream, jnp.arange(STREAMS, dtype=jnp.int32))
```

```python
import functools
import math

import jax
import jax.numpy as jnp
from jax import lax
from jax.experimental import pallas as pl
from jax.experimental.pallas import tpu as pltpu
from jax.sharding import PartitionSpec as P

HEAD_DIM = 128
WB = 14
HALO = 1
NEG_LARGE = -1e30
PIECES = 2
PARTS = 2
VMEM_BYTES = 48 * 1024 * 1024


def ring_order(count):
    width = max(w for w in range(1, count + 1) if count % w == 0 and w * w <= count)
    height = count // width
    if width == 1 or height % 2:
        return list(range(count))
    order = []
    for row in range(height):
        columns = range(1, width) if row % 2 == 0 else range(width - 1, 0, -1)
        order += [row * width + column for column in columns]
    return order + [row * width for row in range(height - 1, -1, -1)]


def swap(value, axes):
    count = math.prod(lax.axis_size(axis) for axis in axes)
    return lax.ppermute(value, axes, [(i, count - 1 - i) for i in range(count)])


def token_place(count, dim, spots, first_frame):
    shape = (count, 1) if dim == 0 else (1, count)
    token = lax.broadcasted_iota(jnp.int32, shape, dim).astype(jnp.float32)
    frame = jnp.floor((token + 0.5) * (1.0 / spots))
    spot = token - frame * spots
    row = jnp.floor((spot + 0.5) * (1.0 / WB))
    return frame + first_frame, row, spot - row * WB


def attend_kernel(spots, windows_ref, q_ref, k_ref, v_ref, k_halo_ref, v_halo_ref, out_ref, bias_own, bias_halo):
    rows = q_ref.shape[0]
    frames_here = rows // spots

    @pl.when(pl.program_id(0) == 0)
    def _():
        request = lax.axis_index("owner") // 2
        halo_frame = jnp.where(lax.axis_index("slab") == 0, frames_here, -HALO).astype(jnp.float32)
        query = token_place(rows, 0, spots, 0.0)
        for ref, first in ((bias_own, 0.0), (bias_halo, halo_frame)):
            key = token_place(ref.shape[1], 1, spots, first)
            allowed = None
            for part in range(3):
                near = jnp.abs(query[part] - key[part]) <= windows_ref[request, part].astype(jnp.float32)
                allowed = near if allowed is None else allowed & near
            ref[...] = jnp.where(allowed, 0.0, NEG_LARGE)

    scale = 1.0 / math.sqrt(HEAD_DIM)
    contract = (((1,), (1,)), ((), ()))
    for head in range(q_ref.shape[1] // HEAD_DIM):
        at = slice(head * HEAD_DIM, (head + 1) * HEAD_DIM)
        query = q_ref[:, at]
        own = lax.dot_general(query, k_ref[:, at], contract, preferred_element_type=jnp.float32)
        halo = lax.dot_general(query, k_halo_ref[:, at], contract, preferred_element_type=jnp.float32)
        own = own * scale + bias_own[...]
        halo = halo * scale + bias_halo[...]
        highest = jnp.maximum(jnp.max(own, axis=1, keepdims=True), jnp.max(halo, axis=1, keepdims=True))
        own = jnp.exp(own - highest)
        halo = jnp.exp(halo - highest)
        total = jnp.sum(own, axis=1, keepdims=True) + jnp.sum(halo, axis=1, keepdims=True)
        share = 1.0 / total
        own = (own * share).astype(jnp.bfloat16)
        halo = (halo * share).astype(jnp.bfloat16)
        mixture = jnp.dot(own, v_ref[:, at], preferred_element_type=jnp.float32)
        mixture = mixture + jnp.dot(halo, v_halo_ref[:, at], preferred_element_type=jnp.float32)
        out_ref[:, at] = mixture.astype(jnp.bfloat16)


def attend(query_rows, key_value_rows, halo, windows, spots, part):
    rows, features = query_rows.shape
    width = features // PARTS
    heads = width // HEAD_DIM
    steps = 2 if heads % 2 == 0 else 1
    block = width // steps
    halo_rows = halo.shape[1]
    first = part * steps
    keys = rows + halo_rows
    return pl.pallas_call(
        functools.partial(attend_kernel, spots),
        grid=(steps,),
        out_shape=jax.ShapeDtypeStruct((rows, width), jnp.bfloat16),
        in_specs=[
            pl.BlockSpec(memory_space=pltpu.SMEM),
            pl.BlockSpec((rows, block), lambda i: (0, first + i)),
            pl.BlockSpec((None, rows, block), lambda i: (0, 0, first + i)),
            pl.BlockSpec((None, rows, block), lambda i: (1, 0, first + i)),
            pl.BlockSpec((None, halo_rows, block), lambda i: (0, 0, first + i)),
            pl.BlockSpec((None, halo_rows, block), lambda i: (1, 0, first + i)),
        ],
        out_specs=pl.BlockSpec((rows, block), lambda i: (0, i)),
        scratch_shapes=[pltpu.VMEM((rows, rows), jnp.float32), pltpu.VMEM((rows, halo_rows), jnp.float32)],
        compiler_params=pltpu.CompilerParams(vmem_limit_bytes=VMEM_BYTES),
        cost_estimate=pl.CostEstimate(
            flops=4 * rows * keys * width, bytes_accessed=2 * width * (2 * rows + 2 * keys), transcendentals=heads * rows * keys
        ),
        name="attend",
    )(windows, query_rows, key_value_rows, key_value_rows, halo, halo)


def project_kernel(count, blocks, piece, order_ref, *refs):
    a_refs = refs[: blocks * PARTS]
    w_refs = refs[blocks * PARTS : blocks * PARTS + count]
    gate_ref, far_gate_ref = refs[blocks * PARTS + count : blocks * PARTS + count + 2]
    out_refs = refs[blocks * PARTS + count + 2 : blocks * PARTS + count + 2 + blocks]
    weight, arrived = refs[-2:]
    copies = [pltpu.make_async_copy(w_refs[j], weight.at[order_ref[j]], arrived.at[j]) for j in range(count)]
    for copy in copies:
        copy.start()
    for copy in copies:
        copy.wait()
    width = weight.shape[2]
    quarter = lax.axis_index("groups") * lax.axis_size("slab") + lax.axis_index("slab")
    columns = pl.ds(pl.multiple_of((quarter * PIECES + piece) * width, 128), width)
    share = count // PARTS
    for block in range(blocks):
        gate = (gate_ref if block < blocks // 2 else far_gate_ref)[:, columns]
        product = None
        for part in range(PARTS):
            rows = weight[part * share : (part + 1) * share].reshape(-1, width)
            term = jnp.dot(a_refs[block * PARTS + part][...], rows, preferred_element_type=jnp.float32)
            product = term if product is None else product + term
        out_refs[block][...] = (product * gate).astype(jnp.bfloat16)


def project(order, a_blocks, chunks, gate, far_gate, piece):
    count = len(chunks)
    blocks = len(a_blocks) // PARTS
    rows = a_blocks[0].shape[0]
    depth, width = chunks[0].shape
    vmem = pl.BlockSpec(memory_space=pltpu.VMEM)
    return pl.pallas_call(
        functools.partial(project_kernel, count, blocks, piece),
        out_shape=[jax.ShapeDtypeStruct((rows, width), jnp.bfloat16)] * blocks,
        in_specs=[pl.BlockSpec(memory_space=pltpu.SMEM)]
        + [vmem] * len(a_blocks)
        + [pl.BlockSpec(memory_space=pl.ANY)] * count
        + [vmem] * 2,
        out_specs=[vmem] * blocks,
        scratch_shapes=[pltpu.VMEM((count, depth, width), jnp.bfloat16), pltpu.SemaphoreType.DMA((count,))],
        compiler_params=pltpu.CompilerParams(vmem_limit_bytes=VMEM_BYTES),
        cost_estimate=pl.CostEstimate(
            flops=2 * blocks * rows * width * depth * count,
            bytes_accessed=2 * (blocks * rows * (depth * count + width) + count * depth * width),
            transcendentals=0,
        ),
        name="project",
    )(order, *a_blocks, *chunks, gate, far_gate)


def place_kernel(blocks, *refs):
    in_refs = refs[: blocks * PIECES]
    out_ref, done = refs[-2:]
    width = in_refs[0].shape[1]
    group, slab = lax.axis_index("groups"), lax.axis_index("slab")
    slabs = lax.axis_size("slab")
    copies = []
    for block in range(blocks):
        far, mate = divmod(block, 2)
        quarter = (1 - group if far else group) * slabs + (1 - slab if mate else slab)
        for piece in range(PIECES):
            at = pl.ds(pl.multiple_of((quarter * PIECES + piece) * width, 128), width)
            index = piece * blocks + block
            copies.append(pltpu.make_async_copy(in_refs[index], out_ref.at[:, at], done.at[index]))
    for copy in copies:
        copy.start()
    for copy in copies:
        copy.wait()


def place(pieces, blocks):
    rows, width = pieces[0].shape
    anywhere = pl.BlockSpec(memory_space=pl.ANY)
    return pl.pallas_call(
        functools.partial(place_kernel, blocks),
        out_shape=jax.ShapeDtypeStruct((rows, width * len(pieces)), jnp.bfloat16),
        in_specs=[anywhere] * len(pieces),
        out_specs=anywhere,
        scratch_shapes=[pltpu.SemaphoreType.DMA((len(pieces),))],
        cost_estimate=pl.CostEstimate(flops=0, bytes_accessed=4 * rows * width * len(pieces), transcendentals=0),
        name="place",
    )(*pieces)


def gather_rings(own_pieces, order):
    count = len(order)
    ahead = [(order[i], order[(i + 1) % count]) for i in range(count)]
    back = [(to, at) for at, to in ahead]
    position = [order.index(owner) for owner in range(count)]
    place_here = jnp.array(position, jnp.int32)[lax.axis_index("owner")]
    table = jnp.array(order, jnp.int32)
    gathered = []
    for piece, own in enumerate(own_pieces):
        ups = (count - 1 + (piece + 1) % 2) // 2
        steps = [0]
        chunks = [own]
        for turns, perm, sign in ((ups, ahead, -1), (count - 1 - ups, back, 1)):
            chunk = own
            for turn in range(1, turns + 1):
                chunk = lax.ppermute(chunk, "owner", perm)
                chunks.append(chunk)
                steps.append(sign * turn)
        gathered.append((chunks, table[(place_here + jnp.array(steps, jnp.int32)) % count]))
    return gathered


def on_device(queries, key_value, keep, windows, gate, out_weight):
    frames_here, spots, features = queries.shape[1:]
    model_width = gate.shape[1]
    rows = frames_here * spots
    slab_index = lax.axis_index("slab")
    slabs = lax.axis_size("slab")
    groups = lax.axis_size("groups")
    owner = lax.axis_index("owner")
    quarter = lax.axis_index("groups") * slabs + slab_index

    width = model_width // (groups * slabs * PIECES)
    own_pieces = [
        lax.dynamic_slice_in_dim(out_weight, (quarter * PIECES + piece) * width, width, 1) for piece in range(PIECES)
    ]
    gathered = gather_rings(own_pieces, ring_order(lax.axis_size("owner")))

    border = lax.dynamic_slice_in_dim(key_value[:, 0], jnp.where(slab_index == 0, frames_here - HALO, 0), HALO, 1)
    halo = swap(border, ("slab",)).reshape(2, HALO * spots, features)

    gate_row = lax.dynamic_index_in_dim(gate, owner // 2, 0, keepdims=True)
    keep_flag = lax.dynamic_index_in_dim(keep, owner // 2, 0, keepdims=False)
    near_gate = gate_row * jnp.where(owner % 2 == 1, keep_flag, 1).astype(jnp.float32)
    far_gate = swap(near_gate, ("groups",))

    query_rows = queries.reshape(rows, features)
    key_value_rows = key_value.reshape(2, rows, features)
    parts = [[], [], [], []]
    for part in range(PARTS):
        attended = attend(query_rows, key_value_rows, halo, windows, spots, part)
        across = swap(attended, ("groups",))
        for held, value in zip(parts, (attended, swap(attended, ("slab",)), across, swap(across, ("slab",)))):
            held.append(value)
    a_blocks = [value for held in parts for value in held]

    placed = []
    for piece, (chunks, order) in enumerate(gathered):
        own, mate, far, far_mate = project(order, a_blocks, chunks, near_gate, far_gate, piece)
        placed += [own, swap(mate, ("slab",)), swap(far, ("groups",)), swap(far_mate, ("groups", "slab"))]
    return place(placed, groups * slabs).reshape((1, frames_here, spots, model_width))


def solution(mesh):
    placed = (
        P(("groups", "owner"), "slab", None, None),
        P(None, ("groups", "owner"), "slab", None, None),
        P("groups"),
        P("groups", None),
        P("groups", None),
        P("owner", None),
    )
    return jax.shard_map(
        on_device,
        mesh=mesh,
        in_specs=placed,
        out_specs=P(("groups", "owner"), "slab", None, None),
        check_vma=False,
    )
```

```python
import functools
import math

import jax
import jax.numpy as jnp
import numpy as np
from jax import lax
from jax.experimental import pallas as pl
from jax.experimental.pallas import tpu as pltpu
from jax.sharding import PartitionSpec as P

HEAD_DIM = 128
WB = 14
HALO = 1
LANES = 128
NEG_LARGE = -1e30
PARTS = 2
FLIGHT = 2
VMEM_BYTES = 24 * 1024 * 1024
ANYWHERE = pl.BlockSpec(memory_space=pl.ANY)
IN_HBM = pl.BlockSpec(memory_space=pltpu.HBM)
IN_VMEM = pl.BlockSpec(memory_space=pltpu.VMEM)
IN_SMEM = pl.BlockSpec(memory_space=pltpu.SMEM)


def ring_order(count):
    width = max(w for w in range(1, count + 1) if count % w == 0 and w * w <= count)
    height = count // width
    if width == 1 or height % 2:
        return list(range(count))
    order = []
    for row in range(height):
        columns = range(1, width) if row % 2 == 0 else range(width - 1, 0, -1)
        order += [row * width + column for column in columns]
    return order + [row * width for row in range(height - 1, -1, -1)]


def piece_widths(quarter_width):
    tiles = quarter_width // LANES
    late = 2 * (tiles // 5) if tiles >= 5 else 0
    strips = []
    for count in (tiles - late, late):
        if count:
            strips.append([(count - count // 2) * LANES, count // 2 * LANES])
    return strips


def swap(value, axes):
    count = math.prod(lax.axis_size(axis) for axis in axes)
    return lax.ppermute(value, axes, [(i, count - 1 - i) for i in range(count)])


def after(value, *others):
    return lax.optimization_barrier((value,) + others)[0]


def run_copies(copies):
    for copy in copies:
        copy.start()
    for copy in copies:
        copy.wait()


def cut_kernel(strips, key_value_ref, keep_ref, gate_ref, weight_ref, *refs):
    strip_refs, border_ref, out_gate_ref, done = refs[: len(strips)], *refs[len(strips) :]
    owner, slab = lax.axis_index("owner"), lax.axis_index("slab")
    quarter = lax.axis_index("groups") * lax.axis_size("slab") + slab
    total = sum(strips)
    frames_here = key_value_ref.shape[2]
    copies, column = [], 0
    for index, width in enumerate(strips):
        at = pl.ds(pl.multiple_of(quarter * total + column, LANES), width)
        copies.append(pltpu.make_async_copy(weight_ref.at[:, at], strip_refs[index], done.at[index]))
        column += width
    frame = jnp.where(slab == 0, frames_here - HALO, 0)
    for kind in range(2):
        source = key_value_ref.at[kind, 0, pl.ds(frame, HALO)]
        copies.append(pltpu.make_async_copy(source, border_ref.at[kind], done.at[len(strips) + kind]))
    for copy in copies:
        copy.start()
    factor = jnp.where(owner % 2 == 1, keep_ref[owner // 2], 1).astype(jnp.float32)
    out_gate_ref[...] = gate_ref[pl.ds(owner // 2, 1), :] * factor
    for copy in copies:
        copy.wait()


def cut(key_value, keep, gate, out_weight, strips):
    kinds, _, _, spots, features = key_value.shape
    depth = out_weight.shape[0]
    shapes = [jax.ShapeDtypeStruct((depth, width), jnp.bfloat16) for width in strips]
    shapes.append(jax.ShapeDtypeStruct((kinds, HALO, spots, features), jnp.bfloat16))
    shapes.append(jax.ShapeDtypeStruct((1, gate.shape[1]), jnp.float32))
    outs = pl.pallas_call(
        functools.partial(cut_kernel, strips),
        out_shape=shapes,
        in_specs=[IN_HBM, IN_SMEM, IN_VMEM, IN_HBM],
        out_specs=[IN_VMEM] * len(shapes),
        scratch_shapes=[pltpu.SemaphoreType.DMA((len(strips) + kinds,))],
        compiler_params=pltpu.CompilerParams(vmem_limit_bytes=VMEM_BYTES),
        name="cut",
    )(key_value, keep, gate, out_weight)
    return outs[: len(strips)], outs[-2].reshape(kinds, HALO * spots, features), outs[-1]


def token_place(count, dim, spots, first_frame):
    shape = (count, 1) if dim == 0 else (1, count)
    token = lax.broadcasted_iota(jnp.int32, shape, dim).astype(jnp.float32)
    frame = jnp.floor((token + 0.5) * (1.0 / spots))
    spot = token - frame * spots
    row = jnp.floor((spot + 0.5) * (1.0 / WB))
    return frame + first_frame, row, spot - row * WB


def attend_kernel(spots, windows_ref, q_ref, k_ref, v_ref, k_halo_ref, v_halo_ref, out_ref, bias):
    rows = q_ref.shape[0]
    halo_rows = k_halo_ref.shape[0]
    keys = bias.shape[1]
    frames_here = rows // spots

    @pl.when(pl.program_id(0) == 0)
    def _():
        request = lax.axis_index("owner") // 2
        halo_frame = jnp.where(lax.axis_index("slab") == 0, 0, -HALO - frames_here).astype(jnp.float32)
        query = token_place(rows, 0, spots, 0.0)
        key = token_place(keys, 1, spots, 0.0)
        index = lax.broadcasted_iota(jnp.int32, (1, keys), 1)
        frame = jnp.where(index < rows, key[0], key[0] + halo_frame)
        frame = jnp.where(index < rows + halo_rows, frame, -NEG_LARGE)
        allowed = None
        for part, place in enumerate((frame, key[1], key[2])):
            near = jnp.abs(query[part] - place) <= windows_ref[request, part].astype(jnp.float32)
            allowed = near if allowed is None else allowed & near
        bias[...] = jnp.where(allowed, 0.0, NEG_LARGE)

    scale = math.log2(math.e) / math.sqrt(HEAD_DIM)
    pad = jnp.zeros((keys - rows - halo_rows, HEAD_DIM), jnp.bfloat16)
    for head in range(q_ref.shape[1] // HEAD_DIM):
        at = slice(head * HEAD_DIM, (head + 1) * HEAD_DIM)
        key = jnp.concatenate([k_ref[:, at], k_halo_ref[:, at], pad], axis=0)
        value = jnp.concatenate([v_ref[:, at], v_halo_ref[:, at], pad], axis=0)
        score = lax.dot_general(q_ref[:, at], key, (((1,), (1,)), ((), ())), preferred_element_type=jnp.float32)
        score = score * scale + bias[...]
        weight = jnp.exp2(score - jnp.max(score, axis=1, keepdims=True))
        weight = weight * (1.0 / jnp.sum(weight, axis=1, keepdims=True))
        mixture = jnp.dot(weight.astype(jnp.bfloat16), value, preferred_element_type=jnp.float32)
        out_ref[:, at] = mixture.astype(jnp.bfloat16)


def attend(query_rows, key_value_rows, halo, windows, spots, part):
    rows, features = query_rows.shape
    width = features // PARTS
    heads = width // HEAD_DIM
    steps = 2 if heads % 2 == 0 else 1
    block = width // steps
    halo_rows = halo.shape[1]
    first = part * steps
    keys = pl.cdiv(rows + halo_rows, LANES) * LANES
    return pl.pallas_call(
        functools.partial(attend_kernel, spots),
        grid=(steps,),
        out_shape=jax.ShapeDtypeStruct((rows, width), jnp.bfloat16),
        in_specs=[
            IN_SMEM,
            pl.BlockSpec((rows, block), lambda i: (0, first + i)),
            pl.BlockSpec((None, rows, block), lambda i: (0, 0, first + i)),
            pl.BlockSpec((None, rows, block), lambda i: (1, 0, first + i)),
            pl.BlockSpec((None, halo_rows, block), lambda i: (0, 0, first + i)),
            pl.BlockSpec((None, halo_rows, block), lambda i: (1, 0, first + i)),
        ],
        out_specs=pl.BlockSpec((rows, block), lambda i: (0, i)),
        scratch_shapes=[pltpu.VMEM((rows, keys), jnp.float32)],
        compiler_params=pltpu.CompilerParams(vmem_limit_bytes=VMEM_BYTES),
        cost_estimate=pl.CostEstimate(
            flops=4 * rows * keys * width, bytes_accessed=2 * width * (2 * rows + 2 * keys), transcendentals=heads * rows * keys
        ),
        name="attend",
    )(windows, query_rows, key_value_rows, key_value_rows, halo, halo)


def project_kernel(count, strips, column, total, tables_ref, *refs):
    blocks = 4
    a_refs, refs = refs[: blocks * PARTS], refs[blocks * PARTS :]
    w_refs, refs = refs[: count * len(strips)], refs[count * len(strips) :]
    gate_refs, out_refs, (rows_all, weight, arrived) = refs[:2], refs[2 : 2 + blocks], refs[2 + blocks :]
    owner = lax.axis_index("owner")
    rows, part_width = a_refs[0].shape
    copies, at = [], 0
    for strip, width in enumerate(strips):
        for turn in range(count):
            index = strip * count + turn
            target = weight.at[tables_ref[strip, owner, turn], :, at : at + width]
            copies.append(pltpu.make_async_copy(w_refs[index], target, arrived.at[index]))
        at += width
    for index, a_ref in enumerate(a_refs):
        block, part = divmod(index, PARTS)
        target = rows_all.at[block * rows : (block + 1) * rows, part * part_width : (part + 1) * part_width]
        copies.append(pltpu.make_async_copy(a_ref, target, arrived.at[count * len(strips) + index]))
    run_copies(copies)
    quarter = lax.axis_index("groups") * lax.axis_size("slab") + lax.axis_index("slab")
    tile = 2 * LANES if at % (2 * LANES) == 0 else LANES
    for first in range(0, at, tile):
        columns = weight[:, :, first : first + tile].reshape(-1, tile)
        product = jnp.dot(rows_all[...], columns, preferred_element_type=jnp.float32)
        here = pl.ds(pl.multiple_of(quarter * total + column + first, LANES), tile)
        for block in range(blocks):
            gate = gate_refs[block // 2][:, here]
            result = product[block * rows : (block + 1) * rows] * gate
            out_refs[block][:, first : first + tile] = result.astype(jnp.bfloat16)


def project(tables, a_blocks, chunks, gates, strips, column, total):
    count = len(chunks) // len(strips)
    blocks = len(a_blocks) // PARTS
    rows, part_width = a_blocks[0].shape
    depth = chunks[0].shape[0]
    width = sum(strips)
    return pl.pallas_call(
        functools.partial(project_kernel, count, strips, column, total),
        out_shape=[jax.ShapeDtypeStruct((rows, width), jnp.bfloat16)] * blocks,
        in_specs=[IN_SMEM] + [ANYWHERE] * (len(a_blocks) + len(chunks)) + [IN_VMEM] * 2,
        out_specs=[IN_VMEM] * blocks,
        scratch_shapes=[
            pltpu.VMEM((blocks * rows, PARTS * part_width), jnp.bfloat16),
            pltpu.VMEM((count, depth, width), jnp.bfloat16),
            pltpu.SemaphoreType.DMA((len(chunks) + len(a_blocks),)),
        ],
        compiler_params=pltpu.CompilerParams(vmem_limit_bytes=VMEM_BYTES),
        cost_estimate=pl.CostEstimate(
            flops=2 * blocks * rows * width * depth * count,
            bytes_accessed=2 * (blocks * rows * (depth * count + width) + count * depth * width),
            transcendentals=0,
        ),
        name="project",
    )(tables, *a_blocks, *chunks, *gates)


def place_kernel(column, total, *refs):
    in_refs, (out_ref, done) = refs[:4], refs[-2:]
    width = in_refs[0].shape[1]
    group, slab = lax.axis_index("groups"), lax.axis_index("slab")
    copies = []
    for block, in_ref in enumerate(in_refs):
        far, mate = divmod(block, 2)
        quarter = (1 - group if far else group) * lax.axis_size("slab") + (1 - slab if mate else slab)
        at = pl.ds(pl.multiple_of(quarter * total + column, LANES), width)
        copies.append(pltpu.make_async_copy(in_ref, out_ref.at[:, at], done.at[block]))
    run_copies(copies)


def place(blocks, out, column, total, model_width):
    rows, width = blocks[0].shape
    held = [] if out is None else [out]
    return pl.pallas_call(
        functools.partial(place_kernel, column, total),
        out_shape=jax.ShapeDtypeStruct((rows, model_width), jnp.bfloat16),
        in_specs=[IN_VMEM] * len(blocks) + [ANYWHERE] * len(held),
        out_specs=ANYWHERE,
        scratch_shapes=[pltpu.SemaphoreType.DMA((len(blocks),))],
        input_output_aliases={len(blocks): 0} if held else {},
        compiler_params=pltpu.CompilerParams(vmem_limit_bytes=VMEM_BYTES),
        cost_estimate=pl.CostEstimate(flops=0, bytes_accessed=4 * rows * width * len(blocks), transcendentals=0),
        name="place",
    )(*blocks, *held)


def ring_hops(count, strips):
    ways = ([], [])
    for first in range(0, len(strips), 2):
        pair = list(range(first, min(first + 2, len(strips))))
        for way, hops in enumerate(ways):
            turns = {strip: (count - 1 + (strip + way + 1) % 2) // 2 for strip in pair}
            for turn in range(1, max(turns.values()) + 1):
                for strip in sorted(pair, key=lambda s: (s + way) % 2):
                    if turn <= turns[strip]:
                        hops.append((strip, turn))
    return ways


def on_device(queries, key_value, keep, windows, gate, out_weight):
    frames_here, spots, features = queries.shape[1:]
    model_width = gate.shape[1]
    rows = frames_here * spots
    total = model_width // (lax.axis_size("groups") * lax.axis_size("slab"))
    pieces = piece_widths(total)
    strips = [width for piece in pieces for width in piece]

    count = lax.axis_size("owner")
    order = ring_order(count)
    ahead = [(order[i], order[(i + 1) % count]) for i in range(count)]
    perms = (ahead, [(to, at) for at, to in ahead])
    ways = ring_hops(count, strips)
    sources = [[0] for _ in strips]
    for hops, sign in zip(ways, (-1, 1)):
        for strip, turn in hops:
            sources[strip].append(sign * turn)
    tables = np.zeros((len(strips), count, count), np.int32)
    for strip, turns in enumerate(sources):
        for at, owner in enumerate(order):
            tables[strip, owner] = [order[(at + turn) % count] for turn in turns]

    own_strips, border, near_gate = cut(key_value, keep, gate, out_weight, strips)
    chunks = [{0: own} for own in own_strips]
    arrived = ([], [])

    def hop(slot, *others):
        for way, (hops, sign) in enumerate(zip(ways, (-1, 1))):
            if slot < len(hops):
                strip, turn = hops[slot]
                held = chunks[strip][sign * (turn - 1)]
                waits = list(others)
                if slot >= FLIGHT:
                    waits.append(arrived[way][slot - FLIGHT])
                if waits:
                    held = after(held, *waits)
                value = lax.ppermute(held, "owner", perms[way])
                chunks[strip][sign * turn] = value
                arrived[way].append(value)

    slots = max(len(hops) for hops in ways)
    early = len([hop for hop in ways[0] if hop[0] < len(pieces[0])])
    hop(0)
    hop(1)
    halo = swap(border, ("slab",))
    gates = (near_gate, swap(near_gate, ("groups",)))

    query_rows = queries.reshape(rows, features)
    key_value_rows = key_value.reshape(2, rows, features)
    parts = [[], [], [], []]
    waits = {}
    for part in range(PARTS):
        query = query_rows if part == 0 else after(query_rows, arrived[0][part - 1], arrived[1][part - 1])
        attended = attend(query, key_value_rows, halo, windows, spots, part)
        hop(FLIGHT + part, attended, gates[1])
        mate, across = swap(attended, ("slab",)), swap(attended, ("groups",))
        far_mate = swap(across, ("slab",))
        landing = max(early + 1 - 3 * (PARTS - 1 - part), FLIGHT + PARTS)
        waits.setdefault(landing, []).extend((across, mate))
        for held, value in zip(parts, (attended, mate, across, far_mate)):
            held.append(value)
    a_blocks = [value for held in parts for value in held]

    def project_piece(index, *others):
        strip = sum(len(widths) for widths in pieces[:index])
        span = range(strip, strip + len(pieces[index]))
        held = [chunks[s][turn] for s in span for turn in sources[s]]
        if others:
            held[0] = after(held[0], *others)
        table = jnp.asarray(tables[strip : strip + len(pieces[index])])
        column = sum(sum(widths) for widths in pieces[:index])
        own, mate, far, far_mate = project(table, a_blocks, held, gates, pieces[index], column, total)
        return [own, swap(mate, ("slab",)), swap(far, ("groups",)), swap(far_mate, ("groups", "slab"))], column

    results = []
    for slot in range(FLIGHT + PARTS, slots):
        if slot == early + 2:
            results.append(project_piece(0))
            waits.setdefault(slot, []).append(results[0][0][0])
            waits.setdefault(slots - 1, []).append(results[0][0][2])
        hop(slot, *waits.get(slot, []))
    results += [project_piece(index, *results[0][0][2:]) for index in range(len(results), len(pieces))]
    out = None
    for blocks, column in results:
        out = place(blocks, out, column, total, model_width)
    return out.reshape((1, frames_here, spots, model_width))


def solution(mesh):
    placed = (
        P(("groups", "owner"), "slab", None, None),
        P(None, ("groups", "owner"), "slab", None, None),
        P("groups"),
        P("groups", None),
        P("groups", None),
        P("owner", None),
    )
    return jax.shard_map(
        on_device,
        mesh=mesh,
        in_specs=placed,
        out_specs=P(("groups", "owner"), "slab", None, None),
        check_vma=False,
    )
```

```python
import functools
import math

import jax
import jax.numpy as jnp
import numpy as np
from jax import lax
from jax.experimental import pallas as pl
from jax.experimental.pallas import tpu as pltpu
from jax.sharding import PartitionSpec as P

HEAD_DIM = 128
WB = 14
HALO = 1
LANES = 128
NEG_LARGE = -1e30
PARTS = 2
FLIGHT = 2
VMEM_BYTES = 24 * 1024 * 1024
WHOLE_VMEM_BYTES = 62 * 1024 * 1024
ANYWHERE = pl.BlockSpec(memory_space=pl.ANY)
IN_HBM = pl.BlockSpec(memory_space=pltpu.HBM)
IN_VMEM = pl.BlockSpec(memory_space=pltpu.VMEM)
IN_SMEM = pl.BlockSpec(memory_space=pltpu.SMEM)


def ring_order(count):
    width = max(w for w in range(1, count + 1) if count % w == 0 and w * w <= count)
    height = count // width
    if width == 1 or height % 2:
        return list(range(count))
    order = []
    for row in range(height):
        columns = range(1, width) if row % 2 == 0 else range(width - 1, 0, -1)
        order += [row * width + column for column in columns]
    return order + [row * width for row in range(height - 1, -1, -1)]


def piece_widths(half_width):
    tiles = half_width // (2 * LANES)
    late = 2 * tiles // 5
    return [count * LANES for count in (tiles - late, late) if count]


def swap(value, axes):
    count = math.prod(lax.axis_size(axis) for axis in axes)
    return lax.ppermute(value, axes, [(i, count - 1 - i) for i in range(count)])


def after(value, *others):
    return lax.optimization_barrier((value,) + others)[0]


def run_copies(copies):
    for copy in copies:
        copy.start()
    for copy in copies:
        copy.wait()


def cut_kernel(strips, key_value_ref, keep_ref, gate_ref, weight_ref, *refs):
    strip_refs, border_ref, out_gate_ref, done = refs[: len(strips)], *refs[len(strips) :]
    owner, slab = lax.axis_index("owner"), lax.axis_index("slab")
    group = lax.axis_index("groups")
    total = sum(strips)
    frames_here = key_value_ref.shape[2]
    copies, column = [], 0
    for index, width in enumerate(strips):
        at = pl.ds(pl.multiple_of(group * total + column, LANES), width)
        copies.append(pltpu.make_async_copy(weight_ref.at[:, at], strip_refs[index], done.at[index]))
        column += width
    frame = jnp.where(slab == 0, frames_here - HALO, 0)
    for kind in range(2):
        source = key_value_ref.at[kind, 0, pl.ds(frame, HALO)]
        copies.append(pltpu.make_async_copy(source, border_ref.at[kind], done.at[len(strips) + kind]))
    for copy in copies:
        copy.start()
    factor = jnp.where(owner % 2 == 1, keep_ref[owner // 2], 1).astype(jnp.float32)
    out_gate_ref[...] = gate_ref[pl.ds(owner // 2, 1), :] * factor
    for copy in copies:
        copy.wait()


def cut(key_value, keep, gate, out_weight, strips):
    kinds, _, _, spots, features = key_value.shape
    depth = out_weight.shape[0]
    shapes = [jax.ShapeDtypeStruct((depth, width), jnp.bfloat16) for width in strips]
    shapes.append(jax.ShapeDtypeStruct((kinds, HALO, spots, features), jnp.bfloat16))
    shapes.append(jax.ShapeDtypeStruct((1, gate.shape[1]), jnp.float32))
    outs = pl.pallas_call(
        functools.partial(cut_kernel, strips),
        out_shape=shapes,
        in_specs=[IN_HBM, IN_SMEM, IN_VMEM, IN_HBM],
        out_specs=[IN_VMEM] * len(shapes),
        scratch_shapes=[pltpu.SemaphoreType.DMA((len(strips) + kinds,))],
        compiler_params=pltpu.CompilerParams(vmem_limit_bytes=WHOLE_VMEM_BYTES),
        name="cut",
    )(key_value, keep, gate, out_weight)
    return outs[: len(strips)], outs[-2].reshape(kinds, HALO * spots, features), outs[-1]


def token_place(count, dim, spots, first_frame):
    shape = (count, 1) if dim == 0 else (1, count)
    token = lax.broadcasted_iota(jnp.int32, shape, dim).astype(jnp.float32)
    frame = jnp.floor((token + 0.5) * (1.0 / spots))
    spot = token - frame * spots
    row = jnp.floor((spot + 0.5) * (1.0 / WB))
    return frame + first_frame, row, spot - row * WB


def attend_kernel(spots, windows_ref, q_ref, k_ref, v_ref, k_halo_ref, v_halo_ref, out_ref, bias):
    rows = q_ref.shape[0]
    halo_rows = k_halo_ref.shape[0]
    keys = bias.shape[1]
    frames_here = rows // spots

    @pl.when(pl.program_id(0) == 0)
    def _():
        request = lax.axis_index("owner") // 2
        halo_frame = jnp.where(lax.axis_index("slab") == 0, 0, -HALO - frames_here).astype(jnp.float32)
        query = token_place(rows, 0, spots, 0.0)
        key = token_place(keys, 1, spots, 0.0)
        index = lax.broadcasted_iota(jnp.int32, (1, keys), 1)
        frame = jnp.where(index < rows, key[0], key[0] + halo_frame)
        frame = jnp.where(index < rows + halo_rows, frame, -NEG_LARGE)
        allowed = None
        for part, place in enumerate((frame, key[1], key[2])):
            near = jnp.abs(query[part] - place) <= windows_ref[request, part].astype(jnp.float32)
            allowed = near if allowed is None else allowed & near
        bias[...] = jnp.where(allowed, 0.0, NEG_LARGE)

    scale = math.log2(math.e) / math.sqrt(HEAD_DIM)
    pad = jnp.zeros((keys - rows - halo_rows, HEAD_DIM), jnp.bfloat16)
    for head in range(q_ref.shape[1] // HEAD_DIM):
        at = slice(head * HEAD_DIM, (head + 1) * HEAD_DIM)
        key = jnp.concatenate([k_ref[:, at], k_halo_ref[:, at], pad], axis=0)
        value = jnp.concatenate([v_ref[:, at], v_halo_ref[:, at], pad], axis=0)
        score = lax.dot_general(q_ref[:, at], key, (((1,), (1,)), ((), ())), preferred_element_type=jnp.float32)
        score = score * scale + bias[...]
        weight = jnp.exp2(score - jnp.max(score, axis=1, keepdims=True))
        weight = weight * (1.0 / jnp.sum(weight, axis=1, keepdims=True))
        mixture = jnp.dot(weight.astype(jnp.bfloat16), value, preferred_element_type=jnp.float32)
        out_ref[:, at] = mixture.astype(jnp.bfloat16)


def attend(query_rows, key_value_rows, halo, windows, spots, part):
    rows, features = query_rows.shape
    width = features // PARTS
    heads = width // HEAD_DIM
    steps = 2 if heads % 2 == 0 else 1
    block = width // steps
    halo_rows = halo.shape[1]
    first = part * steps
    keys = pl.cdiv(rows + halo_rows, LANES) * LANES
    return pl.pallas_call(
        functools.partial(attend_kernel, spots),
        grid=(steps,),
        out_shape=jax.ShapeDtypeStruct((rows, width), jnp.bfloat16),
        in_specs=[
            IN_SMEM,
            pl.BlockSpec((rows, block), lambda i: (0, first + i)),
            pl.BlockSpec((None, rows, block), lambda i: (0, 0, first + i)),
            pl.BlockSpec((None, rows, block), lambda i: (1, 0, first + i)),
            pl.BlockSpec((None, halo_rows, block), lambda i: (0, 0, first + i)),
            pl.BlockSpec((None, halo_rows, block), lambda i: (1, 0, first + i)),
        ],
        out_specs=pl.BlockSpec((rows, block), lambda i: (0, i)),
        scratch_shapes=[pltpu.VMEM((rows, keys), jnp.float32)],
        compiler_params=pltpu.CompilerParams(vmem_limit_bytes=VMEM_BYTES),
        cost_estimate=pl.CostEstimate(
            flops=4 * rows * keys * width, bytes_accessed=2 * width * (2 * rows + 2 * keys), transcendentals=heads * rows * keys
        ),
        name="attend",
    )(windows, query_rows, key_value_rows, key_value_rows, halo, halo)


def project_kernel(strip, column, total, fixed, tables_ref, *refs):
    a_refs, refs = refs[: 2 * PARTS], refs[2 * PARTS :]
    w_refs, refs = refs[: len(fixed)], refs[len(fixed) :]
    gate_refs, out_refs, (rows_all, weight, arrived) = refs[:2], refs[2:4], refs[4:]
    owner, slab = lax.axis_index("owner"), lax.axis_index("slab")
    rows, part_width = a_refs[0].shape
    copies = []
    for index, where in enumerate(fixed):
        source = tables_ref[slab, owner, index]
        if where is None:
            at = pl.ds(pl.multiple_of((1 - slab if index == len(fixed) - 1 else slab) * strip, LANES), strip)
        else:
            at = slice(where * strip, (where + 1) * strip)
        copies.append(pltpu.make_async_copy(w_refs[index], weight.at[source, :, at], arrived.at[index]))
    for index, a_ref in enumerate(a_refs):
        block, part = divmod(index, PARTS)
        target = rows_all.at[block * rows : (block + 1) * rows, part * part_width : (part + 1) * part_width]
        copies.append(pltpu.make_async_copy(a_ref, target, arrived.at[len(fixed) + index]))
    run_copies(copies)
    width = weight.shape[2]
    tile = 2 * LANES
    for first in range(0, width, tile):
        columns = weight[:, :, first : first + tile].reshape(-1, tile)
        product = jnp.dot(rows_all[...], columns, preferred_element_type=jnp.float32)
        here = pl.ds(pl.multiple_of(lax.axis_index("groups") * total + column + first, LANES), tile)
        for block in range(2):
            gate = gate_refs[block][:, here]
            result = product[block * rows : (block + 1) * rows] * gate
            out_refs[block][:, first : first + tile] = result.astype(jnp.bfloat16)


def project(table, a_blocks, chunks, fixed, gates, column, total):
    slabs, count, held = table.shape
    rows, part_width = a_blocks[0].shape
    depth, strip = chunks[0].shape
    width = 2 * strip
    return pl.pallas_call(
        functools.partial(project_kernel, strip, column, total, fixed),
        out_shape=[jax.ShapeDtypeStruct((rows, width), jnp.bfloat16)] * 2,
        in_specs=[IN_SMEM] + [ANYWHERE] * (len(a_blocks) + held) + [IN_VMEM] * 2,
        out_specs=[IN_VMEM] * 2,
        scratch_shapes=[
            pltpu.VMEM((2 * rows, PARTS * part_width), jnp.bfloat16),
            pltpu.VMEM((count, depth, width), jnp.bfloat16),
            pltpu.SemaphoreType.DMA((held + len(a_blocks),)),
        ],
        compiler_params=pltpu.CompilerParams(vmem_limit_bytes=VMEM_BYTES),
        cost_estimate=pl.CostEstimate(
            flops=4 * rows * width * depth * count,
            bytes_accessed=2 * (2 * rows * (depth * count + width) + count * depth * width),
            transcendentals=0,
        ),
        name="project",
    )(table, *a_blocks, *chunks, *gates)


def place_kernel(column, total, *refs):
    in_refs, (out_ref, done) = refs[:2], refs[-2:]
    width = in_refs[0].shape[1]
    group = lax.axis_index("groups")
    copies = []
    for block, in_ref in enumerate(in_refs):
        start = (1 - group if block else group) * total + column
        at = pl.ds(pl.multiple_of(start, LANES), width)
        copies.append(pltpu.make_async_copy(in_ref, out_ref.at[:, at], done.at[block]))
    run_copies(copies)


def place(blocks, out, column, total, model_width):
    rows, width = blocks[0].shape
    held = [] if out is None else [out]
    return pl.pallas_call(
        functools.partial(place_kernel, column, total),
        out_shape=jax.ShapeDtypeStruct((rows, model_width), jnp.bfloat16),
        in_specs=[IN_VMEM] * len(blocks) + [ANYWHERE] * len(held),
        out_specs=ANYWHERE,
        scratch_shapes=[pltpu.SemaphoreType.DMA((len(blocks),))],
        input_output_aliases={len(blocks): 0} if held else {},
        compiler_params=pltpu.CompilerParams(vmem_limit_bytes=VMEM_BYTES),
        cost_estimate=pl.CostEstimate(flops=0, bytes_accessed=4 * rows * width * len(blocks), transcendentals=0),
        name="place",
    )(*blocks, *held)


def hop_order(pieces, turns, opposite):
    hops, late = [], None
    for piece in range(pieces):
        for turn in range(1, turns + 1):
            for strip in range(2):
                hops.append((piece, strip, turn))
                if late is not None:
                    hops.append(late)
                    late = None
        if opposite:
            late = (piece, None, turns + 1)
    return hops + ([late] if late else [])


def on_device(queries, key_value, keep, windows, gate, out_weight):
    frames_here, spots, features = queries.shape[1:]
    model_width = gate.shape[1]
    rows = frames_here * spots
    slab_index = lax.axis_index("slab")
    slabs = lax.axis_size("slab")
    total = model_width // lax.axis_size("groups")
    widths = piece_widths(total)

    count = lax.axis_size("owner")
    order = ring_order(count)
    spot_of = [order.index(owner) for owner in range(count)]
    ring = [
        (owner * slabs + slab, order[(spot_of[owner] + (1 if slab == 0 else -1)) % count] * slabs + slab)
        for owner in range(count)
        for slab in range(slabs)
    ]
    turns, opposite = (count - 1) // 2, count % 2 == 0
    hops = hop_order(len(widths), turns, opposite)

    strips = [width for width in widths for _ in range(2)]
    own_strips, border, near_gate = cut(key_value, keep, gate, out_weight, strips)
    held = {(index // 2, index % 2, 0): own for index, own in enumerate(own_strips)}
    arrived, crossed = [], {}

    def hop(slot, *others):
        if slot >= len(hops):
            return
        piece, strip, turn = hops[slot]
        if strip is None:
            value = jnp.where(slab_index == 0, held[piece, 0, turn - 1], held[piece, 1, turn - 1])
        else:
            value = held[piece, strip, turn - 1]
        waits = list(others)
        if slot >= FLIGHT:
            waits.append(arrived[slot - FLIGHT])
        if slot >= 2 * FLIGHT + 1:
            waits.append(crossed[hops[slot - 2 * FLIGHT - 1]])
        if waits:
            value = after(value, *waits)
        value = lax.ppermute(value, ("owner", "slab"), ring)
        held[hops[slot]] = value
        arrived.append(value)
        crossed[hops[slot]] = swap(after(value, arrived[slot - 1]) if slot else value, ("slab",))

    first_done = max(slot for slot, at in enumerate(hops) if at[0] == 0) if hops else 0
    hop(0)
    hop(1)
    halo = swap(border, ("slab",))
    gates = (near_gate, swap(near_gate, ("groups",)))

    query_rows = queries.reshape(rows, features)
    key_value_rows = key_value.reshape(2, rows, features)
    near, far, waits = [], [], {}
    for part in range(PARTS):
        query = query_rows if part == 0 else after(query_rows, *arrived[part - 1 : part])
        attended = attend(query, key_value_rows, halo, windows, spots, part)
        hop(FLIGHT + part, attended, gates[1])
        across = swap(attended, ("groups",))
        near.append(attended)
        far.append(across)
        waits.setdefault(max(first_done - PARTS + part, FLIGHT + PARTS), []).append(across)

    def project_piece(piece, *others):
        chunks = [held[piece, 0, 0], held[piece, 1, 0]]
        fixed = [0, 1]
        sources = [(0, 0), (0, 0)]
        for turn in range(1, turns + 1):
            for strip in range(2):
                chunks += [held[piece, strip, turn], crossed[piece, strip, turn]]
                fixed += [strip, strip]
                sources += [(-turn, turn), (turn, -turn)]
        if opposite:
            chunks += [held[piece, None, turns + 1], crossed[piece, None, turns + 1]]
            fixed += [None, None]
            sources += [(turns + 1, turns + 1)] * 2
        table = np.zeros((slabs, count, len(chunks)), np.int32)
        for slab in range(slabs):
            for owner in range(count):
                table[slab, owner] = [order[(spot_of[owner] + source[slab]) % count] for source in sources]
        if others:
            chunks[0] = after(chunks[0], *others)
        column = 2 * sum(widths[:piece])
        own, away = project(jnp.asarray(table), near + far, chunks, tuple(fixed), gates, column, total)
        return [own, swap(away, ("groups",))], column

    results = []
    for slot in range(FLIGHT + PARTS, len(hops)):
        if slot == first_done + FLIGHT + 1:
            results.append(project_piece(0))
            waits.setdefault(slot, []).append(results[0][0][0])
        hop(slot, *waits.get(slot, []))
    for piece in range(len(results), len(widths)):
        results.append(project_piece(piece, *(results[-1][0][1:] if results else [])))
    out = None
    for blocks, column in results:
        out = place(blocks, out, column, total, model_width)
    return out.reshape((1, frames_here, spots, model_width))


def solution(mesh):
    placed = (
        P(("groups", "owner"), "slab", None, None),
        P(None, ("groups", "owner"), "slab", None, None),
        P("groups"),
        P("groups", None),
        P("groups", None),
        P("owner", None),
    )
    return jax.shard_map(
        on_device,
        mesh=mesh,
        in_specs=placed,
        out_specs=P(("groups", "owner"), "slab", None, None),
        check_vma=False,
    )
```

```python
import functools
import math

import jax
import jax.numpy as jnp
import numpy as np
from jax import lax
from jax.experimental import pallas as pl
from jax.experimental.pallas import tpu as pltpu
from jax.sharding import PartitionSpec as P

HEAD_DIM = 128
WB = 14
HALO = 1
LANES = 128
NEG_LARGE = -1e30
PARTS = 2
FLIGHT = 2
VMEM_BYTES = 24 * 1024 * 1024
ANYWHERE = pl.BlockSpec(memory_space=pl.ANY)
IN_HBM = pl.BlockSpec(memory_space=pltpu.HBM)
IN_VMEM = pl.BlockSpec(memory_space=pltpu.VMEM)
IN_SMEM = pl.BlockSpec(memory_space=pltpu.SMEM)


def ring_order(count):
    width = max(w for w in range(1, count + 1) if count % w == 0 and w * w <= count)
    height = count // width
    if width == 1 or height % 2:
        return list(range(count))
    order = []
    for row in range(height):
        columns = range(1, width) if row % 2 == 0 else range(width - 1, 0, -1)
        order += [row * width + column for column in columns]
    return order + [row * width for row in range(height - 1, -1, -1)]


def piece_widths(half_width):
    tiles = half_width // (2 * LANES)
    late = 2 * tiles // 5
    return [count * LANES for count in (tiles - late, late) if count]


def swap(value, axes):
    count = math.prod(lax.axis_size(axis) for axis in axes)
    return lax.ppermute(value, axes, [(i, count - 1 - i) for i in range(count)])


def after(value, *others):
    return lax.optimization_barrier((value,) + others)[0]


def run_copies(copies):
    for copy in copies:
        copy.start()
    for copy in copies:
        copy.wait()


def through(sources, buffers, targets, arrived, left):
    first = [pltpu.make_async_copy(s, b, arrived.at[i]) for i, (s, b) in enumerate(zip(sources, buffers))]
    second = [pltpu.make_async_copy(b, t, left.at[i]) for i, (b, t) in enumerate(zip(buffers, targets))]
    for copy in first:
        copy.start()
    for before, copy in zip(first, second):
        before.wait()
        copy.start()
    for copy in second:
        copy.wait()


def cut_kernel(first, total, weight_ref, *refs):
    count = len(refs) // 2 - 1
    out_refs, buffers, (arrived, left) = refs[:count], refs[count : 2 * count], refs[2 * count :]
    column = lax.axis_index("groups") * total + first
    sources = []
    for ref in out_refs:
        sources.append(weight_ref.at[:, pl.ds(pl.multiple_of(column, LANES), ref.shape[1])])
        column += ref.shape[1]
    through(sources, buffers, out_refs, arrived, left)


def cut(out_weight, strips, first, total):
    depth = out_weight.shape[0]
    out_weight = pltpu.with_memory_space_constraint(out_weight, pltpu.HBM)
    return pl.pallas_call(
        functools.partial(cut_kernel, first, total),
        out_shape=[jax.ShapeDtypeStruct((depth, width), jnp.bfloat16) for width in strips],
        in_specs=[IN_HBM],
        out_specs=[IN_HBM] * len(strips),
        scratch_shapes=[pltpu.VMEM((depth, width), jnp.bfloat16) for width in strips]
        + [pltpu.SemaphoreType.DMA((len(strips),))] * 2,
        compiler_params=pltpu.CompilerParams(vmem_limit_bytes=VMEM_BYTES),
        cost_estimate=pl.CostEstimate(flops=0, bytes_accessed=4 * depth * sum(strips), transcendentals=0),
        name="cut",
    )(out_weight)


def border_kernel(key_value_ref, keep_ref, gate_ref, border_ref, out_gate_ref, buffer, arrived, left):
    owner = lax.axis_index("owner")
    kinds, _, frames_here = key_value_ref.shape[:3]
    frame = jnp.where(lax.axis_index("slab") == 0, frames_here - HALO, 0)
    factor = jnp.where(owner % 2 == 1, keep_ref[owner // 2], 1).astype(jnp.float32)
    out_gate_ref[...] = gate_ref[pl.ds(owner // 2, 1), :] * factor
    sources = [key_value_ref.at[kind, 0, pl.ds(frame, HALO)] for kind in range(kinds)]
    through(sources, [buffer.at[k] for k in range(kinds)], [border_ref.at[k] for k in range(kinds)], arrived, left)


def border(key_value, keep, gate):
    kinds, _, _, spots, features = key_value.shape
    key_value = pltpu.with_memory_space_constraint(key_value, pltpu.HBM)
    edge, scaled = pl.pallas_call(
        border_kernel,
        out_shape=[
            jax.ShapeDtypeStruct((kinds, HALO, spots, features), jnp.bfloat16),
            jax.ShapeDtypeStruct((1, gate.shape[1]), jnp.float32),
        ],
        in_specs=[IN_HBM, IN_SMEM, IN_VMEM],
        out_specs=[IN_HBM, IN_VMEM],
        scratch_shapes=[pltpu.VMEM((kinds, HALO, spots, features), jnp.bfloat16)]
        + [pltpu.SemaphoreType.DMA((kinds,))] * 2,
        compiler_params=pltpu.CompilerParams(vmem_limit_bytes=VMEM_BYTES),
        cost_estimate=pl.CostEstimate(flops=0, bytes_accessed=4 * kinds * spots * features, transcendentals=0),
        name="border",
    )(key_value, keep, gate)
    return edge.reshape(kinds, HALO * spots, features), scaled


def token_place(count, dim, spots, first_frame):
    shape = (count, 1) if dim == 0 else (1, count)
    token = lax.broadcasted_iota(jnp.int32, shape, dim).astype(jnp.float32)
    frame = jnp.floor((token + 0.5) * (1.0 / spots))
    spot = token - frame * spots
    row = jnp.floor((spot + 0.5) * (1.0 / WB))
    return frame + first_frame, row, spot - row * WB


def attend_kernel(spots, windows_ref, q_ref, k_ref, v_ref, k_halo_ref, v_halo_ref, out_ref, bias):
    rows = q_ref.shape[0]
    halo_rows = k_halo_ref.shape[0]
    keys = bias.shape[1]
    frames_here = rows // spots

    @pl.when(pl.program_id(0) == 0)
    def _():
        request = lax.axis_index("owner") // 2
        halo_frame = jnp.where(lax.axis_index("slab") == 0, 0, -HALO - frames_here).astype(jnp.float32)
        query = token_place(rows, 0, spots, 0.0)
        key = token_place(keys, 1, spots, 0.0)
        index = lax.broadcasted_iota(jnp.int32, (1, keys), 1)
        frame = jnp.where(index < rows, key[0], key[0] + halo_frame)
        frame = jnp.where(index < rows + halo_rows, frame, -NEG_LARGE)
        allowed = None
        for part, place in enumerate((frame, key[1], key[2])):
            near = jnp.abs(query[part] - place) <= windows_ref[request, part].astype(jnp.float32)
            allowed = near if allowed is None else allowed & near
        bias[...] = jnp.where(allowed, 0.0, NEG_LARGE)

    scale = math.log2(math.e) / math.sqrt(HEAD_DIM)
    pad = jnp.zeros((keys - rows - halo_rows, HEAD_DIM), jnp.bfloat16)
    ones = jnp.ones((keys, HEAD_DIM), jnp.bfloat16)
    for head in range(q_ref.shape[1] // HEAD_DIM):
        at = slice(head * HEAD_DIM, (head + 1) * HEAD_DIM)
        key = jnp.concatenate([k_ref[:, at], k_halo_ref[:, at], pad], axis=0)
        value = jnp.concatenate([v_ref[:, at], v_halo_ref[:, at], pad], axis=0)
        value = jnp.concatenate([value, ones], axis=1)
        score = lax.dot_general(q_ref[:, at], key, (((1,), (1,)), ((), ())), preferred_element_type=jnp.float32)
        score = score * scale + bias[...]
        weight = jnp.exp2(score - jnp.max(score, axis=1, keepdims=True)).astype(jnp.bfloat16)
        mixture = jnp.dot(weight, value, preferred_element_type=jnp.float32)
        out_ref[:, at] = (mixture[:, :HEAD_DIM] / mixture[:, HEAD_DIM:]).astype(jnp.bfloat16)


def attend(query_rows, key_value_rows, halo, windows, spots, part):
    rows, features = query_rows.shape
    width = features // PARTS
    heads = width // HEAD_DIM
    steps = 2 if heads % 2 == 0 else 1
    block = width // steps
    halo_rows = halo.shape[1]
    first = part * steps
    keys = pl.cdiv(rows + halo_rows, LANES) * LANES
    return pl.pallas_call(
        functools.partial(attend_kernel, spots),
        grid=(steps,),
        out_shape=jax.ShapeDtypeStruct((rows, width), jnp.bfloat16),
        in_specs=[
            IN_SMEM,
            pl.BlockSpec((rows, block), lambda i: (0, first + i)),
            pl.BlockSpec((None, rows, block), lambda i: (0, 0, first + i)),
            pl.BlockSpec((None, rows, block), lambda i: (1, 0, first + i)),
            pl.BlockSpec((None, halo_rows, block), lambda i: (0, 0, first + i)),
            pl.BlockSpec((None, halo_rows, block), lambda i: (1, 0, first + i)),
        ],
        out_specs=pl.BlockSpec((rows, block), lambda i: (0, i)),
        scratch_shapes=[pltpu.VMEM((rows, keys), jnp.float32)],
        compiler_params=pltpu.CompilerParams(vmem_limit_bytes=VMEM_BYTES),
        cost_estimate=pl.CostEstimate(
            flops=4 * rows * keys * width, bytes_accessed=2 * width * (2 * rows + 2 * keys), transcendentals=heads * rows * keys
        ),
        name="attend",
    )(windows, query_rows, key_value_rows, key_value_rows, halo, halo)


def project_kernel(strip, column, total, fixed, tables_ref, *refs):
    a_refs, refs = refs[: 2 * PARTS], refs[2 * PARTS :]
    w_refs, refs = refs[: len(fixed)], refs[len(fixed) :]
    gate_refs, out_refs, (rows_all, weight, arrived) = refs[:2], refs[2:4], refs[4:]
    owner, slab = lax.axis_index("owner"), lax.axis_index("slab")
    rows, part_width = a_refs[0].shape
    row_copies = []
    for index, a_ref in enumerate(a_refs):
        block, part = divmod(index, PARTS)
        target = rows_all.at[block * rows : (block + 1) * rows, part * part_width : (part + 1) * part_width]
        row_copies.append(pltpu.make_async_copy(a_ref, target, arrived.at[len(fixed) + index]))
        row_copies[-1].start()
    for where in range(2):
        for index, (place, holder) in enumerate(fixed):
            if place != where:
                continue
            at = slice(where * strip, (where + 1) * strip)
            target = weight.at[tables_ref[slab, owner, index], :, at]
            copy = pltpu.make_async_copy(w_refs[index], target, arrived.at[index])
            if holder is None:
                copy.start()
            else:
                pl.when(slab == holder)(copy.start)
    for copy in row_copies:
        copy.wait()
    tile = 2 * LANES if strip % (2 * LANES) == 0 else LANES
    for where in range(2):
        for index, (place, holder) in enumerate(fixed):
            if place != where:
                continue
            copy = pltpu.make_async_copy(w_refs[index], weight.at[0, :, :strip], arrived.at[index])
            if holder is None:
                copy.wait()
            else:
                pl.when(slab == holder)(copy.wait)
        for first in range(where * strip, (where + 1) * strip, tile):
            columns = weight[:, :, first : first + tile].reshape(-1, tile)
            product = jnp.dot(rows_all[...], columns, preferred_element_type=jnp.float32)
            here = pl.ds(pl.multiple_of(lax.axis_index("groups") * total + column + first, LANES), tile)
            for block in range(2):
                gate = gate_refs[block][:, here]
                result = product[block * rows : (block + 1) * rows] * gate
                out_refs[block][:, first : first + tile] = result.astype(jnp.bfloat16)


def project(table, a_blocks, chunks, fixed, gates, column, total):
    slabs, count, held = table.shape
    rows, part_width = a_blocks[0].shape
    depth, strip = chunks[0].shape
    width = 2 * strip
    return pl.pallas_call(
        functools.partial(project_kernel, strip, column, total, fixed),
        out_shape=[jax.ShapeDtypeStruct((rows, width), jnp.bfloat16)] * 2,
        in_specs=[IN_SMEM] + [ANYWHERE] * (len(a_blocks) + held) + [IN_VMEM] * 2,
        out_specs=[IN_VMEM] * 2,
        scratch_shapes=[
            pltpu.VMEM((2 * rows, PARTS * part_width), jnp.bfloat16),
            pltpu.VMEM((count, depth, width), jnp.bfloat16),
            pltpu.SemaphoreType.DMA((held + len(a_blocks),)),
        ],
        compiler_params=pltpu.CompilerParams(vmem_limit_bytes=VMEM_BYTES),
        cost_estimate=pl.CostEstimate(
            flops=4 * rows * width * depth * count,
            bytes_accessed=2 * (2 * rows * (depth * count + width) + count * depth * width),
            transcendentals=0,
        ),
        name="project",
    )(table, *a_blocks, *chunks, *gates)


def place_kernel(column, total, *refs):
    in_refs, (out_ref, done) = refs[:2], refs[-2:]
    width = in_refs[0].shape[1]
    group = lax.axis_index("groups")
    copies = []
    for block, in_ref in enumerate(in_refs):
        start = (1 - group if block else group) * total + column
        at = pl.ds(pl.multiple_of(start, LANES), width)
        copies.append(pltpu.make_async_copy(in_ref, out_ref.at[:, at], done.at[block]))
    run_copies(copies)


def place(blocks, out, column, total, model_width):
    rows, width = blocks[0].shape
    held = [] if out is None else [out]
    return pl.pallas_call(
        functools.partial(place_kernel, column, total),
        out_shape=jax.ShapeDtypeStruct((rows, model_width), jnp.bfloat16),
        in_specs=[IN_VMEM] * len(blocks) + [ANYWHERE] * len(held),
        out_specs=ANYWHERE,
        scratch_shapes=[pltpu.SemaphoreType.DMA((len(blocks),))],
        input_output_aliases={len(blocks): 0} if held else {},
        compiler_params=pltpu.CompilerParams(vmem_limit_bytes=VMEM_BYTES),
        cost_estimate=pl.CostEstimate(flops=0, bytes_accessed=4 * rows * width * len(blocks), transcendentals=0),
        name="place",
    )(*blocks, *held)


def hop_order(pieces, turns, opposite):
    hops, waits = [], []
    for piece in range(pieces):
        for turn in range(1, turns + 1 + opposite):
            for strip in range(2):
                step = FLIGHT + (opposite and piece > 0 and turn == 1 and strip == 0)
                waits.append(len(hops) - step)
                hops.append((piece, strip, turn))
    return hops, waits


def on_device(queries, key_value, keep, windows, gate, out_weight):
    frames_here, spots, features = queries.shape[1:]
    model_width = gate.shape[1]
    rows = frames_here * spots
    slab_index = lax.axis_index("slab")
    slabs = lax.axis_size("slab")
    total = model_width // lax.axis_size("groups")
    widths = piece_widths(total)

    count = lax.axis_size("owner")
    order = ring_order(count)
    spot_of = [order.index(owner) for owner in range(count)]
    ways = [
        [(owner * slabs + slab, order[(spot_of[owner] + step) % count] * slabs + slab) for owner in range(count)]
        for slab, step in enumerate((1, -1))
    ]
    turns, opposite = (count - 1) // 2, count % 2 == 0
    hops, needs = hop_order(len(widths), turns, opposite)

    firsts = [2 * sum(widths[:piece]) for piece in range(len(widths))]
    held, arrived, crossed = {}, [], {}
    for piece, width in enumerate(widths):
        for strip, own in enumerate(cut(out_weight, [width] * 2, firsts[piece], total)):
            held[piece, strip, 0] = own
    edge, near_gate = border(key_value, after(keep, held[0, 0, 0]), gate)

    def hop(slot, *others):
        if slot >= len(hops):
            return
        piece, strip, turn = hops[slot]
        waits = list(others)
        if needs[slot] >= 0:
            waits.append(arrived[needs[slot]])
        if slot >= 2 * FLIGHT + 1:
            waits.append(crossed[hops[slot - 2 * FLIGHT - 1]])
        value = held[piece, strip, turn - 1]
        if waits:
            value = after(value, *waits)
        ring = ways[0] + ways[1] if turn <= turns else ways[strip]
        value = lax.ppermute(value, ("owner", "slab"), ring)
        held[hops[slot]] = value
        arrived.append(value)
        crossed[hops[slot]] = swap(after(value, arrived[slot - 1]) if slot else value, ("slab",))

    first_done = max(slot for slot, at in enumerate(hops) if at[0] == 0) if hops else 0
    hop(0)
    hop(1)
    halo = swap(edge, ("slab",))
    gates = (near_gate, swap(near_gate, ("groups",)))

    query_rows = queries.reshape(rows, features)
    key_value_rows = key_value.reshape(2, rows, features)
    near, far = [], []
    waits = {FLIGHT + PARTS: [held[piece, 0, 0] for piece in range(1, len(widths))]}
    for part in range(PARTS):
        query = after(query_rows, *(arrived[part - 1 : part] if part else gates[1:]))
        attended = attend(query, key_value_rows, halo, windows, spots, part)
        hop(FLIGHT + part, attended)
        across = swap(attended, ("groups",))
        near.append(attended)
        far.append(across)
        waits.setdefault(max(first_done - 2 * (PARTS - 1 - part), FLIGHT + PARTS), []).append(across)

    def project_piece(piece, *others):
        chunks = [held[piece, 0, 0], held[piece, 1, 0]]
        fixed = [(0, None), (1, None)]
        sources = [(0, 0), (0, 0)]
        for turn in range(1, turns + 1 + opposite):
            for strip in range(2):
                chunks += [held[piece, strip, turn], crossed[piece, strip, turn]]
                fixed += [(strip, None)] * 2 if turn <= turns else [(strip, strip), (strip, 1 - strip)]
                sources += [(-turn, turn), (turn, -turn)]
        table = np.zeros((slabs, count, len(chunks)), np.int32)
        for slab in range(slabs):
            for owner in range(count):
                table[slab, owner] = [order[(spot_of[owner] + source[slab]) % count] for source in sources]
        if others:
            chunks[0] = after(chunks[0], *others)
        column = firsts[piece]
        own, away = project(jnp.asarray(table), near + far, chunks, tuple(fixed), gates, column, total)
        return [own, swap(away, ("groups",))], column

    results = []
    for slot in range(FLIGHT + PARTS, len(hops)):
        if slot == first_done + FLIGHT + opposite:
            results.append(project_piece(0))
            waits.setdefault(slot, []).append(results[0][0][0])
        hop(slot, *waits.get(slot, []))
    for piece in range(len(results), len(widths)):
        results.append(project_piece(piece, *(results[-1][0][1:] if results else [])))
    out = None
    for blocks, column in results:
        out = place(blocks, out, column, total, model_width)
    return out.reshape((1, frames_here, spots, model_width))


def solution(mesh):
    placed = (
        P(("groups", "owner"), "slab", None, None),
        P(None, ("groups", "owner"), "slab", None, None),
        P("groups"),
        P("groups", None),
        P("groups", None),
        P("owner", None),
    )
    return jax.shard_map(
        on_device,
        mesh=mesh,
        in_specs=placed,
        out_specs=P(("groups", "owner"), "slab", None, None),
        check_vma=False,
    )
```

```python
import functools
import math

import jax
import jax.numpy as jnp
import numpy as np
from jax import lax
from jax.experimental import pallas as pl
from jax.experimental.pallas import tpu as pltpu
from jax.sharding import PartitionSpec as P

HEAD_DIM = 128
WB = 14
HALO = 1
LANES = 128
NEG_LARGE = -1e30
PARTS = 2
FLIGHT = 2
VMEM_BYTES = 24 * 1024 * 1024
ANYWHERE = pl.BlockSpec(memory_space=pl.ANY)
IN_HBM = pl.BlockSpec(memory_space=pltpu.HBM)
IN_VMEM = pl.BlockSpec(memory_space=pltpu.VMEM)
IN_SMEM = pl.BlockSpec(memory_space=pltpu.SMEM)


def ring_order(count):
    width = max(w for w in range(1, count + 1) if count % w == 0 and w * w <= count)
    height = count // width
    if width == 1 or height % 2:
        return list(range(count))
    order = []
    for row in range(height):
        columns = range(1, width) if row % 2 == 0 else range(width - 1, 0, -1)
        order += [row * width + column for column in columns]
    return order + [row * width for row in range(height - 1, -1, -1)]


def piece_widths(half_width):
    tiles = half_width // (2 * LANES)
    late = 2 * tiles // 5
    return [count * LANES for count in (tiles - late, late) if count]


def swap(value, axes):
    count = math.prod(lax.axis_size(axis) for axis in axes)
    return lax.ppermute(value, axes, [(i, count - 1 - i) for i in range(count)])


def after(value, *others):
    return lax.optimization_barrier((value,) + others)[0]


def run_copies(copies):
    for copy in copies:
        copy.start()
    for copy in copies:
        copy.wait()


def through(sources, buffers, targets, arrived, left):
    first = [pltpu.make_async_copy(s, b, arrived.at[i]) for i, (s, b) in enumerate(zip(sources, buffers))]
    second = [pltpu.make_async_copy(b, t, left.at[i]) for i, (b, t) in enumerate(zip(buffers, targets))]
    for copy in first:
        copy.start()
    for before, copy in zip(first, second):
        before.wait()
        copy.start()
    for copy in second:
        copy.wait()


def cut_kernel(first, total, weight_ref, *refs):
    count = len(refs) // 2 - 1
    out_refs, buffers, (arrived, left) = refs[:count], refs[count : 2 * count], refs[2 * count :]
    column = lax.axis_index("groups") * total + first
    sources = []
    for ref in out_refs:
        sources.append(weight_ref.at[:, pl.ds(pl.multiple_of(column, LANES), ref.shape[1])])
        column += ref.shape[1]
    through(sources, buffers, out_refs, arrived, left)


def cut(out_weight, strips, first, total):
    depth = out_weight.shape[0]
    out_weight = pltpu.with_memory_space_constraint(out_weight, pltpu.HBM)
    return pl.pallas_call(
        functools.partial(cut_kernel, first, total),
        out_shape=[jax.ShapeDtypeStruct((depth, width), jnp.bfloat16) for width in strips],
        in_specs=[IN_HBM],
        out_specs=[IN_HBM] * len(strips),
        scratch_shapes=[pltpu.VMEM((depth, width), jnp.bfloat16) for width in strips]
        + [pltpu.SemaphoreType.DMA((len(strips),))] * 2,
        compiler_params=pltpu.CompilerParams(vmem_limit_bytes=VMEM_BYTES),
        cost_estimate=pl.CostEstimate(flops=0, bytes_accessed=4 * depth * sum(strips), transcendentals=0),
        name="cut",
    )(out_weight)


def scale_kernel(keep_ref, gate_ref, out_ref):
    owner = lax.axis_index("owner")
    factor = jnp.where(owner % 2 == 1, keep_ref[owner // 2], 1).astype(jnp.float32)
    out_ref[...] = gate_ref[pl.ds(owner // 2, 1), :] * factor


def scale_gate(keep, gate):
    return pl.pallas_call(
        scale_kernel,
        out_shape=jax.ShapeDtypeStruct((1, gate.shape[1]), jnp.float32),
        in_specs=[IN_SMEM, IN_VMEM],
        out_specs=IN_VMEM,
        name="scale_gate",
    )(keep, gate)


def token_place(count, dim, spots, first_frame):
    shape = (count, 1) if dim == 0 else (1, count)
    token = lax.broadcasted_iota(jnp.int32, shape, dim).astype(jnp.float32)
    frame = jnp.floor((token + 0.5) * (1.0 / spots))
    spot = token - frame * spots
    row = jnp.floor((spot + 0.5) * (1.0 / WB))
    return frame + first_frame, row, spot - row * WB


def attend_kernel(spots, windows_ref, q_ref, k_ref, v_ref, k_other_ref, v_other_ref, *refs):
    out_ref, bias = refs[-2:]
    rows = q_ref.shape[0]
    halo_rows = HALO * spots
    first_row = jnp.where(lax.axis_index("slab") == 0, 0, rows - halo_rows)
    halo = pl.ds(pl.multiple_of(first_row, 16 if spots % 16 == 0 else 8), halo_rows)
    keys = bias.shape[1]
    frames_here = rows // spots

    @pl.when(pl.program_id(0) == 0)
    def _():
        request = lax.axis_index("owner") // 2
        halo_frame = jnp.where(lax.axis_index("slab") == 0, 0, -HALO - frames_here).astype(jnp.float32)
        query = token_place(rows, 0, spots, 0.0)
        key = token_place(keys, 1, spots, 0.0)
        index = lax.broadcasted_iota(jnp.int32, (1, keys), 1)
        frame = jnp.where(index < rows, key[0], key[0] + halo_frame)
        frame = jnp.where(index < rows + halo_rows, frame, -NEG_LARGE)
        allowed = None
        for part, place in enumerate((frame, key[1], key[2])):
            near = jnp.abs(query[part] - place) <= windows_ref[request, part].astype(jnp.float32)
            allowed = near if allowed is None else allowed & near
        bias[...] = jnp.where(allowed, 0.0, NEG_LARGE)

    scale = math.log2(math.e) / math.sqrt(HEAD_DIM)
    pad = jnp.zeros((keys - rows - halo_rows, HEAD_DIM), jnp.bfloat16)
    ones = jnp.ones((keys, HEAD_DIM), jnp.bfloat16)
    for head in range(q_ref.shape[1] // HEAD_DIM):
        at = slice(head * HEAD_DIM, (head + 1) * HEAD_DIM)
        key = jnp.concatenate([k_ref[:, at], k_other_ref[halo, at], pad], axis=0)
        value = jnp.concatenate([v_ref[:, at], v_other_ref[halo, at], pad], axis=0)
        value = jnp.concatenate([value, ones], axis=1)
        score = lax.dot_general(q_ref[:, at], key, (((1,), (1,)), ((), ())), preferred_element_type=jnp.float32)
        score = score * scale + bias[...]
        weight = jnp.exp2(score - jnp.max(score, axis=1, keepdims=True)).astype(jnp.bfloat16)
        mixture = jnp.dot(weight, value, preferred_element_type=jnp.float32)
        out_ref[:, at] = (mixture[:, :HEAD_DIM] / mixture[:, HEAD_DIM:]).astype(jnp.bfloat16)


def attend(query_rows, key_value_rows, other_rows, windows, spots, part, attended):
    before = [] if attended is None else [attended]
    rows, features = query_rows.shape
    width = features // PARTS
    heads = width // HEAD_DIM
    steps = 2 if heads % 2 == 0 else 1
    block = width // steps
    halo_rows = HALO * spots
    first = part * steps
    keys = pl.cdiv(rows + halo_rows, LANES) * LANES
    return pl.pallas_call(
        functools.partial(attend_kernel, spots),
        grid=(steps,),
        out_shape=jax.ShapeDtypeStruct((rows, features), jnp.bfloat16),
        in_specs=[
            IN_SMEM,
            pl.BlockSpec((rows, block), lambda i: (0, first + i)),
            pl.BlockSpec((None, rows, block), lambda i: (0, 0, first + i)),
            pl.BlockSpec((None, rows, block), lambda i: (1, 0, first + i)),
            pl.BlockSpec((None, rows, block), lambda i: (0, 0, first + i)),
            pl.BlockSpec((None, rows, block), lambda i: (1, 0, first + i)),
        ]
        + [ANYWHERE] * len(before),
        out_specs=pl.BlockSpec((rows, block), lambda i: (0, first + i)),
        input_output_aliases={6: 0} if before else {},
        scratch_shapes=[pltpu.VMEM((rows, keys), jnp.float32)],
        compiler_params=pltpu.CompilerParams(vmem_limit_bytes=VMEM_BYTES),
        cost_estimate=pl.CostEstimate(
            flops=4 * rows * keys * width, bytes_accessed=2 * width * (2 * rows + 2 * keys), transcendentals=heads * rows * keys
        ),
        name="attend",
    )(windows, query_rows, key_value_rows, key_value_rows, other_rows, other_rows, *before)


def project_kernel(strip, column, total, fixed, tables_ref, *refs):
    a_refs, refs = refs[:2], refs[2:]
    w_refs, refs = refs[: len(fixed)], refs[len(fixed) :]
    gate_refs, out_refs, (rows_all, weight, arrived) = refs[:2], refs[2:4], refs[4:]
    owner, slab = lax.axis_index("owner"), lax.axis_index("slab")
    rows = a_refs[0].shape[0]
    row_copies = []
    for index, a_ref in enumerate(a_refs):
        target = rows_all.at[index * rows : (index + 1) * rows]
        row_copies.append(pltpu.make_async_copy(a_ref, target, arrived.at[len(fixed) + index]))
        row_copies[-1].start()
    for where in range(2):
        for index, (place, holder) in enumerate(fixed):
            if place != where:
                continue
            at = slice(where * strip, (where + 1) * strip)
            target = weight.at[tables_ref[slab, owner, index], :, at]
            copy = pltpu.make_async_copy(w_refs[index], target, arrived.at[index])
            if holder is None:
                copy.start()
            else:
                pl.when(slab == holder)(copy.start)
    for copy in row_copies:
        copy.wait()
    tile = 2 * LANES if strip % (2 * LANES) == 0 else LANES
    for where in range(2):
        for index, (place, holder) in enumerate(fixed):
            if place != where:
                continue
            copy = pltpu.make_async_copy(w_refs[index], weight.at[0, :, :strip], arrived.at[index])
            if holder is None:
                copy.wait()
            else:
                pl.when(slab == holder)(copy.wait)
        for first in range(where * strip, (where + 1) * strip, tile):
            columns = weight[:, :, first : first + tile].reshape(-1, tile)
            product = jnp.dot(rows_all[...], columns, preferred_element_type=jnp.float32)
            here = pl.ds(pl.multiple_of(lax.axis_index("groups") * total + column + first, LANES), tile)
            for block in range(2):
                gate = gate_refs[block][:, here]
                result = product[block * rows : (block + 1) * rows] * gate
                out_refs[block][:, first : first + tile] = result.astype(jnp.bfloat16)


def project(table, a_blocks, chunks, fixed, gates, column, total):
    slabs, count, held = table.shape
    rows, features = a_blocks[0].shape
    depth, strip = chunks[0].shape
    width = 2 * strip
    return pl.pallas_call(
        functools.partial(project_kernel, strip, column, total, fixed),
        out_shape=[jax.ShapeDtypeStruct((rows, width), jnp.bfloat16)] * 2,
        in_specs=[IN_SMEM] + [ANYWHERE] * (len(a_blocks) + held) + [IN_VMEM] * 2,
        out_specs=[IN_VMEM] * 2,
        scratch_shapes=[
            pltpu.VMEM((2 * rows, features), jnp.bfloat16),
            pltpu.VMEM((count, depth, width), jnp.bfloat16),
            pltpu.SemaphoreType.DMA((held + len(a_blocks),)),
        ],
        compiler_params=pltpu.CompilerParams(vmem_limit_bytes=VMEM_BYTES),
        cost_estimate=pl.CostEstimate(
            flops=4 * rows * width * depth * count,
            bytes_accessed=2 * (2 * rows * (depth * count + width) + count * depth * width),
            transcendentals=0,
        ),
        name="project",
    )(table, *a_blocks, *chunks, *gates)


def place_kernel(column, total, *refs):
    in_refs, (out_ref, done) = refs[:2], refs[-2:]
    width = in_refs[0].shape[1]
    group = lax.axis_index("groups")
    copies = []
    for block, in_ref in enumerate(in_refs):
        start = (1 - group if block else group) * total + column
        at = pl.ds(pl.multiple_of(start, LANES), width)
        copies.append(pltpu.make_async_copy(in_ref, out_ref.at[:, at], done.at[block]))
    run_copies(copies)


def place(blocks, out, column, total, model_width):
    rows, width = blocks[0].shape
    held = [] if out is None else [out]
    return pl.pallas_call(
        functools.partial(place_kernel, column, total),
        out_shape=jax.ShapeDtypeStruct((rows, model_width), jnp.bfloat16),
        in_specs=[IN_VMEM] * len(blocks) + [ANYWHERE] * len(held),
        out_specs=ANYWHERE,
        scratch_shapes=[pltpu.SemaphoreType.DMA((len(blocks),))],
        input_output_aliases={len(blocks): 0} if held else {},
        compiler_params=pltpu.CompilerParams(vmem_limit_bytes=VMEM_BYTES),
        cost_estimate=pl.CostEstimate(flops=0, bytes_accessed=4 * rows * width * len(blocks), transcendentals=0),
        name="place",
    )(*blocks, *held)


def hop_order(pieces, turns, opposite):
    hops, late = [], []
    for piece in range(pieces):
        for turn in range(1, turns + 1):
            for strip in range(2):
                hops += [(piece, strip, turn)] + late
                late = []
        late = [(piece, None, turns + 1)] if opposite else []
    return hops + late


def on_device(queries, key_value, keep, windows, gate, out_weight):
    frames_here, spots, features = queries.shape[1:]
    model_width = gate.shape[1]
    rows = frames_here * spots
    slab_index = lax.axis_index("slab")
    slabs = lax.axis_size("slab")
    total = model_width // lax.axis_size("groups")
    widths = piece_widths(total)

    count = lax.axis_size("owner")
    order = ring_order(count)
    spot_of = [order.index(owner) for owner in range(count)]
    ring = [
        (owner * slabs + slab, order[(spot_of[owner] + step) % count] * slabs + slab)
        for owner in range(count)
        for slab, step in enumerate((1, -1))
    ]
    turns, opposite = (count - 1) // 2, count % 2 == 0
    hops = hop_order(len(widths), turns, opposite)

    firsts = [2 * sum(widths[:piece]) for piece in range(len(widths))]
    held, arrived, crossed = {}, [], {}
    for piece, width in enumerate(widths):
        for strip, own in enumerate(cut(out_weight, [width] * 2, firsts[piece], total)):
            held[piece, strip, 0] = own
    def hop(slot, *others):
        if slot >= len(hops):
            return
        piece, strip, turn = hops[slot]
        waits = list(others)
        if slot >= FLIGHT:
            waits.append(arrived[slot - FLIGHT])
        if slot >= 2 * FLIGHT + 1:
            waits.append(crossed[hops[slot - 2 * FLIGHT - 1]])
        if strip is None:
            value = jnp.where(slab_index == 0, held[piece, 0, turn - 1], held[piece, 1, turn - 1])
        else:
            value = held[piece, strip, turn - 1]
        if waits:
            value = after(value, *waits)
        value = lax.ppermute(value, ("owner", "slab"), ring)
        held[hops[slot]] = value
        arrived.append(value)
        crossed[hops[slot]] = swap(after(value, arrived[slot - 1]) if slot else value, ("slab",))

    first_done = max(slot for slot, at in enumerate(hops) if at[0] == 0) if hops else 0
    other = swap(key_value, ("slab",))
    hop(0)
    hop(1)

    query_rows = queries.reshape(rows, features)
    key_value_rows = key_value.reshape(2, rows, features)
    other_rows = other.reshape(2, rows, features)
    waits = {FLIGHT + PARTS: [held[piece, 0, 0] for piece in range(1, len(widths))]}
    attended = None
    for part in range(PARTS):
        query = after(query_rows, arrived[part - 1]) if part else query_rows
        attended = attend(query, key_value_rows, other_rows, windows, spots, part, attended)
        hop(FLIGHT + part, attended)
    a_blocks = (attended, swap(attended, ("groups",)))
    near_gate = scale_gate(after(keep, attended), gate)
    gates = (near_gate, swap(near_gate, ("groups",)))
    waits.setdefault(max(first_done, FLIGHT + PARTS), []).extend((a_blocks[1], gates[1]))

    def project_piece(piece, *others):
        chunks = [held[piece, 0, 0], held[piece, 1, 0]]
        fixed = [(0, None), (1, None)]
        sources = [(0, 0), (0, 0)]
        for turn in range(1, turns + 1):
            for strip in range(2):
                chunks += [held[piece, strip, turn], crossed[piece, strip, turn]]
                fixed += [(strip, None)] * 2
                sources += [(-turn, turn), (turn, -turn)]
        if opposite:
            chunks += [held[piece, None, turns + 1], crossed[piece, None, turns + 1]] * 2
            fixed += [(strip, strip ^ mate) for strip in range(2) for mate in range(2)]
            sources += [(turns + 1, turns + 1)] * 4
        table = np.zeros((slabs, count, len(chunks)), np.int32)
        for slab in range(slabs):
            for owner in range(count):
                table[slab, owner] = [order[(spot_of[owner] + source[slab]) % count] for source in sources]
        if others:
            chunks[0] = after(chunks[0], *others)
        column = firsts[piece]
        own, away = project(jnp.asarray(table), a_blocks, chunks, tuple(fixed), gates, column, total)
        return [own, swap(away, ("groups",))], column

    results = []
    for slot in range(FLIGHT + PARTS, len(hops)):
        if slot == first_done + FLIGHT + 1:
            results.append(project_piece(0))
            waits.setdefault(slot, []).append(results[0][0][0])
        hop(slot, *waits.get(slot, []))
    for piece in range(len(results), len(widths)):
        results.append(project_piece(piece, *(results[-1][0][1:] if results else [])))
    out = None
    for blocks, column in results:
        out = place(blocks, out, column, total, model_width)
    return out.reshape((1, frames_here, spots, model_width))


def solution(mesh):
    placed = (
        P(("groups", "owner"), "slab", None, None),
        P(None, ("groups", "owner"), "slab", None, None),
        P("groups"),
        P("groups", None),
        P("groups", None),
        P("owner", None),
    )
    return jax.shard_map(
        on_device,
        mesh=mesh,
        in_specs=placed,
        out_specs=P(("groups", "owner"), "slab", None, None),
        check_vma=False,
    )
```

```python
import functools
import math

import jax
import jax.numpy as jnp
import numpy as np
from jax import lax
from jax.experimental import pallas as pl
from jax.experimental.pallas import tpu as pltpu
from jax.sharding import PartitionSpec as P

HEAD_DIM = 128
WB = 14
HALO = 1
LANES = 128
NEG_LARGE = -1e30
PARTS = 2
FLIGHT = 3
VMEM_BYTES = 24 * 1024 * 1024
ANYWHERE = pl.BlockSpec(memory_space=pl.ANY)
IN_HBM = pl.BlockSpec(memory_space=pltpu.HBM)
IN_VMEM = pl.BlockSpec(memory_space=pltpu.VMEM)
IN_SMEM = pl.BlockSpec(memory_space=pltpu.SMEM)


def ring_order(count):
    width = max(w for w in range(1, count + 1) if count % w == 0 and w * w <= count)
    height = count // width
    if width == 1 or height % 2:
        return list(range(count))
    order = []
    for row in range(height):
        columns = range(1, width) if row % 2 == 0 else range(width - 1, 0, -1)
        order += [row * width + column for column in columns]
    return order + [row * width for row in range(height - 1, -1, -1)]


def piece_widths(half_width):
    tiles = half_width // (2 * LANES)
    late = 2 * tiles // 5
    return [count * LANES for count in (tiles - late, late) if count]


def swap(value, axes):
    count = math.prod(lax.axis_size(axis) for axis in axes)
    return lax.ppermute(value, axes, [(i, count - 1 - i) for i in range(count)])


def after(value, *others):
    return lax.optimization_barrier((value,) + others)[0]


def run_copies(copies):
    for copy in copies:
        copy.start()
    for copy in copies:
        copy.wait()


def through(sources, buffers, targets, arrived, left):
    first = [pltpu.make_async_copy(s, b, arrived.at[i]) for i, (s, b) in enumerate(zip(sources, buffers))]
    second = [pltpu.make_async_copy(b, t, left.at[i]) for i, (b, t) in enumerate(zip(buffers, targets))]
    for copy in first:
        copy.start()
    for before, copy in zip(first, second):
        before.wait()
        copy.start()
    for copy in second:
        copy.wait()


def cut_kernel(first, total, weight_ref, *refs):
    count = len(refs) // 2 - 1
    out_refs, buffers, (arrived, left) = refs[:count], refs[count : 2 * count], refs[2 * count :]
    column = lax.axis_index("groups") * total + first
    sources = []
    for ref in out_refs:
        sources.append(weight_ref.at[:, pl.ds(pl.multiple_of(column, LANES), ref.shape[1])])
        column += ref.shape[1]
    through(sources, buffers, out_refs, arrived, left)


def cut(out_weight, strips, first, total):
    depth = out_weight.shape[0]
    out_weight = pltpu.with_memory_space_constraint(out_weight, pltpu.HBM)
    return pl.pallas_call(
        functools.partial(cut_kernel, first, total),
        out_shape=[jax.ShapeDtypeStruct((depth, width), jnp.bfloat16) for width in strips],
        in_specs=[IN_HBM],
        out_specs=[IN_HBM] * len(strips),
        scratch_shapes=[pltpu.VMEM((depth, width), jnp.bfloat16) for width in strips]
        + [pltpu.SemaphoreType.DMA((len(strips),))] * 2,
        compiler_params=pltpu.CompilerParams(vmem_limit_bytes=VMEM_BYTES),
        cost_estimate=pl.CostEstimate(flops=0, bytes_accessed=4 * depth * sum(strips), transcendentals=0),
        name="cut",
    )(out_weight)


def scale_kernel(keep_ref, gate_ref, out_ref):
    owner = lax.axis_index("owner")
    factor = jnp.where(owner % 2 == 1, keep_ref[owner // 2], 1).astype(jnp.float32)
    out_ref[...] = gate_ref[pl.ds(owner // 2, 1), :] * factor


def scale_gate(keep, gate):
    return pl.pallas_call(
        scale_kernel,
        out_shape=jax.ShapeDtypeStruct((1, gate.shape[1]), jnp.float32),
        in_specs=[IN_SMEM, IN_VMEM],
        out_specs=IN_VMEM,
        name="scale_gate",
    )(keep, gate)


def token_place(count, dim, spots, first_frame):
    shape = (count, 1) if dim == 0 else (1, count)
    token = lax.broadcasted_iota(jnp.int32, shape, dim).astype(jnp.float32)
    frame = jnp.floor((token + 0.5) * (1.0 / spots))
    spot = token - frame * spots
    row = jnp.floor((spot + 0.5) * (1.0 / WB))
    return frame + first_frame, row, spot - row * WB


def attend_kernel(spots, windows_ref, q_ref, k_ref, v_ref, k_other_ref, v_other_ref, *refs):
    out_ref, bias = refs[-2:]
    rows = q_ref.shape[0]
    halo_rows = HALO * spots
    first_row = jnp.where(lax.axis_index("slab") == 0, 0, rows - halo_rows)
    halo = pl.ds(pl.multiple_of(first_row, 16 if spots % 16 == 0 else 8), halo_rows)
    keys = bias.shape[1]
    frames_here = rows // spots

    @pl.when(pl.program_id(0) == 0)
    def _():
        request = lax.axis_index("owner") // 2
        halo_frame = jnp.where(lax.axis_index("slab") == 0, 0, -HALO - frames_here).astype(jnp.float32)
        query = token_place(rows, 0, spots, 0.0)
        key = token_place(keys, 1, spots, 0.0)
        index = lax.broadcasted_iota(jnp.int32, (1, keys), 1)
        frame = jnp.where(index < rows, key[0], key[0] + halo_frame)
        frame = jnp.where(index < rows + halo_rows, frame, -NEG_LARGE)
        allowed = None
        for part, place in enumerate((frame, key[1], key[2])):
            near = jnp.abs(query[part] - place) <= windows_ref[request, part].astype(jnp.float32)
            allowed = near if allowed is None else allowed & near
        bias[...] = jnp.where(allowed, 0.0, NEG_LARGE)

    scale = math.log2(math.e) / math.sqrt(HEAD_DIM)
    pad = jnp.zeros((keys - rows - halo_rows, HEAD_DIM), jnp.bfloat16)
    ones = jnp.ones((keys, HEAD_DIM), jnp.bfloat16)
    for head in range(q_ref.shape[1] // HEAD_DIM):
        at = slice(head * HEAD_DIM, (head + 1) * HEAD_DIM)
        key = jnp.concatenate([k_ref[:, at], k_other_ref[halo, at], pad], axis=0)
        value = jnp.concatenate([v_ref[:, at], v_other_ref[halo, at], pad], axis=0)
        value = jnp.concatenate([value, ones], axis=1)
        score = lax.dot_general(q_ref[:, at], key, (((1,), (1,)), ((), ())), preferred_element_type=jnp.float32)
        score = score * scale + bias[...]
        weight = jnp.exp2(score - jnp.max(score, axis=1, keepdims=True)).astype(jnp.bfloat16)
        mixture = jnp.dot(weight, value, preferred_element_type=jnp.float32)
        out_ref[:, at] = (mixture[:, :HEAD_DIM] / mixture[:, HEAD_DIM:]).astype(jnp.bfloat16)


def attend(query_rows, key_value_rows, other_rows, windows, spots, part, attended):
    before = [] if attended is None else [attended]
    rows, features = query_rows.shape
    width = features // PARTS
    heads = width // HEAD_DIM
    steps = 2 if heads % 2 == 0 else 1
    block = width // steps
    halo_rows = HALO * spots
    first = part * steps
    keys = pl.cdiv(rows + halo_rows, LANES) * LANES
    return pl.pallas_call(
        functools.partial(attend_kernel, spots),
        grid=(steps,),
        out_shape=jax.ShapeDtypeStruct((rows, features), jnp.bfloat16),
        in_specs=[
            IN_SMEM,
            pl.BlockSpec((rows, block), lambda i: (0, first + i)),
            pl.BlockSpec((None, rows, block), lambda i: (0, 0, first + i)),
            pl.BlockSpec((None, rows, block), lambda i: (1, 0, first + i)),
            pl.BlockSpec((None, rows, block), lambda i: (0, 0, first + i)),
            pl.BlockSpec((None, rows, block), lambda i: (1, 0, first + i)),
        ]
        + [ANYWHERE] * len(before),
        out_specs=pl.BlockSpec((rows, block), lambda i: (0, first + i)),
        input_output_aliases={6: 0} if before else {},
        scratch_shapes=[pltpu.VMEM((rows, keys), jnp.float32)],
        compiler_params=pltpu.CompilerParams(vmem_limit_bytes=VMEM_BYTES),
        cost_estimate=pl.CostEstimate(
            flops=4 * rows * keys * width, bytes_accessed=2 * width * (2 * rows + 2 * keys), transcendentals=heads * rows * keys
        ),
        name="attend",
    )(windows, query_rows, key_value_rows, key_value_rows, other_rows, other_rows, *before)


def project_kernel(strip, column, total, fixed, tables_ref, *refs):
    a_refs, refs = refs[:2], refs[2:]
    w_refs, refs = refs[: len(fixed)], refs[len(fixed) :]
    gate_refs, out_refs, (rows_all, weight, arrived) = refs[:2], refs[2:4], refs[4:]
    owner, slab = lax.axis_index("owner"), lax.axis_index("slab")
    rows = a_refs[0].shape[0]
    row_copies = []
    for index, a_ref in enumerate(a_refs):
        target = rows_all.at[index * rows : (index + 1) * rows]
        row_copies.append(pltpu.make_async_copy(a_ref, target, arrived.at[len(fixed) + index]))
        row_copies[-1].start()
    for where in range(2):
        for index, (place, holder) in enumerate(fixed):
            if place != where:
                continue
            at = slice(where * strip, (where + 1) * strip)
            target = weight.at[tables_ref[slab, owner, index], :, at]
            copy = pltpu.make_async_copy(w_refs[index], target, arrived.at[index])
            if holder is None:
                copy.start()
            else:
                pl.when(slab == holder)(copy.start)
    for copy in row_copies:
        copy.wait()
    tile = 2 * LANES if strip % (2 * LANES) == 0 else LANES
    for where in range(2):
        for index, (place, holder) in enumerate(fixed):
            if place != where:
                continue
            copy = pltpu.make_async_copy(w_refs[index], weight.at[0, :, :strip], arrived.at[index])
            if holder is None:
                copy.wait()
            else:
                pl.when(slab == holder)(copy.wait)
        for first in range(where * strip, (where + 1) * strip, tile):
            columns = weight[:, :, first : first + tile].reshape(-1, tile)
            product = jnp.dot(rows_all[...], columns, preferred_element_type=jnp.float32)
            here = pl.ds(pl.multiple_of(lax.axis_index("groups") * total + column + first, LANES), tile)
            for block in range(2):
                gate = gate_refs[block][:, here]
                result = product[block * rows : (block + 1) * rows] * gate
                out_refs[block][:, first : first + tile] = result.astype(jnp.bfloat16)


def project(table, a_blocks, chunks, fixed, gates, column, total):
    slabs, count, held = table.shape
    rows, features = a_blocks[0].shape
    depth, strip = chunks[0].shape
    width = 2 * strip
    return pl.pallas_call(
        functools.partial(project_kernel, strip, column, total, fixed),
        out_shape=[jax.ShapeDtypeStruct((rows, width), jnp.bfloat16)] * 2,
        in_specs=[IN_SMEM] + [ANYWHERE] * (len(a_blocks) + held) + [IN_VMEM] * 2,
        out_specs=[IN_VMEM] * 2,
        scratch_shapes=[
            pltpu.VMEM((2 * rows, features), jnp.bfloat16),
            pltpu.VMEM((count, depth, width), jnp.bfloat16),
            pltpu.SemaphoreType.DMA((held + len(a_blocks),)),
        ],
        compiler_params=pltpu.CompilerParams(vmem_limit_bytes=VMEM_BYTES),
        cost_estimate=pl.CostEstimate(
            flops=4 * rows * width * depth * count,
            bytes_accessed=2 * (2 * rows * (depth * count + width) + count * depth * width),
            transcendentals=0,
        ),
        name="project",
    )(table, *a_blocks, *chunks, *gates)


def place_kernel(column, total, *refs):
    in_refs, (out_ref, done) = refs[:2], refs[-2:]
    width = in_refs[0].shape[1]
    group = lax.axis_index("groups")
    copies = []
    for block, in_ref in enumerate(in_refs):
        start = (1 - group if block else group) * total + column
        at = pl.ds(pl.multiple_of(start, LANES), width)
        copies.append(pltpu.make_async_copy(in_ref, out_ref.at[:, at], done.at[block]))
    run_copies(copies)


def place(blocks, out, column, total, model_width):
    rows, width = blocks[0].shape
    held = [] if out is None else [out]
    return pl.pallas_call(
        functools.partial(place_kernel, column, total),
        out_shape=jax.ShapeDtypeStruct((rows, model_width), jnp.bfloat16),
        in_specs=[IN_VMEM] * len(blocks) + [ANYWHERE] * len(held),
        out_specs=ANYWHERE,
        scratch_shapes=[pltpu.SemaphoreType.DMA((len(blocks),))],
        input_output_aliases={len(blocks): 0} if held else {},
        compiler_params=pltpu.CompilerParams(vmem_limit_bytes=VMEM_BYTES),
        cost_estimate=pl.CostEstimate(flops=0, bytes_accessed=4 * rows * width * len(blocks), transcendentals=0),
        name="place",
    )(*blocks, *held)


def hop_order(pieces, turns, opposite):
    order = []
    for piece in range(pieces):
        hops = [(piece, strip, turn) for turn in range(1, turns + 1) for strip in range(2)]
        hops += [(piece, None, turns + 1)] if opposite else []
        if not order:
            order = hops
            continue
        start = max([index for index, hop in enumerate(order) if hop[0] < piece - 1], default=-1) + 1
        merged, rest = order[:start], order[start:]
        while rest:
            merged += rest[:2] + hops[:1]
            rest, hops = rest[2:], hops[1:]
        order = merged + hops
    return order


def on_device(queries, key_value, keep, windows, gate, out_weight):
    frames_here, spots, features = queries.shape[1:]
    model_width = gate.shape[1]
    rows = frames_here * spots
    slab_index = lax.axis_index("slab")
    slabs = lax.axis_size("slab")
    total = model_width // lax.axis_size("groups")
    widths = piece_widths(total)

    count = lax.axis_size("owner")
    order = ring_order(count)
    spot_of = [order.index(owner) for owner in range(count)]
    ring = [
        (owner * slabs + slab, order[(spot_of[owner] + step) % count] * slabs + slab)
        for owner in range(count)
        for slab, step in enumerate((1, -1))
    ]
    turns, opposite = (count - 1) // 2, count % 2 == 0
    hops = hop_order(len(widths), turns, opposite)

    firsts = [2 * sum(widths[:piece]) for piece in range(len(widths))]
    held, arrived, crossed = {}, [], {}
    for piece, width in enumerate(widths):
        for strip, own in enumerate(cut(out_weight, [width] * 2, firsts[piece], total)):
            held[piece, strip, 0] = own
    def hop(slot, *others):
        if slot >= len(hops):
            return
        piece, strip, turn = hops[slot]
        waits = list(others)
        if slot >= FLIGHT:
            waits.append(arrived[slot - FLIGHT])
        if slot >= 2 * FLIGHT:
            waits.append(crossed[hops[slot - 2 * FLIGHT]])
        if strip is None:
            value = jnp.where(slab_index == 0, held[piece, 0, turn - 1], held[piece, 1, turn - 1])
        else:
            value = held[piece, strip, turn - 1]
        if waits:
            value = after(value, *waits)
        value = lax.ppermute(value, ("owner", "slab"), ring)
        held[hops[slot]] = value
        arrived.append(value)
        crossed[hops[slot]] = swap(value, ("slab",))

    first_done = max(slot for slot, at in enumerate(hops) if at[0] == 0) if hops else 0
    other = swap(key_value, ("slab",))
    for slot in range(FLIGHT):
        hop(slot)

    query_rows = queries.reshape(rows, features)
    key_value_rows = key_value.reshape(2, rows, features)
    other_rows = other.reshape(2, rows, features)
    waits, attended = {}, None
    for part in range(PARTS):
        attended = attend(query_rows, key_value_rows, other_rows, windows, spots, part, attended)
        hop(FLIGHT + part, attended)
    a_blocks = (attended, swap(attended, ("groups",)))
    near_gate = scale_gate(after(keep, attended), gate)
    gates = (near_gate, swap(near_gate, ("groups",)))
    waits.setdefault(max(first_done, FLIGHT + PARTS), []).append(a_blocks[1])

    def project_piece(piece, *others):
        chunks = [held[piece, 0, 0], held[piece, 1, 0]]
        fixed = [(0, None), (1, None)]
        sources = [(0, 0), (0, 0)]
        for turn in range(1, turns + 1):
            for strip in range(2):
                chunks += [held[piece, strip, turn], crossed[piece, strip, turn]]
                fixed += [(strip, None)] * 2
                sources += [(-turn, turn), (turn, -turn)]
        if opposite:
            chunks += [held[piece, None, turns + 1], crossed[piece, None, turns + 1]] * 2
            fixed += [(strip, strip ^ mate) for strip in range(2) for mate in range(2)]
            sources += [(turns + 1, turns + 1)] * 4
        table = np.zeros((slabs, count, len(chunks)), np.int32)
        for slab in range(slabs):
            for owner in range(count):
                table[slab, owner] = [order[(spot_of[owner] + source[slab]) % count] for source in sources]
        if others:
            chunks[0] = after(chunks[0], *others)
        chunks = [pltpu.with_memory_space_constraint(chunk, pltpu.VMEM) for chunk in chunks]
        column = firsts[piece]
        own, away = project(jnp.asarray(table), a_blocks, chunks, tuple(fixed), gates, column, total)
        return [own, swap(away, ("groups",))], column

    results = []
    for slot in range(FLIGHT + PARTS, len(hops)):
        if slot == first_done + FLIGHT:
            results.append(project_piece(0))
            waits.setdefault(slot, []).append(results[0][0][0])
        hop(slot, *waits.get(slot, []))
    for piece in range(len(results), len(widths)):
        results.append(project_piece(piece, *(results[-1][0][1:] if results else [])))
    out = None
    for blocks, column in results:
        out = place(blocks, out, column, total, model_width)
    return out.reshape((1, frames_here, spots, model_width))


def solution(mesh):
    placed = (
        P(("groups", "owner"), "slab", None, None),
        P(None, ("groups", "owner"), "slab", None, None),
        P("groups"),
        P("groups", None),
        P("groups", None),
        P("owner", None),
    )
    return jax.shard_map(
        on_device,
        mesh=mesh,
        in_specs=placed,
        out_specs=P(("groups", "owner"), "slab", None, None),
        check_vma=False,
    )
```

```python
import functools
import math

import jax
import jax.numpy as jnp
import numpy as np
from jax import lax
from jax.experimental import pallas as pl
from jax.experimental.pallas import tpu as pltpu
from jax.sharding import PartitionSpec as P

HEAD_DIM = 128
WB = 14
HALO = 1
LANES = 128
NEG_LARGE = -1e30
PARTS = 2
FLIGHT = 2
MIB = 1024 * 1024
ANYWHERE = pl.BlockSpec(memory_space=pl.ANY)
IN_HBM = pl.BlockSpec(memory_space=pltpu.HBM)
IN_VMEM = pl.BlockSpec(memory_space=pltpu.VMEM)
IN_SMEM = pl.BlockSpec(memory_space=pltpu.SMEM)


def ring_order(count):
    width = max(w for w in range(1, count + 1) if count % w == 0 and w * w <= count)
    height = count // width
    if width == 1 or height % 2:
        return list(range(count))
    order = []
    for row in range(height):
        columns = range(1, width) if row % 2 == 0 else range(width - 1, 0, -1)
        order += [row * width + column for column in columns]
    return order + [row * width for row in range(height - 1, -1, -1)]


def piece_widths(half_width):
    tiles = half_width // (2 * LANES)
    late = 2 * tiles // 5
    return [count * LANES for count in (tiles - late, late) if count]


def swap(value, axes):
    count = math.prod(lax.axis_size(axis) for axis in axes)
    return lax.ppermute(value, axes, [(i, count - 1 - i) for i in range(count)])


def after(value, *others):
    return lax.optimization_barrier((value,) + others)[0]


def run_copies(copies):
    for copy in copies:
        copy.start()
    for copy in copies:
        copy.wait()


def through(sources, buffers, targets, arrived, left):
    first = [pltpu.make_async_copy(s, b, arrived.at[i]) for i, (s, b) in enumerate(zip(sources, buffers))]
    second = [pltpu.make_async_copy(b, t, left.at[i]) for i, (b, t) in enumerate(zip(buffers, targets))]
    for copy in first:
        copy.start()
    for before, copy in zip(first, second):
        before.wait()
        copy.start()
    for copy in second:
        copy.wait()


def cut_kernel(first, total, weight_ref, *refs):
    count = len(refs) // 2 - 1
    out_refs, buffers, (arrived, left) = refs[:count], refs[count : 2 * count], refs[2 * count :]
    column = lax.axis_index("groups") * total + first
    sources = []
    for ref in out_refs:
        sources.append(weight_ref.at[:, pl.ds(pl.multiple_of(column, LANES), ref.shape[1])])
        column += ref.shape[1]
    through(sources, buffers, out_refs, arrived, left)


def cut(out_weight, strips, first, total):
    depth = out_weight.shape[0]
    out_weight = pltpu.with_memory_space_constraint(out_weight, pltpu.HBM)
    return pl.pallas_call(
        functools.partial(cut_kernel, first, total),
        out_shape=[jax.ShapeDtypeStruct((depth, width), jnp.bfloat16) for width in strips],
        in_specs=[IN_HBM],
        out_specs=[IN_HBM] * len(strips),
        scratch_shapes=[pltpu.VMEM((depth, width), jnp.bfloat16) for width in strips]
        + [pltpu.SemaphoreType.DMA((len(strips),))] * 2,
        compiler_params=pltpu.CompilerParams(vmem_limit_bytes=4 * MIB),
        cost_estimate=pl.CostEstimate(flops=0, bytes_accessed=4 * depth * sum(strips), transcendentals=0),
        name="cut",
    )(out_weight)


def scale_kernel(keep_ref, gate_ref, out_ref):
    owner = lax.axis_index("owner")
    factor = jnp.where(owner % 2 == 1, keep_ref[owner // 2], 1).astype(jnp.float32)
    out_ref[...] = gate_ref[pl.ds(owner // 2, 1), :] * factor


def scale_gate(keep, gate):
    return pl.pallas_call(
        scale_kernel,
        out_shape=jax.ShapeDtypeStruct((1, gate.shape[1]), jnp.float32),
        in_specs=[IN_SMEM, IN_VMEM],
        out_specs=IN_VMEM,
        name="scale_gate",
    )(keep, gate)


def token_place(count, dim, spots, first_frame):
    shape = (count, 1) if dim == 0 else (1, count)
    token = lax.broadcasted_iota(jnp.int32, shape, dim).astype(jnp.float32)
    frame = jnp.floor((token + 0.5) * (1.0 / spots))
    spot = token - frame * spots
    row = jnp.floor((spot + 0.5) * (1.0 / WB))
    return frame + first_frame, row, spot - row * WB


def attend_kernel(spots, windows_ref, q_ref, k_ref, v_ref, k_other_ref, v_other_ref, out_ref, bias):
    rows = q_ref.shape[0]
    halo_rows = HALO * spots
    first_row = jnp.where(lax.axis_index("slab") == 0, 0, rows - halo_rows)
    halo = pl.ds(pl.multiple_of(first_row, 16 if spots % 16 == 0 else 8), halo_rows)
    keys = bias.shape[1]
    frames_here = rows // spots

    @pl.when(pl.program_id(0) == 0)
    def _():
        request = lax.axis_index("owner") // 2
        halo_frame = jnp.where(lax.axis_index("slab") == 0, 0, -HALO - frames_here).astype(jnp.float32)
        query = token_place(rows, 0, spots, 0.0)
        key = token_place(keys, 1, spots, 0.0)
        index = lax.broadcasted_iota(jnp.int32, (1, keys), 1)
        frame = jnp.where(index < rows, key[0], key[0] + halo_frame)
        frame = jnp.where(index < rows + halo_rows, frame, -NEG_LARGE)
        allowed = None
        for part, place in enumerate((frame, key[1], key[2])):
            near = jnp.abs(query[part] - place) <= windows_ref[request, part].astype(jnp.float32)
            allowed = near if allowed is None else allowed & near
        bias[...] = jnp.where(allowed, 0.0, NEG_LARGE)

    scale = math.log2(math.e) / math.sqrt(HEAD_DIM)
    pad = jnp.zeros((keys - rows - halo_rows, HEAD_DIM), jnp.bfloat16)
    ones = jnp.ones((keys, HEAD_DIM), jnp.bfloat16)
    for head in range(q_ref.shape[1] // HEAD_DIM):
        at = slice(head * HEAD_DIM, (head + 1) * HEAD_DIM)
        key = jnp.concatenate([k_ref[:, at], k_other_ref[halo, at], pad], axis=0)
        value = jnp.concatenate([v_ref[:, at], v_other_ref[halo, at], pad], axis=0)
        value = jnp.concatenate([value, ones], axis=1)
        score = lax.dot_general(q_ref[:, at], key, (((1,), (1,)), ((), ())), preferred_element_type=jnp.float32)
        score = score * scale + bias[...]
        weight = jnp.exp2(score - jnp.max(score, axis=1, keepdims=True)).astype(jnp.bfloat16)
        mixture = jnp.dot(weight, value, preferred_element_type=jnp.float32)
        out_ref[:, at] = (mixture[:, :HEAD_DIM] / mixture[:, HEAD_DIM:]).astype(jnp.bfloat16)


def attend(query_rows, key_value_rows, other_rows, windows, spots, part):
    rows, features = query_rows.shape
    query_rows = pltpu.with_memory_space_constraint(query_rows, pltpu.HBM)
    width = features // PARTS
    heads = width // HEAD_DIM
    steps = 2 if heads % 2 == 0 else 1
    block = width // steps
    halo_rows = HALO * spots
    first = part * steps
    keys = pl.cdiv(rows + halo_rows, LANES) * LANES
    return pl.pallas_call(
        functools.partial(attend_kernel, spots),
        grid=(steps,),
        out_shape=jax.ShapeDtypeStruct((rows, width), jnp.bfloat16),
        in_specs=[
            IN_SMEM,
            pl.BlockSpec((rows, block), lambda i: (0, first + i)),
            pl.BlockSpec((None, rows, block), lambda i: (0, 0, first + i)),
            pl.BlockSpec((None, rows, block), lambda i: (1, 0, first + i)),
            pl.BlockSpec((None, rows, block), lambda i: (0, 0, first + i)),
            pl.BlockSpec((None, rows, block), lambda i: (1, 0, first + i)),
        ],
        out_specs=pl.BlockSpec((rows, block), lambda i: (0, i)),
        scratch_shapes=[pltpu.VMEM((rows, keys), jnp.float32)],
        compiler_params=pltpu.CompilerParams(vmem_limit_bytes=10 * MIB),
        cost_estimate=pl.CostEstimate(
            flops=32 * rows * keys * width, bytes_accessed=2 * width * (2 * rows + 2 * keys), transcendentals=heads * rows * keys
        ),
        name="attend",
    )(windows, query_rows, key_value_rows, key_value_rows, other_rows, other_rows)


def project_kernel(strip, column, total, fixed, tables_ref, *refs):
    a_refs, refs = refs[: 2 * PARTS], refs[2 * PARTS :]
    w_refs, refs = refs[: len(fixed)], refs[len(fixed) :]
    gate_refs, out_refs, (rows_all, weight, arrived) = refs[:2], refs[2:4], refs[4:]
    owner, slab = lax.axis_index("owner"), lax.axis_index("slab")
    rows, part_width = a_refs[0].shape
    row_copies = []
    for index, a_ref in enumerate(a_refs):
        block, part = divmod(index, PARTS)
        target = rows_all.at[block * rows : (block + 1) * rows, part * part_width : (part + 1) * part_width]
        row_copies.append(pltpu.make_async_copy(a_ref, target, arrived.at[len(fixed) + index]))
        row_copies[-1].start()
    for where in range(2):
        for index, (place, holder) in enumerate(fixed):
            if place != where:
                continue
            at = slice(where * strip, (where + 1) * strip)
            target = weight.at[tables_ref[slab, owner, index], :, at]
            copy = pltpu.make_async_copy(w_refs[index], target, arrived.at[index])
            if holder is None:
                copy.start()
            else:
                pl.when(slab == holder)(copy.start)
    for copy in row_copies:
        copy.wait()
    tile = 2 * LANES if strip % (2 * LANES) == 0 else LANES
    for where in range(2):
        for index, (place, holder) in enumerate(fixed):
            if place != where:
                continue
            copy = pltpu.make_async_copy(w_refs[index], weight.at[0, :, :strip], arrived.at[index])
            if holder is None:
                copy.wait()
            else:
                pl.when(slab == holder)(copy.wait)
        for first in range(where * strip, (where + 1) * strip, tile):
            columns = weight[:, :, first : first + tile].reshape(-1, tile)
            product = jnp.dot(rows_all[...], columns, preferred_element_type=jnp.float32)
            here = pl.ds(pl.multiple_of(lax.axis_index("groups") * total + column + first, LANES), tile)
            for block in range(2):
                gate = gate_refs[block][:, here]
                result = product[block * rows : (block + 1) * rows] * gate
                out_refs[block][:, first : first + tile] = result.astype(jnp.bfloat16)


def project(table, a_blocks, chunks, fixed, gates, column, total):
    slabs, count, held = table.shape
    rows, part_width = a_blocks[0].shape
    depth, strip = chunks[0].shape
    width = 2 * strip
    return pl.pallas_call(
        functools.partial(project_kernel, strip, column, total, fixed),
        out_shape=[jax.ShapeDtypeStruct((rows, width), jnp.bfloat16)] * 2,
        in_specs=[IN_SMEM] + [ANYWHERE] * (len(a_blocks) + held) + [IN_VMEM] * 2,
        out_specs=[IN_VMEM] * 2,
        scratch_shapes=[
            pltpu.VMEM((2 * rows, PARTS * part_width), jnp.bfloat16),
            pltpu.VMEM((count, depth, width), jnp.bfloat16),
            pltpu.SemaphoreType.DMA((held + len(a_blocks),)),
        ],
        compiler_params=pltpu.CompilerParams(vmem_limit_bytes=16 * MIB),
        cost_estimate=pl.CostEstimate(
            flops=4 * rows * width * depth * count,
            bytes_accessed=2 * (2 * rows * (depth * count + width) + count * depth * width),
            transcendentals=0,
        ),
        name="project",
    )(table, *a_blocks, *chunks, *gates)


def place_kernel(column, total, *refs):
    in_refs, (out_ref, done) = refs[:2], refs[-2:]
    width = in_refs[0].shape[1]
    group = lax.axis_index("groups")
    copies = []
    for block, in_ref in enumerate(in_refs):
        start = (1 - group if block else group) * total + column
        at = pl.ds(pl.multiple_of(start, LANES), width)
        copies.append(pltpu.make_async_copy(in_ref, out_ref.at[:, at], done.at[block]))
    run_copies(copies)


def place(blocks, out, column, total, model_width):
    rows, width = blocks[0].shape
    held = [] if out is None else [out]
    return pl.pallas_call(
        functools.partial(place_kernel, column, total),
        out_shape=jax.ShapeDtypeStruct((rows, model_width), jnp.bfloat16),
        in_specs=[IN_VMEM] * len(blocks) + [ANYWHERE] * len(held),
        out_specs=ANYWHERE,
        scratch_shapes=[pltpu.SemaphoreType.DMA((len(blocks),))],
        input_output_aliases={len(blocks): 0} if held else {},
        compiler_params=pltpu.CompilerParams(vmem_limit_bytes=4 * MIB),
        cost_estimate=pl.CostEstimate(flops=0, bytes_accessed=4 * rows * width * len(blocks), transcendentals=0),
        name="place",
    )(*blocks, *held)


def hop_order(pieces, turns, opposite):
    order = []
    for piece in range(pieces):
        order += [(piece, strip, turn) for turn in range(1, turns + 1) for strip in range(2)]
        order += [(piece, None, turns + 1)] if opposite else []
    return order


def on_device(queries, key_value, keep, windows, gate, out_weight):
    frames_here, spots, features = queries.shape[1:]
    model_width = gate.shape[1]
    rows = frames_here * spots
    slab_index = lax.axis_index("slab")
    slabs = lax.axis_size("slab")
    total = model_width // lax.axis_size("groups")
    widths = piece_widths(total)

    count = lax.axis_size("owner")
    order = ring_order(count)
    spot_of = [order.index(owner) for owner in range(count)]
    ring = [
        (owner * slabs + slab, order[(spot_of[owner] + step) % count] * slabs + slab)
        for owner in range(count)
        for slab, step in enumerate((1, -1))
    ]
    turns, opposite = (count - 1) // 2, count % 2 == 0
    hops = hop_order(len(widths), turns, opposite)

    firsts = [2 * sum(widths[:piece]) for piece in range(len(widths))]
    held, arrived, crossed = {}, [], {}
    for piece, width in enumerate(widths):
        for strip, own in enumerate(cut(out_weight, [width] * 2, firsts[piece], total)):
            held[piece, strip, 0] = own
    def hop(slot, *others):
        if slot >= len(hops):
            return
        piece, strip, turn = hops[slot]
        waits = list(others)
        if slot >= FLIGHT:
            waits.append(arrived[slot - FLIGHT])
        if slot >= 2 * FLIGHT + 1:
            waits.append(crossed[hops[slot - 2 * FLIGHT - 1]])
        if strip is None:
            value = jnp.where(slab_index == 0, held[piece, 0, turn - 1], held[piece, 1, turn - 1])
        else:
            value = held[piece, strip, turn - 1]
        if waits:
            value = after(value, *waits)
        value = lax.ppermute(value, ("owner", "slab"), ring)
        held[hops[slot]] = value
        arrived.append(value)

    def cross(slot, *others):
        value = arrived[slot]
        crossed[hops[slot]] = swap(after(value, *others) if others else value, ("slab",))

    first_done = max(slot for slot, at in enumerate(hops) if at[0] == 0) if hops else 0
    other = swap(key_value, ("slab",))
    for slot in range(FLIGHT):
        hop(slot)

    query_rows = queries.reshape(rows, features)
    key_value_rows = key_value.reshape(2, rows, features)
    other_rows = other.reshape(2, rows, features)
    near, far = [], []
    waits = {FLIGHT + PARTS: [held[piece, 0, 0] for piece in range(1, len(widths))]}
    for part in range(PARTS):
        attended = attend(query_rows, key_value_rows, other_rows, windows, spots, part)
        across = swap(attended, ("groups",))
        near.append(attended)
        far.append(across)
        waits.setdefault(max(first_done + 1 - 2 * (PARTS - 1 - part), FLIGHT + PARTS), []).append(across)
    for part in range(PARTS):
        hop(FLIGHT + part, *(near if part else []))
    for slot in range(min(FLIGHT + PARTS, len(hops))):
        cross(slot, near[-1])
    near_gate = scale_gate(after(keep, near[-1]), gate)
    gates = (near_gate, swap(near_gate, ("groups",)))

    def project_piece(piece, *others):
        chunks = [held[piece, 0, 0], held[piece, 1, 0]]
        fixed = [(0, None), (1, None)]
        sources = [(0, 0), (0, 0)]
        for turn in range(1, turns + 1):
            for strip in range(2):
                chunks += [held[piece, strip, turn], crossed[piece, strip, turn]]
                fixed += [(strip, None)] * 2
                sources += [(-turn, turn), (turn, -turn)]
        if opposite:
            chunks += [held[piece, None, turns + 1], crossed[piece, None, turns + 1]] * 2
            fixed += [(strip, strip ^ mate) for strip in range(2) for mate in range(2)]
            sources += [(turns + 1, turns + 1)] * 4
        table = np.zeros((slabs, count, len(chunks)), np.int32)
        for slab in range(slabs):
            for owner in range(count):
                table[slab, owner] = [order[(spot_of[owner] + source[slab]) % count] for source in sources]
        if others:
            chunks[0] = after(chunks[0], *others)
        column = firsts[piece]
        own, away = project(jnp.asarray(table), near + far, chunks, tuple(fixed), gates, column, total)
        return [own, swap(away, ("groups",))], column

    results = []
    for slot in range(FLIGHT + PARTS, len(hops)):
        if slot == first_done + 4:
            results.append(project_piece(0))
            waits.setdefault(slot, []).append(results[0][0][0])
        hop(slot, *waits.get(slot, []))
        if slot - 1 >= FLIGHT + PARTS:
            cross(slot - 1, *([arrived[slot]] if slot == first_done + 1 else []))
    if len(hops) > FLIGHT + PARTS:
        cross(len(hops) - 1)
    for piece in range(len(results), len(widths)):
        results.append(project_piece(piece, *(results[-1][0][1:] if results else [])))
    out = None
    for blocks, column in results:
        out = place(blocks, out, column, total, model_width)
    return out.reshape((1, frames_here, spots, model_width))


def solution(mesh):
    placed = (
        P(("groups", "owner"), "slab", None, None),
        P(None, ("groups", "owner"), "slab", None, None),
        P("groups"),
        P("groups", None),
        P("groups", None),
        P("owner", None),
    )
    return jax.shard_map(
        on_device,
        mesh=mesh,
        in_specs=placed,
        out_specs=P(("groups", "owner"), "slab", None, None),
        check_vma=False,
    )
```

```python
import functools
import math

import jax
import jax.numpy as jnp
import numpy as np
from jax import lax
from jax.experimental import pallas as pl
from jax.experimental.pallas import tpu as pltpu
from jax.sharding import PartitionSpec as P

HEAD_DIM = 128
WB = 14
HALO = 1
LANES = 128
NEG_LARGE = -1e30
PARTS = 2
FLIGHT = 2
MIB = 1024 * 1024
ANYWHERE = pl.BlockSpec(memory_space=pl.ANY)
IN_HBM = pl.BlockSpec(memory_space=pltpu.HBM)
IN_VMEM = pl.BlockSpec(memory_space=pltpu.VMEM)
IN_SMEM = pl.BlockSpec(memory_space=pltpu.SMEM)


def ring_order(count):
    width = max(w for w in range(1, count + 1) if count % w == 0 and w * w <= count)
    height = count // width
    if width == 1 or height % 2:
        return list(range(count))
    order = []
    for row in range(height):
        columns = range(1, width) if row % 2 == 0 else range(width - 1, 0, -1)
        order += [row * width + column for column in columns]
    return order + [row * width for row in range(height - 1, -1, -1)]


def piece_widths(half_width):
    tiles = half_width // (2 * LANES)
    late = 2 * tiles // 5
    return [count * LANES for count in (tiles - late, late) if count]


def swap(value, axes):
    count = math.prod(lax.axis_size(axis) for axis in axes)
    return lax.ppermute(value, axes, [(i, count - 1 - i) for i in range(count)])


def after(value, *others):
    return lax.optimization_barrier((value,) + others)[0]


def run_copies(copies):
    for copy in copies:
        copy.start()
    for copy in copies:
        copy.wait()


def through(sources, buffers, targets, arrived, left):
    first = [pltpu.make_async_copy(s, b, arrived.at[i]) for i, (s, b) in enumerate(zip(sources, buffers))]
    second = [pltpu.make_async_copy(b, t, left.at[i]) for i, (b, t) in enumerate(zip(buffers, targets))]
    for copy in first:
        copy.start()
    for before, copy in zip(first, second):
        before.wait()
        copy.start()
    for copy in second:
        copy.wait()


def cut_kernel(first, total, weight_ref, *refs):
    count = len(refs) // 2 - 1
    out_refs, buffers, (arrived, left) = refs[:count], refs[count : 2 * count], refs[2 * count :]
    column = lax.axis_index("groups") * total + first
    sources = []
    for ref in out_refs:
        sources.append(weight_ref.at[:, pl.ds(pl.multiple_of(column, LANES), ref.shape[1])])
        column += ref.shape[1]
    through(sources, buffers, out_refs, arrived, left)


def cut(out_weight, strips, first, total):
    depth = out_weight.shape[0]
    out_weight = pltpu.with_memory_space_constraint(out_weight, pltpu.HBM)
    return pl.pallas_call(
        functools.partial(cut_kernel, first, total),
        out_shape=[jax.ShapeDtypeStruct((depth, width), jnp.bfloat16) for width in strips],
        in_specs=[IN_HBM],
        out_specs=[IN_HBM] * len(strips),
        scratch_shapes=[pltpu.VMEM((depth, width), jnp.bfloat16) for width in strips]
        + [pltpu.SemaphoreType.DMA((len(strips),))] * 2,
        compiler_params=pltpu.CompilerParams(vmem_limit_bytes=4 * MIB),
        cost_estimate=pl.CostEstimate(flops=0, bytes_accessed=4 * depth * sum(strips), transcendentals=0),
        name="cut",
    )(out_weight)


def scale_kernel(keep_ref, gate_ref, out_ref):
    owner = lax.axis_index("owner")
    factor = jnp.where(owner % 2 == 1, keep_ref[owner // 2], 1).astype(jnp.float32)
    out_ref[...] = gate_ref[pl.ds(owner // 2, 1), :] * factor


def scale_gate(keep, gate):
    return pl.pallas_call(
        scale_kernel,
        out_shape=jax.ShapeDtypeStruct((1, gate.shape[1]), jnp.float32),
        in_specs=[IN_SMEM, IN_VMEM],
        out_specs=IN_VMEM,
        compiler_params=pltpu.CompilerParams(vmem_limit_bytes=MIB),
        name="scale_gate",
    )(keep, gate)


def token_place(count, dim, spots, first_frame):
    shape = (count, 1) if dim == 0 else (1, count)
    token = lax.broadcasted_iota(jnp.int32, shape, dim).astype(jnp.float32)
    frame = jnp.floor((token + 0.5) * (1.0 / spots))
    spot = token - frame * spots
    row = jnp.floor((spot + 0.5) * (1.0 / WB))
    return frame + first_frame, row, spot - row * WB


def attend_kernel(spots, windows_ref, q_ref, k_ref, v_ref, k_other_ref, v_other_ref, out_ref, bias):
    rows = q_ref.shape[0]
    halo_rows = HALO * spots
    first_row = jnp.where(lax.axis_index("slab") == 0, 0, rows - halo_rows)
    halo = pl.ds(pl.multiple_of(first_row, 16 if spots % 16 == 0 else 8), halo_rows)
    keys = bias.shape[1]
    frames_here = rows // spots

    @pl.when(pl.program_id(0) == 0)
    def _():
        request = lax.axis_index("owner") // 2
        halo_frame = jnp.where(lax.axis_index("slab") == 0, 0, -HALO - frames_here).astype(jnp.float32)
        query = token_place(rows, 0, spots, 0.0)
        key = token_place(keys, 1, spots, 0.0)
        index = lax.broadcasted_iota(jnp.int32, (1, keys), 1)
        frame = jnp.where(index < rows, key[0], key[0] + halo_frame)
        frame = jnp.where(index < rows + halo_rows, frame, -NEG_LARGE)
        allowed = None
        for part, place in enumerate((frame, key[1], key[2])):
            near = jnp.abs(query[part] - place) <= windows_ref[request, part].astype(jnp.float32)
            allowed = near if allowed is None else allowed & near
        bias[...] = jnp.where(allowed, 0.0, NEG_LARGE)

    scale = math.log2(math.e) / math.sqrt(HEAD_DIM)
    pad = jnp.zeros((keys - rows - halo_rows, HEAD_DIM), jnp.bfloat16)
    ones = jnp.ones((keys, HEAD_DIM), jnp.bfloat16)
    for head in range(q_ref.shape[1] // HEAD_DIM):
        at = slice(head * HEAD_DIM, (head + 1) * HEAD_DIM)
        key = jnp.concatenate([k_ref[:, at], k_other_ref[halo, at], pad], axis=0)
        value = jnp.concatenate([v_ref[:, at], v_other_ref[halo, at], pad], axis=0)
        value = jnp.concatenate([value, ones], axis=1)
        score = lax.dot_general(q_ref[:, at], key, (((1,), (1,)), ((), ())), preferred_element_type=jnp.float32)
        score = score * scale + bias[...]
        weight = jnp.exp2(score - jnp.max(score, axis=1, keepdims=True)).astype(jnp.bfloat16)
        mixture = jnp.dot(weight, value, preferred_element_type=jnp.float32)
        out_ref[:, at] = (mixture[:, :HEAD_DIM] / mixture[:, HEAD_DIM:]).astype(jnp.bfloat16)


def attend(query_rows, key_value_rows, other_rows, windows, spots, part):
    rows, features = query_rows.shape
    query_rows = pltpu.with_memory_space_constraint(query_rows, pltpu.HBM)
    width = features // PARTS
    heads = width // HEAD_DIM
    steps = 2 if heads % 2 == 0 else 1
    block = width // steps
    halo_rows = HALO * spots
    first = part * steps
    keys = pl.cdiv(rows + halo_rows, LANES) * LANES
    return pl.pallas_call(
        functools.partial(attend_kernel, spots),
        grid=(steps,),
        out_shape=jax.ShapeDtypeStruct((rows, width), jnp.bfloat16),
        in_specs=[
            IN_SMEM,
            pl.BlockSpec((rows, block), lambda i: (0, first + i)),
            pl.BlockSpec((None, rows, block), lambda i: (0, 0, first + i)),
            pl.BlockSpec((None, rows, block), lambda i: (1, 0, first + i)),
            pl.BlockSpec((None, rows, block), lambda i: (0, 0, first + i)),
            pl.BlockSpec((None, rows, block), lambda i: (1, 0, first + i)),
        ],
        out_specs=pl.BlockSpec((rows, block), lambda i: (0, i)),
        scratch_shapes=[pltpu.VMEM((rows, keys), jnp.float32)],
        compiler_params=pltpu.CompilerParams(vmem_limit_bytes=10 * MIB),
        cost_estimate=pl.CostEstimate(
            flops=32 * rows * keys * width, bytes_accessed=2 * width * (2 * rows + 2 * keys), transcendentals=heads * rows * keys
        ),
        name="attend",
    )(windows, query_rows, key_value_rows, key_value_rows, other_rows, other_rows)


def project_kernel(strip, column, total, fixed, tables_ref, *refs):
    a_refs, refs = refs[: 2 * PARTS], refs[2 * PARTS :]
    w_refs, refs = refs[: len(fixed)], refs[len(fixed) :]
    gate_refs, out_refs, (rows_all, weight, arrived) = refs[:2], refs[2:4], refs[4:]
    owner, slab = lax.axis_index("owner"), lax.axis_index("slab")
    rows, part_width = a_refs[0].shape
    row_copies = []
    for index, a_ref in enumerate(a_refs):
        block, part = divmod(index, PARTS)
        target = rows_all.at[block * rows : (block + 1) * rows, part * part_width : (part + 1) * part_width]
        row_copies.append(pltpu.make_async_copy(a_ref, target, arrived.at[len(fixed) + index]))
        row_copies[-1].start()
    for where in range(2):
        for index, (place, holder) in enumerate(fixed):
            if place != where:
                continue
            at = slice(where * strip, (where + 1) * strip)
            target = weight.at[tables_ref[slab, owner, index], :, at]
            copy = pltpu.make_async_copy(w_refs[index], target, arrived.at[index])
            if holder is None:
                copy.start()
            else:
                pl.when(slab == holder)(copy.start)
    for copy in row_copies:
        copy.wait()
    tile = 2 * LANES if strip % (2 * LANES) == 0 else LANES
    for where in range(2):
        for index, (place, holder) in enumerate(fixed):
            if place != where:
                continue
            copy = pltpu.make_async_copy(w_refs[index], weight.at[0, :, :strip], arrived.at[index])
            if holder is None:
                copy.wait()
            else:
                pl.when(slab == holder)(copy.wait)
        for first in range(where * strip, (where + 1) * strip, tile):
            columns = weight[:, :, first : first + tile].reshape(-1, tile)
            product = jnp.dot(rows_all[...], columns, preferred_element_type=jnp.float32)
            here = pl.ds(pl.multiple_of(lax.axis_index("groups") * total + column + first, LANES), tile)
            for block in range(2):
                gate = gate_refs[block][:, here]
                result = product[block * rows : (block + 1) * rows] * gate
                out_refs[block][:, first : first + tile] = result.astype(jnp.bfloat16)


def project(table, a_blocks, chunks, fixed, gates, column, total):
    slabs, count, held = table.shape
    rows, part_width = a_blocks[0].shape
    depth, strip = chunks[0].shape
    width = 2 * strip
    return pl.pallas_call(
        functools.partial(project_kernel, strip, column, total, fixed),
        out_shape=[jax.ShapeDtypeStruct((rows, width), jnp.bfloat16)] * 2,
        in_specs=[IN_SMEM] + [ANYWHERE] * (len(a_blocks) + held) + [IN_VMEM] * 2,
        out_specs=[IN_VMEM] * 2,
        scratch_shapes=[
            pltpu.VMEM((2 * rows, PARTS * part_width), jnp.bfloat16),
            pltpu.VMEM((count, depth, width), jnp.bfloat16),
            pltpu.SemaphoreType.DMA((held + len(a_blocks),)),
        ],
        compiler_params=pltpu.CompilerParams(vmem_limit_bytes=16 * MIB),
        cost_estimate=pl.CostEstimate(
            flops=4 * rows * width * depth * count,
            bytes_accessed=2 * (2 * rows * (depth * count + width) + count * depth * width),
            transcendentals=0,
        ),
        name="project",
    )(table, *a_blocks, *chunks, *gates)


def place_kernel(column, total, *refs):
    in_refs, (out_ref, done) = refs[:2], refs[-2:]
    width = in_refs[0].shape[1]
    group = lax.axis_index("groups")
    copies = []
    for block, in_ref in enumerate(in_refs):
        start = (1 - group if block else group) * total + column
        at = pl.ds(pl.multiple_of(start, LANES), width)
        copies.append(pltpu.make_async_copy(in_ref, out_ref.at[:, at], done.at[block]))
    run_copies(copies)


def place(blocks, out, column, total, model_width):
    rows, width = blocks[0].shape
    held = [] if out is None else [out]
    return pl.pallas_call(
        functools.partial(place_kernel, column, total),
        out_shape=jax.ShapeDtypeStruct((rows, model_width), jnp.bfloat16),
        in_specs=[IN_VMEM] * len(blocks) + [ANYWHERE] * len(held),
        out_specs=ANYWHERE,
        scratch_shapes=[pltpu.SemaphoreType.DMA((len(blocks),))],
        input_output_aliases={len(blocks): 0} if held else {},
        compiler_params=pltpu.CompilerParams(vmem_limit_bytes=4 * MIB),
        cost_estimate=pl.CostEstimate(flops=0, bytes_accessed=4 * rows * width * len(blocks), transcendentals=0),
        name="place",
    )(*blocks, *held)


def hop_order(pieces, turns, opposite):
    order = []
    for piece in range(pieces):
        order += [(piece, strip, turn) for turn in range(1, turns + 1) for strip in range(2)]
        order += [(piece, None, turns + 1)] if opposite else []
    return order


def on_device(queries, key_value, keep, windows, gate, out_weight):
    frames_here, spots, features = queries.shape[1:]
    model_width = gate.shape[1]
    rows = frames_here * spots
    slab_index = lax.axis_index("slab")
    slabs = lax.axis_size("slab")
    total = model_width // lax.axis_size("groups")
    widths = piece_widths(total)

    count = lax.axis_size("owner")
    order = ring_order(count)
    spot_of = [order.index(owner) for owner in range(count)]
    ring = [
        (owner * slabs + slab, order[(spot_of[owner] + step) % count] * slabs + slab)
        for owner in range(count)
        for slab, step in enumerate((1, -1))
    ]
    turns, opposite = (count - 1) // 2, count % 2 == 0
    hops = hop_order(len(widths), turns, opposite)

    firsts = [2 * sum(widths[:piece]) for piece in range(len(widths))]
    held, arrived, crossed = {}, [], {}
    for piece, width in enumerate(widths):
        for strip, own in enumerate(cut(out_weight, [width] * 2, firsts[piece], total)):
            held[piece, strip, 0] = own
    def hop(slot, *others):
        if slot >= len(hops):
            return
        piece, strip, turn = hops[slot]
        waits = list(others)
        if slot >= FLIGHT:
            waits.append(arrived[slot - FLIGHT])
        if slot >= 2 * FLIGHT + 1:
            waits.append(crossed[hops[slot - 2 * FLIGHT - 1]])
        if strip is None:
            value = jnp.where(slab_index == 0, held[piece, 0, turn - 1], held[piece, 1, turn - 1])
        else:
            value = held[piece, strip, turn - 1]
        if waits:
            value = after(value, *waits)
        value = lax.ppermute(value, ("owner", "slab"), ring)
        held[hops[slot]] = value
        arrived.append(value)

    def cross(slot, *others):
        value = arrived[slot]
        crossed[hops[slot]] = swap(after(value, *others) if others else value, ("slab",))

    first_done = max(slot for slot, at in enumerate(hops) if at[0] == 0) if hops else 0
    other = swap(key_value, ("slab",))
    for slot in range(FLIGHT):
        hop(slot)

    query_rows = queries.reshape(rows, features)
    key_value_rows = key_value.reshape(2, rows, features)
    other_rows = other.reshape(2, rows, features)
    near, far = [], []
    waits = {FLIGHT + PARTS: [held[piece, 0, 0] for piece in range(1, len(widths))]}
    for part in range(PARTS):
        attended = attend(query_rows, key_value_rows, other_rows, windows, spots, part)
        across = swap(attended, ("groups",))
        near.append(attended)
        far.append(across)
        waits.setdefault(max(first_done - 2 * (PARTS - 1 - part), FLIGHT + PARTS), []).append(across)
    for part in range(PARTS):
        hop(FLIGHT + part)
    for slot in range(min(FLIGHT + PARTS, len(hops))):
        cross(slot, near[-1])
    near_gate = scale_gate(after(keep, near[-1]), gate)
    gates = (near_gate, swap(near_gate, ("groups",)))

    def project_piece(piece, *others):
        chunks = [held[piece, 0, 0], held[piece, 1, 0]]
        fixed = [(0, None), (1, None)]
        sources = [(0, 0), (0, 0)]
        for turn in range(1, turns + 1):
            for strip in range(2):
                chunks += [held[piece, strip, turn], crossed[piece, strip, turn]]
                fixed += [(strip, None)] * 2
                sources += [(-turn, turn), (turn, -turn)]
        if opposite:
            chunks += [held[piece, None, turns + 1], crossed[piece, None, turns + 1]] * 2
            fixed += [(strip, strip ^ mate) for strip in range(2) for mate in range(2)]
            sources += [(turns + 1, turns + 1)] * 4
        table = np.zeros((slabs, count, len(chunks)), np.int32)
        for slab in range(slabs):
            for owner in range(count):
                table[slab, owner] = [order[(spot_of[owner] + source[slab]) % count] for source in sources]
        if others:
            chunks[0] = after(chunks[0], *others)
        column = firsts[piece]
        own, away = project(jnp.asarray(table), near + far, chunks, tuple(fixed), gates, column, total)
        return [own, swap(away, ("groups",))], column

    results = []
    for slot in range(FLIGHT + PARTS, len(hops)):
        if slot == first_done + 5:
            results.append(project_piece(0))
            waits.setdefault(slot, []).append(results[0][0][0])
        hop(slot, *waits.get(slot, []))
        if slot - 1 >= FLIGHT + PARTS:
            cross(slot - 1, *([arrived[slot]] if slot == first_done + 1 else []))
    if len(hops) > FLIGHT + PARTS:
        cross(len(hops) - 1)
    for piece in range(len(results), len(widths)):
        results.append(project_piece(piece, *(results[-1][0][1:] if results else [])))
    out = None
    for blocks, column in results:
        out = place(blocks, out, column, total, model_width)
    return out.reshape((1, frames_here, spots, model_width))


def solution(mesh):
    placed = (
        P(("groups", "owner"), "slab", None, None),
        P(None, ("groups", "owner"), "slab", None, None),
        P("groups"),
        P("groups", None),
        P("groups", None),
        P("owner", None),
    )
    return jax.shard_map(
        on_device,
        mesh=mesh,
        in_specs=placed,
        out_specs=P(("groups", "owner"), "slab", None, None),
        check_vma=False,
    )
```

```python
import functools
import math

import jax
import jax.numpy as jnp
import numpy as np
from jax import lax
from jax.experimental import pallas as pl
from jax.experimental.pallas import tpu as pltpu
from jax.sharding import PartitionSpec as P

HEAD_DIM = 128
WB = 14
HALO = 1
LANES = 128
NEG_LARGE = -1e30
PARTS = 2
FLIGHT = 2
MIB = 1024 * 1024
ANYWHERE = pl.BlockSpec(memory_space=pl.ANY)
IN_HBM = pl.BlockSpec(memory_space=pltpu.HBM)
IN_VMEM = pl.BlockSpec(memory_space=pltpu.VMEM)
IN_SMEM = pl.BlockSpec(memory_space=pltpu.SMEM)


def ring_order(count):
    width = max(w for w in range(1, count + 1) if count % w == 0 and w * w <= count)
    height = count // width
    if width == 1 or height % 2:
        return list(range(count))
    order = []
    for row in range(height):
        columns = range(1, width) if row % 2 == 0 else range(width - 1, 0, -1)
        order += [row * width + column for column in columns]
    return order + [row * width for row in range(height - 1, -1, -1)]


def piece_widths(half_width):
    tiles = half_width // (2 * LANES)
    late = 2 * tiles // 5
    return [count * LANES for count in (tiles - late, late) if count]


def swap(value, axes):
    count = math.prod(lax.axis_size(axis) for axis in axes)
    return lax.ppermute(value, axes, [(i, count - 1 - i) for i in range(count)])


def after(value, *others):
    return lax.optimization_barrier((value,) + others)[0]


def run_copies(copies):
    for copy in copies:
        copy.start()
    for copy in copies:
        copy.wait()


def through(sources, buffers, targets, arrived, left):
    first = [pltpu.make_async_copy(s, b, arrived.at[i]) for i, (s, b) in enumerate(zip(sources, buffers))]
    second = [pltpu.make_async_copy(b, t, left.at[i]) for i, (b, t) in enumerate(zip(buffers, targets))]
    for copy in first:
        copy.start()
    for before, copy in zip(first, second):
        before.wait()
        copy.start()
    for copy in second:
        copy.wait()


def cut_kernel(first, total, with_border, weight_ref, key_value_ref, *refs):
    count = len(refs) // 2 - 1
    out_refs, buffers, (arrived, left) = refs[:count], refs[count : 2 * count], refs[2 * count :]
    column = lax.axis_index("groups") * total + first
    sources = []
    for ref in out_refs[: count - PARTS] if with_border else out_refs:
        sources.append(weight_ref.at[:, pl.ds(pl.multiple_of(column, LANES), ref.shape[1])])
        column += ref.shape[1]
    if with_border:
        frames_here = key_value_ref.shape[2]
        frame = jnp.where(lax.axis_index("slab") == 0, frames_here - HALO, 0)
        width = out_refs[-1].shape[3]
        for part in range(PARTS):
            sources.append(key_value_ref.at[:, 0, pl.ds(frame, HALO), :, part * width : (part + 1) * width])
    through(sources, buffers, out_refs, arrived, left)


def cut(out_weight, key_value, strips, first, total, with_border):
    depth = out_weight.shape[0]
    kinds, _, _, spots, features = key_value.shape
    shapes = [(depth, width) for width in strips]
    shapes += [(kinds, HALO, spots, features // PARTS)] * PARTS if with_border else []
    out_weight = pltpu.with_memory_space_constraint(out_weight, pltpu.HBM)
    key_value = pltpu.with_memory_space_constraint(key_value, pltpu.HBM)
    outs = pl.pallas_call(
        functools.partial(cut_kernel, first, total, with_border),
        out_shape=[jax.ShapeDtypeStruct(shape, jnp.bfloat16) for shape in shapes],
        in_specs=[IN_HBM] * 2,
        out_specs=[ANYWHERE] * len(shapes),
        scratch_shapes=[pltpu.VMEM(shape, jnp.bfloat16) for shape in shapes]
        + [pltpu.SemaphoreType.DMA((len(shapes),))] * 2,
        compiler_params=pltpu.CompilerParams(vmem_limit_bytes=4 * MIB),
        cost_estimate=pl.CostEstimate(flops=0, bytes_accessed=4 * depth * sum(strips), transcendentals=0),
        name="cut",
    )(out_weight, key_value)
    return outs[: len(strips)], [edge.reshape(kinds, HALO * spots, features // PARTS) for edge in outs[len(strips) :]]


def pick_kernel(one_ref, other_ref, out_ref, done):
    for slab, ref in enumerate((one_ref, other_ref)):

        @pl.when(lax.axis_index("slab") == slab)
        def _():
            copy = pltpu.make_async_copy(ref, out_ref, done)
            copy.start()
            copy.wait()


def pick(one, other):
    return pl.pallas_call(
        pick_kernel,
        out_shape=jax.ShapeDtypeStruct(one.shape, one.dtype),
        in_specs=[ANYWHERE] * 2,
        out_specs=ANYWHERE,
        scratch_shapes=[pltpu.SemaphoreType.DMA(())],
        compiler_params=pltpu.CompilerParams(vmem_limit_bytes=MIB),
        cost_estimate=pl.CostEstimate(flops=0, bytes_accessed=2 * one.size, transcendentals=0),
        name="pick",
    )(one, other)


def scale_kernel(keep_ref, gate_ref, out_ref):
    owner = lax.axis_index("owner")
    factor = jnp.where(owner % 2 == 1, keep_ref[owner // 2], 1).astype(jnp.float32)
    out_ref[...] = gate_ref[pl.ds(owner // 2, 1), :] * factor


def scale_gate(keep, gate):
    return pl.pallas_call(
        scale_kernel,
        out_shape=jax.ShapeDtypeStruct((1, gate.shape[1]), jnp.float32),
        in_specs=[IN_SMEM, IN_VMEM],
        out_specs=IN_VMEM,
        compiler_params=pltpu.CompilerParams(vmem_limit_bytes=MIB),
        name="scale_gate",
    )(keep, gate)


def token_place(count, dim, spots, first_frame):
    shape = (count, 1) if dim == 0 else (1, count)
    token = lax.broadcasted_iota(jnp.int32, shape, dim).astype(jnp.float32)
    frame = jnp.floor((token + 0.5) * (1.0 / spots))
    spot = token - frame * spots
    row = jnp.floor((spot + 0.5) * (1.0 / WB))
    return frame + first_frame, row, spot - row * WB


def attend_kernel(spots, windows_ref, q_ref, k_ref, v_ref, k_halo_ref, v_halo_ref, *refs):
    out_ref, bias = refs[-2:]
    rows = q_ref.shape[0]
    halo_rows = k_halo_ref.shape[0]
    keys = bias.shape[1]
    frames_here = rows // spots

    @pl.when(pl.program_id(0) == 0)
    def _():
        request = lax.axis_index("owner") // 2
        halo_frame = jnp.where(lax.axis_index("slab") == 0, 0, -HALO - frames_here).astype(jnp.float32)
        query = token_place(rows, 0, spots, 0.0)
        key = token_place(keys, 1, spots, 0.0)
        index = lax.broadcasted_iota(jnp.int32, (1, keys), 1)
        frame = jnp.where(index < rows, key[0], key[0] + halo_frame)
        frame = jnp.where(index < rows + halo_rows, frame, -NEG_LARGE)
        allowed = None
        for part, place in enumerate((frame, key[1], key[2])):
            near = jnp.abs(query[part] - place) <= windows_ref[request, part].astype(jnp.float32)
            allowed = near if allowed is None else allowed & near
        bias[...] = jnp.where(allowed, 0.0, NEG_LARGE)

    scale = math.log2(math.e) / math.sqrt(HEAD_DIM)
    pad = jnp.zeros((keys - rows - halo_rows, HEAD_DIM), jnp.bfloat16)
    ones = jnp.ones((keys, HEAD_DIM), jnp.bfloat16)
    for head in range(q_ref.shape[1] // HEAD_DIM):
        at = slice(head * HEAD_DIM, (head + 1) * HEAD_DIM)
        key = jnp.concatenate([k_ref[:, at], k_halo_ref[:, at], pad], axis=0)
        value = jnp.concatenate([v_ref[:, at], v_halo_ref[:, at], pad], axis=0)
        value = jnp.concatenate([value, ones], axis=1)
        score = lax.dot_general(q_ref[:, at], key, (((1,), (1,)), ((), ())), preferred_element_type=jnp.float32)
        score = score * scale + bias[...]
        weight = jnp.exp2(score - jnp.max(score, axis=1, keepdims=True)).astype(jnp.bfloat16)
        mixture = jnp.dot(weight, value, preferred_element_type=jnp.float32)
        out_ref[:, at] = (mixture[:, :HEAD_DIM] / mixture[:, HEAD_DIM:]).astype(jnp.bfloat16)


def attend(query_rows, key_value_rows, halo, windows, spots, part, attended):
    before = [] if attended is None else [attended]
    rows, features = query_rows.shape
    query_rows = pltpu.with_memory_space_constraint(query_rows, pltpu.HBM)
    width = features // PARTS
    heads = width // HEAD_DIM
    steps = 2 if heads % 2 == 0 else 1
    block = width // steps
    halo_rows = halo.shape[1]
    first = part * steps
    keys = pl.cdiv(rows + halo_rows, LANES) * LANES
    return pl.pallas_call(
        functools.partial(attend_kernel, spots),
        grid=(steps,),
        out_shape=jax.ShapeDtypeStruct((rows, features), jnp.bfloat16),
        in_specs=[
            IN_SMEM,
            pl.BlockSpec((rows, block), lambda i: (0, first + i)),
            pl.BlockSpec((None, rows, block), lambda i: (0, 0, first + i)),
            pl.BlockSpec((None, rows, block), lambda i: (1, 0, first + i)),
            pl.BlockSpec((None, halo_rows, block), lambda i: (0, 0, i)),
            pl.BlockSpec((None, halo_rows, block), lambda i: (1, 0, i)),
        ]
        + [ANYWHERE] * len(before),
        out_specs=pl.BlockSpec((rows, block), lambda i: (0, first + i)),
        input_output_aliases={6: 0} if before else {},
        scratch_shapes=[pltpu.VMEM((rows, keys), jnp.float32)],
        compiler_params=pltpu.CompilerParams(vmem_limit_bytes=10 * MIB),
        cost_estimate=pl.CostEstimate(
            flops=12 * rows * keys * width, bytes_accessed=2 * width * (2 * rows + 2 * keys), transcendentals=heads * rows * keys
        ),
        name="attend",
    )(windows, query_rows, key_value_rows, key_value_rows, halo, halo, *before)


def project_kernel(strip, column, total, fixed, tables_ref, *refs):
    a_refs, refs = refs[:2], refs[2:]
    w_refs, refs = refs[: len(fixed)], refs[len(fixed) :]
    gate_refs, out_refs, (rows_all, weight, arrived) = refs[:2], refs[2:4], refs[4:]
    owner, slab = lax.axis_index("owner"), lax.axis_index("slab")
    rows = a_refs[0].shape[0]
    row_copies = []
    for index, a_ref in enumerate(a_refs):
        target = rows_all.at[index * rows : (index + 1) * rows]
        row_copies.append(pltpu.make_async_copy(a_ref, target, arrived.at[len(fixed) + index]))
        row_copies[-1].start()
    for where in range(2):
        for index, (place, holder) in enumerate(fixed):
            if place != where:
                continue
            at = slice(where * strip, (where + 1) * strip)
            target = weight.at[tables_ref[slab, owner, index], :, at]
            copy = pltpu.make_async_copy(w_refs[index], target, arrived.at[index])
            if holder is None:
                copy.start()
            else:
                pl.when(slab == holder)(copy.start)
    for copy in row_copies:
        copy.wait()
    tile = 2 * LANES if strip % (2 * LANES) == 0 else LANES
    for where in range(2):
        for index, (place, holder) in enumerate(fixed):
            if place != where:
                continue
            copy = pltpu.make_async_copy(w_refs[index], weight.at[0, :, :strip], arrived.at[index])
            if holder is None:
                copy.wait()
            else:
                pl.when(slab == holder)(copy.wait)
        for first in range(where * strip, (where + 1) * strip, tile):
            columns = weight[:, :, first : first + tile].reshape(-1, tile)
            product = jnp.dot(rows_all[...], columns, preferred_element_type=jnp.float32)
            here = pl.ds(pl.multiple_of(lax.axis_index("groups") * total + column + first, LANES), tile)
            for block in range(2):
                gate = gate_refs[block][:, here]
                result = product[block * rows : (block + 1) * rows] * gate
                out_refs[block][:, first : first + tile] = result.astype(jnp.bfloat16)


def project(table, a_blocks, chunks, fixed, gates, column, total):
    slabs, count, held = table.shape
    rows, features = a_blocks[0].shape
    depth, strip = chunks[0].shape
    width = 2 * strip
    return pl.pallas_call(
        functools.partial(project_kernel, strip, column, total, fixed),
        out_shape=[jax.ShapeDtypeStruct((rows, width), jnp.bfloat16)] * 2,
        in_specs=[IN_SMEM] + [ANYWHERE] * (len(a_blocks) + held) + [IN_VMEM] * 2,
        out_specs=[IN_VMEM] * 2,
        scratch_shapes=[
            pltpu.VMEM((2 * rows, features), jnp.bfloat16),
            pltpu.VMEM((count, depth, width), jnp.bfloat16),
            pltpu.SemaphoreType.DMA((held + len(a_blocks),)),
        ],
        compiler_params=pltpu.CompilerParams(vmem_limit_bytes=16 * MIB),
        cost_estimate=pl.CostEstimate(
            flops=4 * rows * width * depth * count,
            bytes_accessed=2 * (2 * rows * (depth * count + width) + count * depth * width),
            transcendentals=0,
        ),
        name="project",
    )(table, *a_blocks, *chunks, *gates)


def place_kernel(column, total, *refs):
    in_refs, (out_ref, done) = refs[:2], refs[-2:]
    width = in_refs[0].shape[1]
    group = lax.axis_index("groups")
    copies = []
    for block, in_ref in enumerate(in_refs):
        start = (1 - group if block else group) * total + column
        at = pl.ds(pl.multiple_of(start, LANES), width)
        copies.append(pltpu.make_async_copy(in_ref, out_ref.at[:, at], done.at[block]))
    run_copies(copies)


def place(blocks, out, column, total, model_width):
    rows, width = blocks[0].shape
    held = [] if out is None else [out]
    return pl.pallas_call(
        functools.partial(place_kernel, column, total),
        out_shape=jax.ShapeDtypeStruct((rows, model_width), jnp.bfloat16),
        in_specs=[IN_VMEM] * len(blocks) + [ANYWHERE] * len(held),
        out_specs=ANYWHERE,
        scratch_shapes=[pltpu.SemaphoreType.DMA((len(blocks),))],
        input_output_aliases={len(blocks): 0} if held else {},
        compiler_params=pltpu.CompilerParams(vmem_limit_bytes=4 * MIB),
        cost_estimate=pl.CostEstimate(flops=0, bytes_accessed=4 * rows * width * len(blocks), transcendentals=0),
        name="place",
    )(*blocks, *held)


def hop_order(pieces, turns, opposite):
    order = []
    for piece in range(pieces):
        order += [(piece, strip, turn) for turn in range(1, turns + 1) for strip in range(2)]
        order += [(piece, None, turns + 1)] if opposite else []
    return order


def on_device(queries, key_value, keep, windows, gate, out_weight):
    frames_here, spots, features = queries.shape[1:]
    model_width = gate.shape[1]
    rows = frames_here * spots
    slabs = lax.axis_size("slab")
    total = model_width // lax.axis_size("groups")
    widths = piece_widths(total)

    count = lax.axis_size("owner")
    order = ring_order(count)
    spot_of = [order.index(owner) for owner in range(count)]
    ring = [
        (owner * slabs + slab, order[(spot_of[owner] + step) % count] * slabs + slab)
        for owner in range(count)
        for slab, step in enumerate((1, -1))
    ]
    turns, opposite = (count - 1) // 2, count % 2 == 0
    hops = hop_order(len(widths), turns, opposite)

    firsts = [2 * sum(widths[:piece]) for piece in range(len(widths))]
    held, arrived, crossed, edges = {}, [], {}, []
    for piece, width in enumerate(widths):
        own_strips, border = cut(out_weight, key_value, [width] * 2, firsts[piece], total, piece == 0)
        edges = border or edges
        for strip, own in enumerate(own_strips):
            held[piece, strip, 0] = own
    def hop(slot, *others):
        if slot >= len(hops):
            return
        piece, strip, turn = hops[slot]
        waits = list(others)
        if slot >= FLIGHT:
            waits.append(arrived[slot - FLIGHT])
        if slot > 2 * FLIGHT:
            waits.append(crossed[hops[slot - 2 * FLIGHT - 1]])
        if strip is None:
            value = pick(held[piece, 0, turn - 1], held[piece, 1, turn - 1])
        else:
            value = held[piece, strip, turn - 1]
        if waits:
            value = after(value, *waits)
        value = lax.ppermute(value, ("owner", "slab"), ring)
        held[hops[slot]] = value
        arrived.append(value)

    def cross(slot, *others):
        value = arrived[slot]
        crossed[hops[slot]] = swap(after(value, *others) if others else value, ("slab",))

    first_done = max(slot for slot, at in enumerate(hops) if at[0] == 0) if hops else 0
    halos = [swap(edge, ("slab",)) for edge in edges]
    for slot in range(FLIGHT):
        hop(slot)

    query_rows = queries.reshape(rows, features)
    key_value_rows = key_value.reshape(2, rows, features)
    waits, attended = {FLIGHT + 2: [held[piece, 0, 0] for piece in range(1, len(widths))]}, None
    for part in range(PARTS):
        attended = attend(query_rows, key_value_rows, halos[part], windows, spots, part, attended)
    a_blocks = (attended, swap(attended, ("groups",)))
    near_gate = scale_gate(after(keep, attended), gate)
    gates = (near_gate, swap(near_gate, ("groups",)))
    waits.setdefault(first_done, []).append(a_blocks[1])

    def project_piece(piece, *others):
        chunks = [held[piece, 0, 0], held[piece, 1, 0]]
        fixed = [(0, None), (1, None)]
        sources = [(0, 0), (0, 0)]
        for turn in range(1, turns + 1):
            for strip in range(2):
                chunks += [held[piece, strip, turn], crossed[piece, strip, turn]]
                fixed += [(strip, None)] * 2
                sources += [(-turn, turn), (turn, -turn)]
        if opposite:
            chunks += [held[piece, None, turns + 1], crossed[piece, None, turns + 1]] * 2
            fixed += [(strip, strip ^ mate) for strip in range(2) for mate in range(2)]
            sources += [(turns + 1, turns + 1)] * 4
        table = np.zeros((slabs, count, len(chunks)), np.int32)
        for slab in range(slabs):
            for owner in range(count):
                table[slab, owner] = [order[(spot_of[owner] + source[slab]) % count] for source in sources]
        if others:
            chunks[0] = after(chunks[0], *others)
        column = firsts[piece]
        own, away = project(jnp.asarray(table), a_blocks, chunks, tuple(fixed), gates, column, total)
        return [own, swap(away, ("groups",))], column

    results = []
    for slot in range(FLIGHT, len(hops)):
        if slot == first_done + 4:
            results.append(project_piece(0))
            waits.setdefault(slot, []).append(results[0][0][0])
        hop(slot, *waits.get(slot, []))
        cross(slot - FLIGHT, *([arrived[slot - FLIGHT + 1], gates[1]] if slot - FLIGHT == first_done else []))
    for slot in range(max(len(hops) - FLIGHT, 0), len(hops)):
        cross(slot)
    for piece in range(len(results), len(widths)):
        results.append(project_piece(piece, *(results[-1][0][1:] if results else [])))
    out = None
    for blocks, column in results:
        out = place(blocks, out, column, total, model_width)
    return out.reshape((1, frames_here, spots, model_width))


def solution(mesh):
    placed = (
        P(("groups", "owner"), "slab", None, None),
        P(None, ("groups", "owner"), "slab", None, None),
        P("groups"),
        P("groups", None),
        P("groups", None),
        P("owner", None),
    )
    return jax.shard_map(
        on_device,
        mesh=mesh,
        in_specs=placed,
        out_specs=P(("groups", "owner"), "slab", None, None),
        check_vma=False,
    )
```

```python
import functools
import math

import jax
import jax.numpy as jnp
import numpy as np
from jax import lax
from jax.experimental import pallas as pl
from jax.experimental.pallas import tpu as pltpu
from jax.sharding import PartitionSpec as P

HEAD_DIM = 128
WB = 14
HALO = 1
LANES = 128
NEG_LARGE = -1e30
PARTS = 2
FLIGHT = 2
MIB = 1024 * 1024
ANYWHERE = pl.BlockSpec(memory_space=pl.ANY)
IN_HBM = pl.BlockSpec(memory_space=pltpu.HBM)
IN_VMEM = pl.BlockSpec(memory_space=pltpu.VMEM)
IN_SMEM = pl.BlockSpec(memory_space=pltpu.SMEM)


def ring_order(count):
    width = max(w for w in range(1, count + 1) if count % w == 0 and w * w <= count)
    height = count // width
    if width == 1 or height % 2:
        return list(range(count))
    order = []
    for row in range(height):
        columns = range(1, width) if row % 2 == 0 else range(width - 1, 0, -1)
        order += [row * width + column for column in columns]
    return order + [row * width for row in range(height - 1, -1, -1)]


def piece_widths(half_width):
    tiles = half_width // (2 * LANES)
    late = 2 * tiles // 5
    return [count * LANES for count in (tiles - late, late) if count]


def swap(value, axes):
    count = math.prod(lax.axis_size(axis) for axis in axes)
    return lax.ppermute(value, axes, [(i, count - 1 - i) for i in range(count)])


def after(value, *others):
    return lax.optimization_barrier((value,) + others)[0]


def run_copies(copies):
    for copy in copies:
        copy.start()
    for copy in copies:
        copy.wait()


def through(sources, buffers, targets, arrived, left):
    first = [pltpu.make_async_copy(s, b, arrived.at[i]) for i, (s, b) in enumerate(zip(sources, buffers))]
    second = [pltpu.make_async_copy(b, t, left.at[i]) for i, (b, t) in enumerate(zip(buffers, targets))]
    for copy in first:
        copy.start()
    for before, copy in zip(first, second):
        before.wait()
        copy.start()
    for copy in second:
        copy.wait()


def cut_kernel(first, total, with_border, weight_ref, key_value_ref, *refs):
    count = len(refs) // 2 - 1
    out_refs, buffers, (arrived, left) = refs[:count], refs[count : 2 * count], refs[2 * count :]
    column = lax.axis_index("groups") * total + first
    sources = []
    for ref in out_refs[: count - PARTS] if with_border else out_refs:
        sources.append(weight_ref.at[:, pl.ds(pl.multiple_of(column, LANES), ref.shape[1])])
        column += ref.shape[1]
    if with_border:
        frames_here = key_value_ref.shape[2]
        frame = jnp.where(lax.axis_index("slab") == 0, frames_here - HALO, 0)
        width = out_refs[-1].shape[3]
        for part in range(PARTS):
            sources.append(key_value_ref.at[:, 0, pl.ds(frame, HALO), :, part * width : (part + 1) * width])
    through(sources, buffers, out_refs, arrived, left)


def cut(out_weight, key_value, strips, first, total, with_border):
    depth = out_weight.shape[0]
    kinds, _, _, spots, features = key_value.shape
    shapes = [(depth, width) for width in strips]
    shapes += [(kinds, HALO, spots, features // PARTS)] * PARTS if with_border else []
    out_weight = pltpu.with_memory_space_constraint(out_weight, pltpu.HBM)
    key_value = pltpu.with_memory_space_constraint(key_value, pltpu.HBM)
    outs = pl.pallas_call(
        functools.partial(cut_kernel, first, total, with_border),
        out_shape=[jax.ShapeDtypeStruct(shape, jnp.bfloat16) for shape in shapes],
        in_specs=[IN_HBM] * 2,
        out_specs=[ANYWHERE] * len(shapes),
        scratch_shapes=[pltpu.VMEM(shape, jnp.bfloat16) for shape in shapes]
        + [pltpu.SemaphoreType.DMA((len(shapes),))] * 2,
        compiler_params=pltpu.CompilerParams(vmem_limit_bytes=4 * MIB),
        cost_estimate=pl.CostEstimate(flops=0, bytes_accessed=4 * depth * sum(strips), transcendentals=0),
        name="cut",
    )(out_weight, key_value)
    return outs[: len(strips)], [edge.reshape(kinds, HALO * spots, features // PARTS) for edge in outs[len(strips) :]]


def pick_kernel(one_ref, other_ref, out_ref, done):
    for slab, ref in enumerate((one_ref, other_ref)):

        @pl.when(lax.axis_index("slab") == slab)
        def _():
            copy = pltpu.make_async_copy(ref, out_ref, done)
            copy.start()
            copy.wait()


def pick(one, other):
    return pl.pallas_call(
        pick_kernel,
        out_shape=jax.ShapeDtypeStruct(one.shape, one.dtype),
        in_specs=[ANYWHERE] * 2,
        out_specs=ANYWHERE,
        scratch_shapes=[pltpu.SemaphoreType.DMA(())],
        compiler_params=pltpu.CompilerParams(vmem_limit_bytes=MIB),
        cost_estimate=pl.CostEstimate(flops=0, bytes_accessed=2 * one.size, transcendentals=0),
        name="pick",
    )(one, other)


def scale_kernel(keep_ref, gate_ref, out_ref):
    owner = lax.axis_index("owner")
    factor = jnp.where(owner % 2 == 1, keep_ref[owner // 2], 1).astype(jnp.float32)
    out_ref[...] = gate_ref[pl.ds(owner // 2, 1), :] * factor


def scale_gate(keep, gate):
    return pl.pallas_call(
        scale_kernel,
        out_shape=jax.ShapeDtypeStruct((1, gate.shape[1]), jnp.float32),
        in_specs=[IN_SMEM, IN_VMEM],
        out_specs=IN_VMEM,
        compiler_params=pltpu.CompilerParams(vmem_limit_bytes=MIB),
        name="scale_gate",
    )(keep, gate)


def token_place(count, dim, spots, first_frame):
    shape = (count, 1) if dim == 0 else (1, count)
    token = lax.broadcasted_iota(jnp.int32, shape, dim).astype(jnp.float32)
    frame = jnp.floor((token + 0.5) * (1.0 / spots))
    spot = token - frame * spots
    row = jnp.floor((spot + 0.5) * (1.0 / WB))
    return frame + first_frame, row, spot - row * WB


def attend_kernel(spots, windows_ref, q_ref, k_ref, v_ref, k_halo_ref, v_halo_ref, *refs):
    out_ref, bias = refs[-2:]
    rows = q_ref.shape[0]
    halo_rows = k_halo_ref.shape[0]
    keys = bias.shape[1]
    frames_here = rows // spots

    @pl.when(pl.program_id(0) == 0)
    def _():
        request = lax.axis_index("owner") // 2
        halo_frame = jnp.where(lax.axis_index("slab") == 0, 0, -HALO - frames_here).astype(jnp.float32)
        query = token_place(rows, 0, spots, 0.0)
        key = token_place(keys, 1, spots, 0.0)
        index = lax.broadcasted_iota(jnp.int32, (1, keys), 1)
        frame = jnp.where(index < rows, key[0], key[0] + halo_frame)
        frame = jnp.where(index < rows + halo_rows, frame, -NEG_LARGE)
        allowed = None
        for part, place in enumerate((frame, key[1], key[2])):
            near = jnp.abs(query[part] - place) <= windows_ref[request, part].astype(jnp.float32)
            allowed = near if allowed is None else allowed & near
        bias[...] = jnp.where(allowed, 0.0, NEG_LARGE)

    scale = math.log2(math.e) / math.sqrt(HEAD_DIM)
    pad = jnp.zeros((keys - rows - halo_rows, HEAD_DIM), jnp.bfloat16)
    ones = jnp.ones((keys, HEAD_DIM), jnp.bfloat16)
    for head in range(q_ref.shape[1] // HEAD_DIM):
        at = slice(head * HEAD_DIM, (head + 1) * HEAD_DIM)
        key = jnp.concatenate([k_ref[:, at], k_halo_ref[:, at], pad], axis=0)
        value = jnp.concatenate([v_ref[:, at], v_halo_ref[:, at], pad], axis=0)
        value = jnp.concatenate([value, ones], axis=1)
        score = lax.dot_general(q_ref[:, at], key, (((1,), (1,)), ((), ())), preferred_element_type=jnp.float32)
        score = score * scale + bias[...]
        weight = jnp.exp2(score - jnp.max(score, axis=1, keepdims=True)).astype(jnp.bfloat16)
        mixture = jnp.dot(weight, value, preferred_element_type=jnp.float32)
        out_ref[:, at] = (mixture[:, :HEAD_DIM] / mixture[:, HEAD_DIM:]).astype(jnp.bfloat16)


def attend(query_rows, key_value_rows, halo, windows, spots, part, attended):
    before = [] if attended is None else [attended]
    rows, features = query_rows.shape
    query_rows = pltpu.with_memory_space_constraint(query_rows, pltpu.HBM)
    width = features // PARTS
    heads = width // HEAD_DIM
    steps = 2 if heads % 2 == 0 else 1
    block = width // steps
    halo_rows = halo.shape[1]
    first = part * steps
    keys = pl.cdiv(rows + halo_rows, LANES) * LANES
    return pl.pallas_call(
        functools.partial(attend_kernel, spots),
        grid=(steps,),
        out_shape=jax.ShapeDtypeStruct((rows, features), jnp.bfloat16),
        in_specs=[
            IN_SMEM,
            pl.BlockSpec((rows, block), lambda i: (0, first + i)),
            pl.BlockSpec((None, rows, block), lambda i: (0, 0, first + i)),
            pl.BlockSpec((None, rows, block), lambda i: (1, 0, first + i)),
            pl.BlockSpec((None, halo_rows, block), lambda i: (0, 0, i)),
            pl.BlockSpec((None, halo_rows, block), lambda i: (1, 0, i)),
        ]
        + [ANYWHERE] * len(before),
        out_specs=pl.BlockSpec((rows, block), lambda i: (0, first + i)),
        input_output_aliases={6: 0} if before else {},
        scratch_shapes=[pltpu.VMEM((rows, keys), jnp.float32)],
        compiler_params=pltpu.CompilerParams(vmem_limit_bytes=10 * MIB),
        cost_estimate=pl.CostEstimate(
            flops=12 * rows * keys * width, bytes_accessed=2 * width * (2 * rows + 2 * keys), transcendentals=heads * rows * keys
        ),
        name="attend",
    )(windows, query_rows, key_value_rows, key_value_rows, halo, halo, *before)


def project_kernel(strip, column, total, fixed, tables_ref, *refs):
    a_refs, refs = refs[:2], refs[2:]
    w_refs, refs = refs[: len(fixed)], refs[len(fixed) :]
    gate_refs, out_refs, (rows_all, weight, arrived) = refs[:2], refs[2:4], refs[4:]
    owner, slab = lax.axis_index("owner"), lax.axis_index("slab")
    rows = a_refs[0].shape[0]
    row_copies = []
    for index, a_ref in enumerate(a_refs):
        target = rows_all.at[index * rows : (index + 1) * rows]
        row_copies.append(pltpu.make_async_copy(a_ref, target, arrived.at[len(fixed) + index]))
        row_copies[-1].start()
    for where in range(2):
        for index, (place, holder) in enumerate(fixed):
            if place != where:
                continue
            at = slice(where * strip, (where + 1) * strip)
            target = weight.at[tables_ref[slab, owner, index], :, at]
            copy = pltpu.make_async_copy(w_refs[index], target, arrived.at[index])
            if holder is None:
                copy.start()
            else:
                pl.when(slab == holder)(copy.start)
    for copy in row_copies:
        copy.wait()
    tiles = [(first, min(2 * LANES, strip - first)) for first in range(0, strip, 2 * LANES)]
    for where in range(2):
        for index, (place, holder) in enumerate(fixed):
            if place != where:
                continue
            copy = pltpu.make_async_copy(w_refs[index], weight.at[0, :, :strip], arrived.at[index])
            if holder is None:
                copy.wait()
            else:
                pl.when(slab == holder)(copy.wait)
        for first, tile in tiles:
            first += where * strip
            columns = weight[:, :, first : first + tile].reshape(-1, tile)
            product = jnp.dot(rows_all[...], columns, preferred_element_type=jnp.float32)
            here = pl.ds(pl.multiple_of(lax.axis_index("groups") * total + column + first, LANES), tile)
            for block in range(2):
                gate = gate_refs[block][:, here]
                result = product[block * rows : (block + 1) * rows] * gate
                out_refs[block][:, first : first + tile] = result.astype(jnp.bfloat16)


def project(table, a_blocks, chunks, fixed, gates, column, total):
    slabs, count, held = table.shape
    rows, features = a_blocks[0].shape
    depth, strip = chunks[0].shape
    width = 2 * strip
    return pl.pallas_call(
        functools.partial(project_kernel, strip, column, total, fixed),
        out_shape=[jax.ShapeDtypeStruct((rows, width), jnp.bfloat16)] * 2,
        in_specs=[IN_SMEM] + [ANYWHERE] * (len(a_blocks) + held) + [IN_VMEM] * 2,
        out_specs=[IN_VMEM] * 2,
        scratch_shapes=[
            pltpu.VMEM((2 * rows, features), jnp.bfloat16),
            pltpu.VMEM((count, depth, width), jnp.bfloat16),
            pltpu.SemaphoreType.DMA((held + len(a_blocks),)),
        ],
        compiler_params=pltpu.CompilerParams(vmem_limit_bytes=16 * MIB),
        cost_estimate=pl.CostEstimate(
            flops=4 * rows * width * depth * count,
            bytes_accessed=2 * (2 * rows * (depth * count + width) + count * depth * width),
            transcendentals=0,
        ),
        name="project",
    )(table, *a_blocks, *chunks, *gates)


def place_kernel(column, total, *refs):
    in_refs, (out_ref, done) = refs[:2], refs[-2:]
    width = in_refs[0].shape[1]
    group = lax.axis_index("groups")
    copies = []
    for block, in_ref in enumerate(in_refs):
        start = (1 - group if block else group) * total + column
        at = pl.ds(pl.multiple_of(start, LANES), width)
        copies.append(pltpu.make_async_copy(in_ref, out_ref.at[:, at], done.at[block]))
    run_copies(copies)


def place(blocks, out, column, total, model_width):
    rows, width = blocks[0].shape
    held = [] if out is None else [out]
    return pl.pallas_call(
        functools.partial(place_kernel, column, total),
        out_shape=jax.ShapeDtypeStruct((rows, model_width), jnp.bfloat16),
        in_specs=[IN_VMEM] * len(blocks) + [ANYWHERE] * len(held),
        out_specs=ANYWHERE,
        scratch_shapes=[pltpu.SemaphoreType.DMA((len(blocks),))],
        input_output_aliases={len(blocks): 0} if held else {},
        compiler_params=pltpu.CompilerParams(vmem_limit_bytes=4 * MIB),
        cost_estimate=pl.CostEstimate(flops=0, bytes_accessed=4 * rows * width * len(blocks), transcendentals=0),
        name="place",
    )(*blocks, *held)


def hop_order(pieces, turns, opposite):
    order = []
    for piece in range(pieces):
        order += [(piece, strip, turn) for turn in range(1, turns + 1) for strip in range(2)]
        order += [(piece, None, turns + 1)] if opposite else []
    return order


def on_device(queries, key_value, keep, windows, gate, out_weight):
    frames_here, spots, features = queries.shape[1:]
    model_width = gate.shape[1]
    rows = frames_here * spots
    slabs = lax.axis_size("slab")
    total = model_width // lax.axis_size("groups")
    widths = piece_widths(total)

    count = lax.axis_size("owner")
    order = ring_order(count)
    spot_of = [order.index(owner) for owner in range(count)]
    ring = [
        (owner * slabs + slab, order[(spot_of[owner] + step) % count] * slabs + slab)
        for owner in range(count)
        for slab, step in enumerate((1, -1))
    ]
    turns, opposite = (count - 1) // 2, count % 2 == 0
    hops = hop_order(len(widths), turns, opposite)

    firsts = [2 * sum(widths[:piece]) for piece in range(len(widths))]
    held, arrived, crossed, edges = {}, [], {}, []
    for piece, width in enumerate(widths):
        own_strips, border = cut(out_weight, key_value, [width] * 2, firsts[piece], total, piece == 0)
        edges = border or edges
        for strip, own in enumerate(own_strips):
            held[piece, strip, 0] = own
    def hop(slot, *others):
        if slot >= len(hops):
            return
        piece, strip, turn = hops[slot]
        waits = list(others)
        if slot >= FLIGHT:
            waits.append(arrived[slot - FLIGHT])
        if slot > 2 * FLIGHT:
            waits.append(crossed[hops[slot - 2 * FLIGHT - 1]])
        if strip is None:
            value = pick(held[piece, 0, turn - 1], held[piece, 1, turn - 1])
        else:
            value = held[piece, strip, turn - 1]
        if waits:
            value = after(value, *waits)
        value = lax.ppermute(value, ("owner", "slab"), ring)
        held[hops[slot]] = value
        arrived.append(value)

    def cross(slot, *others):
        value = arrived[slot]
        crossed[hops[slot]] = swap(after(value, *others) if others else value, ("slab",))

    first_done = max(slot for slot, at in enumerate(hops) if at[0] == 0) if hops else 0
    halos = [swap(edge, ("slab",)) for edge in edges]
    for slot in range(FLIGHT):
        hop(slot)

    query_rows = queries.reshape(rows, features)
    key_value_rows = key_value.reshape(2, rows, features)
    waits, attended = {FLIGHT + 2: [held[piece, 0, 0] for piece in range(1, len(widths))]}, None
    for part in range(PARTS):
        attended = attend(query_rows, key_value_rows, halos[part], windows, spots, part, attended)
    a_blocks = (attended, swap(attended, ("groups",)))
    near_gate = scale_gate(after(keep, attended), gate)
    gates = (near_gate, swap(near_gate, ("groups",)))
    waits.setdefault(first_done, []).append(a_blocks[1])

    def project_piece(piece, *others):
        chunks = [held[piece, 0, 0], held[piece, 1, 0]]
        fixed = [(0, None), (1, None)]
        sources = [(0, 0), (0, 0)]
        for turn in range(1, turns + 1):
            for strip in range(2):
                chunks += [held[piece, strip, turn], crossed[piece, strip, turn]]
                fixed += [(strip, None)] * 2
                sources += [(-turn, turn), (turn, -turn)]
        if opposite:
            chunks += [held[piece, None, turns + 1], crossed[piece, None, turns + 1]] * 2
            fixed += [(strip, strip ^ mate) for strip in range(2) for mate in range(2)]
            sources += [(turns + 1, turns + 1)] * 4
        table = np.zeros((slabs, count, len(chunks)), np.int32)
        for slab in range(slabs):
            for owner in range(count):
                table[slab, owner] = [order[(spot_of[owner] + source[slab]) % count] for source in sources]
        if others:
            chunks[0] = after(chunks[0], *others)
        column = firsts[piece]
        own, away = project(jnp.asarray(table), a_blocks, chunks, tuple(fixed), gates, column, total)
        return [own, swap(away, ("groups",))], column

    results = []
    for slot in range(FLIGHT, len(hops)):
        if slot == first_done + 5:
            results.append(project_piece(0, arrived[first_done + 2]))
            waits.setdefault(slot, []).extend((results[0][0][0], arrived[slot - 1]))
        hop(slot, *waits.get(slot, []))
        cross(slot - FLIGHT, *([arrived[slot - FLIGHT + 1], gates[1]] if slot - FLIGHT == first_done else []))
    for slot in range(max(len(hops) - FLIGHT, 0), len(hops)):
        cross(slot)
    for piece in range(len(results), len(widths)):
        results.append(project_piece(piece, *(results[-1][0][1:] if results else [])))
    out = None
    for blocks, column in results:
        out = place(blocks, out, column, total, model_width)
    return out.reshape((1, frames_here, spots, model_width))


def solution(mesh):
    placed = (
        P(("groups", "owner"), "slab", None, None),
        P(None, ("groups", "owner"), "slab", None, None),
        P("groups"),
        P("groups", None),
        P("groups", None),
        P("owner", None),
    )
    return jax.shard_map(
        on_device,
        mesh=mesh,
        in_specs=placed,
        out_specs=P(("groups", "owner"), "slab", None, None),
        check_vma=False,
    )
```

```python
import functools
import math

import jax
import jax.numpy as jnp
import numpy as np
from jax import lax
from jax.experimental import pallas as pl
from jax.experimental.pallas import tpu as pltpu
from jax.sharding import PartitionSpec as P

HEAD_DIM = 128
WB = 14
HALO = 1
LANES = 128
NEG_LARGE = -1e30
PARTS = 2
FLIGHT = 2
MIB = 1024 * 1024
ANYWHERE = pl.BlockSpec(memory_space=pl.ANY)
IN_HBM = pl.BlockSpec(memory_space=pltpu.HBM)
IN_VMEM = pl.BlockSpec(memory_space=pltpu.VMEM)
IN_SMEM = pl.BlockSpec(memory_space=pltpu.SMEM)


def ring_order(count):
    width = max(w for w in range(1, count + 1) if count % w == 0 and w * w <= count)
    height = count // width
    if width == 1 or height % 2:
        return list(range(count))
    order = []
    for row in range(height):
        columns = range(1, width) if row % 2 == 0 else range(width - 1, 0, -1)
        order += [row * width + column for column in columns]
    return order + [row * width for row in range(height - 1, -1, -1)]


def piece_strips(half_width):
    tiles = half_width // (2 * LANES)
    late = 2 * tiles // 5
    early = (tiles - late) * LANES
    return [[early, early]] + ([[2 * late * LANES]] if late else [])


def swap(value, axes):
    count = math.prod(lax.axis_size(axis) for axis in axes)
    return lax.ppermute(value, axes, [(i, count - 1 - i) for i in range(count)])


def after(value, *others):
    return lax.optimization_barrier((value,) + others)[0]


def run_copies(copies):
    for copy in copies:
        copy.start()
    for copy in copies:
        copy.wait()


def through(sources, buffers, targets, arrived, left):
    first = [pltpu.make_async_copy(s, b, arrived.at[i]) for i, (s, b) in enumerate(zip(sources, buffers))]
    second = [pltpu.make_async_copy(b, t, left.at[i]) for i, (b, t) in enumerate(zip(buffers, targets))]
    for copy in first:
        copy.start()
    for before, copy in zip(first, second):
        before.wait()
        copy.start()
    for copy in second:
        copy.wait()


def cut_kernel(first, total, with_border, weight_ref, key_value_ref, *refs):
    count = len(refs) // 2 - 1
    out_refs, buffers, (arrived, left) = refs[:count], refs[count : 2 * count], refs[2 * count :]
    column = lax.axis_index("groups") * total + first
    sources = []
    for ref in out_refs[: count - PARTS] if with_border else out_refs:
        sources.append(weight_ref.at[:, pl.ds(pl.multiple_of(column, LANES), ref.shape[1])])
        column += ref.shape[1]
    if with_border:
        frames_here = key_value_ref.shape[2]
        frame = jnp.where(lax.axis_index("slab") == 0, frames_here - HALO, 0)
        width = out_refs[-1].shape[3]
        for part in range(PARTS):
            sources.append(key_value_ref.at[:, 0, pl.ds(frame, HALO), :, part * width : (part + 1) * width])
    through(sources, buffers, out_refs, arrived, left)


def cut(out_weight, key_value, strips, first, total, with_border):
    depth = out_weight.shape[0]
    kinds, _, _, spots, features = key_value.shape
    shapes = [(depth, width) for width in strips]
    shapes += [(kinds, HALO, spots, features // PARTS)] * PARTS if with_border else []
    out_weight = pltpu.with_memory_space_constraint(out_weight, pltpu.HBM)
    key_value = pltpu.with_memory_space_constraint(key_value, pltpu.HBM)
    outs = pl.pallas_call(
        functools.partial(cut_kernel, first, total, with_border),
        out_shape=[jax.ShapeDtypeStruct(shape, jnp.bfloat16) for shape in shapes],
        in_specs=[IN_HBM] * 2,
        out_specs=[ANYWHERE] * len(shapes),
        scratch_shapes=[pltpu.VMEM(shape, jnp.bfloat16) for shape in shapes]
        + [pltpu.SemaphoreType.DMA((len(shapes),))] * 2,
        compiler_params=pltpu.CompilerParams(vmem_limit_bytes=4 * MIB),
        cost_estimate=pl.CostEstimate(flops=0, bytes_accessed=4 * depth * sum(strips), transcendentals=0),
        name="cut",
    )(out_weight, key_value)
    return outs[: len(strips)], [edge.reshape(kinds, HALO * spots, features // PARTS) for edge in outs[len(strips) :]]


def pick_kernel(one_ref, other_ref, out_ref, done):
    width = out_ref.shape[1]
    for slab, ref in enumerate((one_ref, other_ref)):
        first = slab * width if ref.shape[1] > width else 0

        @pl.when(lax.axis_index("slab") == slab)
        def _():
            copy = pltpu.make_async_copy(ref.at[:, first : first + width], out_ref, done)
            copy.start()
            copy.wait()


def pick(strips):
    one, other = strips[0], strips[-1]
    shape = one.shape if len(strips) == 2 else (one.shape[0], one.shape[1] // 2)
    return pl.pallas_call(
        pick_kernel,
        out_shape=jax.ShapeDtypeStruct(shape, one.dtype),
        in_specs=[ANYWHERE] * 2,
        out_specs=ANYWHERE,
        scratch_shapes=[pltpu.SemaphoreType.DMA(())],
        compiler_params=pltpu.CompilerParams(vmem_limit_bytes=MIB),
        cost_estimate=pl.CostEstimate(flops=0, bytes_accessed=2 * one.size, transcendentals=0),
        name="pick",
    )(one, other)


def scale_kernel(keep_ref, gate_ref, out_ref):
    owner = lax.axis_index("owner")
    factor = jnp.where(owner % 2 == 1, keep_ref[owner // 2], 1).astype(jnp.float32)
    out_ref[...] = gate_ref[pl.ds(owner // 2, 1), :] * factor


def scale_gate(keep, gate):
    return pl.pallas_call(
        scale_kernel,
        out_shape=jax.ShapeDtypeStruct((1, gate.shape[1]), jnp.float32),
        in_specs=[IN_SMEM, IN_VMEM],
        out_specs=IN_VMEM,
        compiler_params=pltpu.CompilerParams(vmem_limit_bytes=MIB),
        name="scale_gate",
    )(keep, gate)


def token_place(count, dim, spots, first_frame):
    shape = (count, 1) if dim == 0 else (1, count)
    token = lax.broadcasted_iota(jnp.int32, shape, dim).astype(jnp.float32)
    frame = jnp.floor((token + 0.5) * (1.0 / spots))
    spot = token - frame * spots
    row = jnp.floor((spot + 0.5) * (1.0 / WB))
    return frame + first_frame, row, spot - row * WB


def attend_kernel(spots, windows_ref, q_ref, k_ref, v_ref, k_halo_ref, v_halo_ref, *refs):
    out_ref, bias = refs[-2:]
    rows = q_ref.shape[0]
    halo_rows = k_halo_ref.shape[0]
    keys = bias.shape[1]
    frames_here = rows // spots

    @pl.when(pl.program_id(0) == 0)
    def _():
        request = lax.axis_index("owner") // 2
        halo_frame = jnp.where(lax.axis_index("slab") == 0, 0, -HALO - frames_here).astype(jnp.float32)
        query = token_place(rows, 0, spots, 0.0)
        key = token_place(keys, 1, spots, 0.0)
        index = lax.broadcasted_iota(jnp.int32, (1, keys), 1)
        frame = jnp.where(index < rows, key[0], key[0] + halo_frame)
        frame = jnp.where(index < rows + halo_rows, frame, -NEG_LARGE)
        allowed = None
        for part, place in enumerate((frame, key[1], key[2])):
            near = jnp.abs(query[part] - place) <= windows_ref[request, part].astype(jnp.float32)
            allowed = near if allowed is None else allowed & near
        bias[...] = jnp.where(allowed, 0.0, NEG_LARGE)

    scale = math.log2(math.e) / math.sqrt(HEAD_DIM)
    pad = jnp.zeros((keys - rows - halo_rows, HEAD_DIM), jnp.bfloat16)
    ones = jnp.ones((keys, HEAD_DIM), jnp.bfloat16)
    for head in range(q_ref.shape[1] // HEAD_DIM):
        at = slice(head * HEAD_DIM, (head + 1) * HEAD_DIM)
        key = jnp.concatenate([k_ref[:, at], k_halo_ref[:, at], pad], axis=0)
        value = jnp.concatenate([v_ref[:, at], v_halo_ref[:, at], pad], axis=0)
        value = jnp.concatenate([value, ones], axis=1)
        score = lax.dot_general(q_ref[:, at], key, (((1,), (1,)), ((), ())), preferred_element_type=jnp.float32)
        score = score * scale + bias[...]
        weight = jnp.exp2(score - jnp.max(score, axis=1, keepdims=True)).astype(jnp.bfloat16)
        mixture = jnp.dot(weight, value, preferred_element_type=jnp.float32)
        out_ref[:, at] = (mixture[:, :HEAD_DIM] / mixture[:, HEAD_DIM:]).astype(jnp.bfloat16)


def attend(query_rows, key_value_rows, halo, windows, spots, part, attended):
    before = [] if attended is None else [attended]
    rows, features = query_rows.shape
    query_rows = pltpu.with_memory_space_constraint(query_rows, pltpu.HBM)
    width = features // PARTS
    heads = width // HEAD_DIM
    steps = 2 if heads % 2 == 0 else 1
    block = width // steps
    halo_rows = halo.shape[1]
    first = part * steps
    keys = pl.cdiv(rows + halo_rows, LANES) * LANES
    return pl.pallas_call(
        functools.partial(attend_kernel, spots),
        grid=(steps,),
        out_shape=jax.ShapeDtypeStruct((rows, features), jnp.bfloat16),
        in_specs=[
            IN_SMEM,
            pl.BlockSpec((rows, block), lambda i: (0, first + i)),
            pl.BlockSpec((None, rows, block), lambda i: (0, 0, first + i)),
            pl.BlockSpec((None, rows, block), lambda i: (1, 0, first + i)),
            pl.BlockSpec((None, halo_rows, block), lambda i: (0, 0, i)),
            pl.BlockSpec((None, halo_rows, block), lambda i: (1, 0, i)),
        ]
        + [ANYWHERE] * len(before),
        out_specs=pl.BlockSpec((rows, block), lambda i: (0, first + i)),
        input_output_aliases={6: 0} if before else {},
        scratch_shapes=[pltpu.VMEM((rows, keys), jnp.float32)],
        compiler_params=pltpu.CompilerParams(vmem_limit_bytes=10 * MIB),
        cost_estimate=pl.CostEstimate(
            flops=12 * rows * keys * width, bytes_accessed=2 * width * (2 * rows + 2 * keys), transcendentals=heads * rows * keys
        ),
        name="attend",
    )(windows, query_rows, key_value_rows, key_value_rows, halo, halo, *before)


def project_kernel(column, total, starts, tables_ref, *refs):
    a_refs, refs = refs[:2], refs[2:]
    w_refs, refs = refs[: len(starts)], refs[len(starts) :]
    gate_refs, out_refs, (rows_all, weight, arrived) = refs[:2], refs[2:4], refs[4:]
    owner, slab = lax.axis_index("owner"), lax.axis_index("slab")
    rows, half = a_refs[0].shape[0], weight.shape[2] // 2
    groups = ([], [])
    for index, a_ref in enumerate(a_refs):
        target = rows_all.at[index * rows : (index + 1) * rows]
        groups[0].append(pltpu.make_async_copy(a_ref, target, arrived.at[0, len(starts) + index]))
    for index, (w_ref, start) in enumerate(zip(w_refs, starts)):
        target = weight.at[tables_ref[slab, owner, index]]
        if w_ref.shape[1] > half:
            for where, group in enumerate(groups):
                at = slice(where * half, (where + 1) * half)
                group.append(pltpu.make_async_copy(w_ref.at[:, at], target.at[:, at], arrived.at[where, index]))
        elif start[0] == start[1]:
            at = slice(start[0], start[0] + half)
            groups[start[0] // half].append(pltpu.make_async_copy(w_ref, target.at[:, at], arrived.at[0, index]))
        else:
            at = pl.ds(pl.multiple_of(jnp.where(slab == 0, *start), LANES), half)
            groups[0].append(pltpu.make_async_copy(w_ref, target.at[:, at], arrived.at[0, index]))
    for group in groups:
        for copy in group:
            copy.start()
    for where, group in enumerate(groups):
        for copy in group:
            copy.wait()
        for first in range(where * half, (where + 1) * half, 2 * LANES):
            tile = min(2 * LANES, (where + 1) * half - first)
            columns = weight[:, :, first : first + tile].reshape(-1, tile)
            product = jnp.dot(rows_all[...], columns, preferred_element_type=jnp.float32)
            here = pl.ds(pl.multiple_of(lax.axis_index("groups") * total + column + first, LANES), tile)
            for block in range(2):
                gate = gate_refs[block][:, here]
                result = product[block * rows : (block + 1) * rows] * gate
                out_refs[block][:, first : first + tile] = result.astype(jnp.bfloat16)


def project(table, a_blocks, chunks, starts, gates, column, width, total):
    slabs, count, held = table.shape
    rows, features = a_blocks[0].shape
    depth = chunks[0].shape[0]
    return pl.pallas_call(
        functools.partial(project_kernel, column, total, starts),
        out_shape=[jax.ShapeDtypeStruct((rows, width), jnp.bfloat16)] * 2,
        in_specs=[IN_SMEM] + [ANYWHERE] * (len(a_blocks) + held) + [IN_VMEM] * 2,
        out_specs=[IN_VMEM] * 2,
        scratch_shapes=[
            pltpu.VMEM((2 * rows, features), jnp.bfloat16),
            pltpu.VMEM((count, depth, width), jnp.bfloat16),
            pltpu.SemaphoreType.DMA((2, held + len(a_blocks))),
        ],
        compiler_params=pltpu.CompilerParams(vmem_limit_bytes=16 * MIB),
        cost_estimate=pl.CostEstimate(
            flops=4 * rows * width * depth * count,
            bytes_accessed=2 * (2 * rows * (depth * count + width) + count * depth * width),
            transcendentals=0,
        ),
        name="project",
    )(table, *a_blocks, *chunks, *gates)


def place_kernel(column, total, *refs):
    in_refs, (out_ref, done) = refs[:2], refs[-2:]
    width = in_refs[0].shape[1]
    group = lax.axis_index("groups")
    copies = []
    for block, in_ref in enumerate(in_refs):
        start = (1 - group if block else group) * total + column
        at = pl.ds(pl.multiple_of(start, LANES), width)
        copies.append(pltpu.make_async_copy(in_ref, out_ref.at[:, at], done.at[block]))
    run_copies(copies)


def place(blocks, out, column, total, model_width):
    rows, width = blocks[0].shape
    held = [] if out is None else [out]
    return pl.pallas_call(
        functools.partial(place_kernel, column, total),
        out_shape=jax.ShapeDtypeStruct((rows, model_width), jnp.bfloat16),
        in_specs=[IN_VMEM] * len(blocks) + [ANYWHERE] * len(held),
        out_specs=ANYWHERE,
        scratch_shapes=[pltpu.SemaphoreType.DMA((len(blocks),))],
        input_output_aliases={len(blocks): 0} if held else {},
        compiler_params=pltpu.CompilerParams(vmem_limit_bytes=4 * MIB),
        cost_estimate=pl.CostEstimate(flops=0, bytes_accessed=4 * rows * width * len(blocks), transcendentals=0),
        name="place",
    )(*blocks, *held)


def hop_order(pieces, turns, opposite):
    order = []
    for piece, strips in enumerate(pieces):
        hops = [(piece, strip, turn) for turn in range(1, turns + 1) for strip in range(len(strips))]
        hops += [(piece, None, turns + 1)] if opposite else []
        order = order[:-1] + hops[:1] + order[-1:] + hops[1:] if order else hops
    return order


def on_device(queries, key_value, keep, windows, gate, out_weight):
    frames_here, spots, features = queries.shape[1:]
    model_width = gate.shape[1]
    rows = frames_here * spots
    slabs = lax.axis_size("slab")
    total = model_width // lax.axis_size("groups")
    pieces = piece_strips(total)

    count = lax.axis_size("owner")
    order = ring_order(count)
    spot_of = [order.index(owner) for owner in range(count)]
    ring = [
        (owner * slabs + slab, order[(spot_of[owner] + step) % count] * slabs + slab)
        for owner in range(count)
        for slab, step in enumerate((1, -1))
    ]
    turns, opposite = (count - 1) // 2, count % 2 == 0
    hops = hop_order(pieces, turns, opposite)

    firsts = [sum(sum(strips) for strips in pieces[:piece]) for piece in range(len(pieces))]
    held, arrived, crossed, edges = {}, [], {}, []
    for piece, strips in enumerate(pieces):
        own_strips, border = cut(out_weight, key_value, strips, firsts[piece], total, piece == 0)
        edges = border or edges
        for strip, own in enumerate(own_strips):
            held[piece, strip, 0] = own
    def hop(slot, *others):
        if slot >= len(hops):
            return
        piece, strip, turn = hops[slot]
        waits = list(others)
        if slot >= FLIGHT:
            waits.append(arrived[slot - FLIGHT])
        if slot > 2 * FLIGHT:
            waits.append(crossed[hops[slot - 2 * FLIGHT - 1]])
        if strip is None:
            value = pick([held[piece, strip, turn - 1] for strip in range(len(pieces[piece]))])
        else:
            value = held[piece, strip, turn - 1]
        if waits:
            value = after(value, *waits)
        value = lax.ppermute(value, ("owner", "slab"), ring)
        held[hops[slot]] = value
        arrived.append(value)

    def cross(slot, *others):
        value = arrived[slot]
        crossed[hops[slot]] = swap(after(value, *others) if others else value, ("slab",))

    first_done = max(slot for slot, at in enumerate(hops) if at[0] == 0) if hops else 0
    halos = [swap(edge, ("slab",)) for edge in edges]
    for slot in range(FLIGHT):
        hop(slot)

    query_rows = queries.reshape(rows, features)
    key_value_rows = key_value.reshape(2, rows, features)
    waits, attended = {FLIGHT + 2: [held[piece, 0, 0] for piece in range(1, len(pieces))]}, None
    for part in range(PARTS):
        attended = attend(query_rows, key_value_rows, halos[part], windows, spots, part, attended)
    a_blocks = (attended, swap(attended, ("groups",)))
    near_gate = scale_gate(after(keep, attended), gate)
    gates = (near_gate, swap(near_gate, ("groups",)))
    waits.setdefault(first_done, []).append(a_blocks[1])

    def project_piece(piece, *others):
        strips, width = pieces[piece], sum(pieces[piece])
        chunks, starts, sources = [], [], []
        for strip, strip_width in enumerate(strips):
            chunks.append(held[piece, strip, 0])
            starts.append((strip * strip_width,) * 2)
            sources.append((0, 0))
            for turn in range(1, turns + 1):
                chunks += [held[piece, strip, turn], crossed[piece, strip, turn]]
                starts += [(strip * strip_width,) * 2] * 2
                sources += [(-turn, turn), (turn, -turn)]
        if opposite:
            chunks += [held[piece, None, turns + 1], crossed[piece, None, turns + 1]]
            starts += [(0, width // 2), (width // 2, 0)]
            sources += [(turns + 1, turns + 1)] * 2
        table = np.zeros((slabs, count, len(chunks)), np.int32)
        for slab in range(slabs):
            for owner in range(count):
                table[slab, owner] = [order[(spot_of[owner] + source[slab]) % count] for source in sources]
        if others:
            chunks[0] = after(chunks[0], *others)
        column = firsts[piece]
        own, away = project(jnp.asarray(table), a_blocks, chunks, starts, gates, column, width, total)
        return [own, swap(away, ("groups",))], column

    results = []
    for slot in range(FLIGHT, len(hops)):
        cross(slot - FLIGHT, *([arrived[slot - FLIGHT - 1], gates[1]] if slot - FLIGHT == first_done else []))
        if slot == first_done + 2:
            results.append(project_piece(0))
            waits.setdefault(slot, []).extend((results[0][0][0], arrived[slot - 1]))
        hop(slot, *waits.get(slot, []))
    for slot in range(max(len(hops) - FLIGHT, 0), len(hops)):
        cross(slot)
    for piece in range(len(results), len(pieces)):
        results.append(project_piece(piece, *(results[-1][0][1:] if results else [])))
    out = None
    for blocks, column in results:
        out = place(blocks, out, column, total, model_width)
    return out.reshape((1, frames_here, spots, model_width))


def solution(mesh):
    placed = (
        P(("groups", "owner"), "slab", None, None),
        P(None, ("groups", "owner"), "slab", None, None),
        P("groups"),
        P("groups", None),
        P("groups", None),
        P("owner", None),
    )
    return jax.shard_map(
        on_device,
        mesh=mesh,
        in_specs=placed,
        out_specs=P(("groups", "owner"), "slab", None, None),
        check_vma=False,
    )
```

```python
import functools
import math

import jax
import jax.numpy as jnp
import numpy as np
from jax import lax
from jax.experimental import pallas as pl
from jax.experimental.pallas import tpu as pltpu
from jax.sharding import PartitionSpec as P

HEAD_DIM = 128
WB = 14
HALO = 1
LANES = 128
NEG_LARGE = -1e30
PARTS = 2
FLIGHT = 2
MIB = 1024 * 1024
ANYWHERE = pl.BlockSpec(memory_space=pl.ANY)
IN_HBM = pl.BlockSpec(memory_space=pltpu.HBM)
IN_VMEM = pl.BlockSpec(memory_space=pltpu.VMEM)
IN_SMEM = pl.BlockSpec(memory_space=pltpu.SMEM)


def ring_order(count):
    width = max(w for w in range(1, count + 1) if count % w == 0 and w * w <= count)
    height = count // width
    if width == 1 or height % 2:
        return list(range(count))
    order = []
    for row in range(height):
        columns = range(1, width) if row % 2 == 0 else range(width - 1, 0, -1)
        order += [row * width + column for column in columns]
    return order + [row * width for row in range(height - 1, -1, -1)]


def piece_widths(half_width):
    tiles = half_width // (2 * LANES)
    late = 2 * tiles // 5
    return [count * LANES for count in (tiles - late, late) if count]


def swap(value, axes):
    count = math.prod(lax.axis_size(axis) for axis in axes)
    return lax.ppermute(value, axes, [(i, count - 1 - i) for i in range(count)])


def after(value, *others):
    return lax.optimization_barrier((value,) + others)[0]


def run_copies(copies):
    for copy in copies:
        copy.start()
    for copy in copies:
        copy.wait()


def through(sources, buffers, targets, arrived, left):
    first = [pltpu.make_async_copy(s, b, arrived.at[i]) for i, (s, b) in enumerate(zip(sources, buffers))]
    second = [pltpu.make_async_copy(b, t, left.at[i]) for i, (b, t) in enumerate(zip(buffers, targets))]
    for copy in first:
        copy.start()
    for before, copy in zip(first, second):
        before.wait()
        copy.start()
    for copy in second:
        copy.wait()


def cut_kernel(first, total, with_border, weight_ref, key_value_ref, *refs):
    count = len(refs) // 2 - 1
    out_refs, buffers, (arrived, left) = refs[:count], refs[count : 2 * count], refs[2 * count :]
    slab = lax.axis_index("slab")
    width = out_refs[0].shape[1]
    sources = []
    for strip in range(2):
        column = lax.axis_index("groups") * total + first + (1 - slab if strip else slab) * width
        sources.append(weight_ref.at[:, pl.ds(pl.multiple_of(column, LANES), width)])
    if with_border:
        frames_here = key_value_ref.shape[2]
        frame = jnp.where(slab == 0, frames_here - HALO, 0)
        width = out_refs[-1].shape[3]
        for part in range(PARTS):
            sources.append(key_value_ref.at[:, 0, pl.ds(frame, HALO), :, part * width : (part + 1) * width])
    through(sources, buffers, out_refs, arrived, left)


def cut(out_weight, key_value, width, first, total, with_border):
    depth = out_weight.shape[0]
    kinds, _, _, spots, features = key_value.shape
    shapes = [(depth, width)] * 2
    shapes += [(kinds, HALO, spots, features // PARTS)] * PARTS if with_border else []
    out_weight = pltpu.with_memory_space_constraint(out_weight, pltpu.HBM)
    key_value = pltpu.with_memory_space_constraint(key_value, pltpu.HBM)
    outs = pl.pallas_call(
        functools.partial(cut_kernel, first, total, with_border),
        out_shape=[jax.ShapeDtypeStruct(shape, jnp.bfloat16) for shape in shapes],
        in_specs=[IN_HBM] * 2,
        out_specs=[ANYWHERE] * len(shapes),
        scratch_shapes=[pltpu.VMEM(shape, jnp.bfloat16) for shape in shapes]
        + [pltpu.SemaphoreType.DMA((len(shapes),))] * 2,
        compiler_params=pltpu.CompilerParams(vmem_limit_bytes=4 * MIB),
        cost_estimate=pl.CostEstimate(flops=0, bytes_accessed=8 * depth * width, transcendentals=0),
        name="cut",
    )(out_weight, key_value)
    return outs[:2], [edge.reshape(kinds, HALO * spots, features // PARTS) for edge in outs[2:]]


def scale_kernel(keep_ref, gate_ref, out_ref):
    owner = lax.axis_index("owner")
    factor = jnp.where(owner % 2 == 1, keep_ref[owner // 2], 1).astype(jnp.float32)
    out_ref[...] = gate_ref[pl.ds(owner // 2, 1), :] * factor


def scale_gate(keep, gate):
    return pl.pallas_call(
        scale_kernel,
        out_shape=jax.ShapeDtypeStruct((1, gate.shape[1]), jnp.float32),
        in_specs=[IN_SMEM, IN_VMEM],
        out_specs=IN_VMEM,
        compiler_params=pltpu.CompilerParams(vmem_limit_bytes=MIB),
        name="scale_gate",
    )(keep, gate)


def token_place(count, dim, spots, first_frame):
    shape = (count, 1) if dim == 0 else (1, count)
    token = lax.broadcasted_iota(jnp.int32, shape, dim).astype(jnp.float32)
    frame = jnp.floor((token + 0.5) * (1.0 / spots))
    spot = token - frame * spots
    row = jnp.floor((spot + 0.5) * (1.0 / WB))
    return frame + first_frame, row, spot - row * WB


def attend_kernel(spots, windows_ref, q_ref, k_ref, v_ref, k_halo_ref, v_halo_ref, *refs):
    out_ref, bias = refs[-2:]
    rows = q_ref.shape[0]
    halo_rows = k_halo_ref.shape[0]
    keys = bias.shape[1]
    frames_here = rows // spots

    @pl.when(pl.program_id(0) == 0)
    def _():
        request = lax.axis_index("owner") // 2
        halo_frame = jnp.where(lax.axis_index("slab") == 0, 0, -HALO - frames_here).astype(jnp.float32)
        query = token_place(rows, 0, spots, 0.0)
        key = token_place(keys, 1, spots, 0.0)
        index = lax.broadcasted_iota(jnp.int32, (1, keys), 1)
        frame = jnp.where(index < rows, key[0], key[0] + halo_frame)
        frame = jnp.where(index < rows + halo_rows, frame, -NEG_LARGE)
        allowed = None
        for part, place in enumerate((frame, key[1], key[2])):
            near = jnp.abs(query[part] - place) <= windows_ref[request, part].astype(jnp.float32)
            allowed = near if allowed is None else allowed & near
        bias[...] = jnp.where(allowed, 0.0, NEG_LARGE)

    scale = math.log2(math.e) / math.sqrt(HEAD_DIM)
    pad = jnp.zeros((keys - rows - halo_rows, HEAD_DIM), jnp.bfloat16)
    ones = jnp.ones((keys, HEAD_DIM), jnp.bfloat16)
    for head in range(q_ref.shape[1] // HEAD_DIM):
        at = slice(head * HEAD_DIM, (head + 1) * HEAD_DIM)
        key = jnp.concatenate([k_ref[:, at], k_halo_ref[:, at], pad], axis=0)
        value = jnp.concatenate([v_ref[:, at], v_halo_ref[:, at], pad], axis=0)
        value = jnp.concatenate([value, ones], axis=1)
        score = lax.dot_general(q_ref[:, at], key, (((1,), (1,)), ((), ())), preferred_element_type=jnp.float32)
        score = score * scale + bias[...]
        weight = jnp.exp2(score - jnp.max(score, axis=1, keepdims=True)).astype(jnp.bfloat16)
        mixture = jnp.dot(weight, value, preferred_element_type=jnp.float32)
        out_ref[:, at] = (mixture[:, :HEAD_DIM] / mixture[:, HEAD_DIM:]).astype(jnp.bfloat16)


def attend(query_rows, key_value_rows, halo, windows, spots, part, attended):
    before = [] if attended is None else [attended]
    rows, features = query_rows.shape
    query_rows = pltpu.with_memory_space_constraint(query_rows, pltpu.HBM)
    width = features // PARTS
    heads = width // HEAD_DIM
    steps = 2 if heads % 2 == 0 else 1
    block = width // steps
    halo_rows = halo.shape[1]
    first = part * steps
    keys = pl.cdiv(rows + halo_rows, LANES) * LANES
    return pl.pallas_call(
        functools.partial(attend_kernel, spots),
        grid=(steps,),
        out_shape=jax.ShapeDtypeStruct((rows, features), jnp.bfloat16),
        in_specs=[
            IN_SMEM,
            pl.BlockSpec((rows, block), lambda i: (0, first + i)),
            pl.BlockSpec((None, rows, block), lambda i: (0, 0, first + i)),
            pl.BlockSpec((None, rows, block), lambda i: (1, 0, first + i)),
            pl.BlockSpec((None, halo_rows, block), lambda i: (0, 0, i)),
            pl.BlockSpec((None, halo_rows, block), lambda i: (1, 0, i)),
        ]
        + [ANYWHERE] * len(before),
        out_specs=pl.BlockSpec((rows, block), lambda i: (0, first + i)),
        input_output_aliases={6: 0} if before else {},
        scratch_shapes=[pltpu.VMEM((rows, keys), jnp.float32)],
        compiler_params=pltpu.CompilerParams(vmem_limit_bytes=10 * MIB),
        cost_estimate=pl.CostEstimate(
            flops=32 * rows * keys * width, bytes_accessed=2 * width * (2 * rows + 2 * keys), transcendentals=heads * rows * keys
        ),
        name="attend",
    )(windows, query_rows, key_value_rows, key_value_rows, halo, halo, *before)


def project_kernel(strip, column, total, tables_ref, *refs):
    a_refs, refs = refs[:2], refs[2:]
    w_refs, refs = refs[: tables_ref.shape[2]], refs[tables_ref.shape[2] :]
    gate_refs, out_refs, (rows_all, weight, arrived) = refs[:2], refs[2:4], refs[4:]
    owner, slab = lax.axis_index("owner"), lax.axis_index("slab")
    rows, width = a_refs[0].shape[0], weight.shape[2]
    copies = []
    for index, a_ref in enumerate(a_refs):
        target = rows_all.at[index * rows : (index + 1) * rows]
        copies.append(pltpu.make_async_copy(a_ref, target, arrived.at[len(w_refs) + index]))
    for index, w_ref in enumerate(w_refs):
        target = weight.at[tables_ref[slab, owner, index]]
        copies.append(pltpu.make_async_copy(w_ref, target, arrived.at[index]))
    run_copies(copies)
    place = lax.axis_index("groups") * total + column + (1 - slab if strip else slab) * width
    for first in range(0, width, 2 * LANES):
        tile = min(2 * LANES, width - first)
        columns = weight[:, :, first : first + tile].reshape(-1, tile)
        product = jnp.dot(rows_all[...], columns, preferred_element_type=jnp.float32)
        here = pl.ds(pl.multiple_of(place + first, LANES), tile)
        for block in range(2):
            gate = gate_refs[block][:, here]
            result = product[block * rows : (block + 1) * rows] * gate
            out_refs[block][:, first : first + tile] = result.astype(jnp.bfloat16)


def project(table, a_blocks, chunks, gates, strip, column, total):
    rows, features = a_blocks[0].shape
    depth, width = chunks[0].shape
    count = len(chunks)
    return pl.pallas_call(
        functools.partial(project_kernel, strip, column, total),
        out_shape=[jax.ShapeDtypeStruct((rows, width), jnp.bfloat16)] * 2,
        in_specs=[IN_SMEM] + [ANYWHERE] * (len(a_blocks) + count) + [IN_VMEM] * 2,
        out_specs=[IN_VMEM] * 2,
        scratch_shapes=[
            pltpu.VMEM((2 * rows, features), jnp.bfloat16),
            pltpu.VMEM((count, depth, width), jnp.bfloat16),
            pltpu.SemaphoreType.DMA((count + len(a_blocks),)),
        ],
        compiler_params=pltpu.CompilerParams(vmem_limit_bytes=12 * MIB),
        cost_estimate=pl.CostEstimate(
            flops=4 * rows * width * depth * count,
            bytes_accessed=2 * (2 * rows * (depth * count + width) + count * depth * width),
            transcendentals=0,
        ),
        name="project",
    )(table, *a_blocks, *chunks, *gates)


def place_kernel(count, columns, total, *refs):
    in_refs, (out_ref, done) = refs[:count], refs[-2:]
    group, slab = lax.axis_index("groups"), lax.axis_index("slab")
    copies = []
    for index, in_ref in enumerate(in_refs):
        strip, away = divmod(index, 2)
        width = in_ref.shape[1]
        start = (1 - group if away else group) * total + columns[strip][0] + (1 - slab if columns[strip][1] else slab) * width
        at = pl.ds(pl.multiple_of(start, LANES), width)
        copies.append(pltpu.make_async_copy(in_ref, out_ref.at[:, at], done.at[index]))
    run_copies(copies)


def place(blocks, out, columns, total, model_width):
    rows = blocks[0].shape[0]
    held = [] if out is None else [out]
    return pl.pallas_call(
        functools.partial(place_kernel, len(blocks), columns, total),
        out_shape=jax.ShapeDtypeStruct((rows, model_width), jnp.bfloat16),
        in_specs=[IN_VMEM] * len(blocks) + [ANYWHERE] * len(held),
        out_specs=ANYWHERE,
        scratch_shapes=[pltpu.SemaphoreType.DMA((len(blocks),))],
        input_output_aliases={len(blocks): 0} if held else {},
        compiler_params=pltpu.CompilerParams(vmem_limit_bytes=4 * MIB),
        cost_estimate=pl.CostEstimate(flops=0, bytes_accessed=4 * sum(block.size for block in blocks), transcendentals=0),
        name="place",
    )(*blocks, *held)


def hop_order(pieces, turns):
    order = []
    for piece in range(pieces):
        hops = [(piece, strip, turn) for turn in range(1, turns[0] + 1) for strip in range(2) if turn <= turns[strip]]
        order = order[:-1] + hops[:1] + order[-1:] + hops[1:] if order else hops
    return order


def on_device(queries, key_value, keep, windows, gate, out_weight):
    frames_here, spots, features = queries.shape[1:]
    model_width = gate.shape[1]
    rows = frames_here * spots
    slabs = lax.axis_size("slab")
    total = model_width // lax.axis_size("groups")
    widths = piece_widths(total)

    count = lax.axis_size("owner")
    order = ring_order(count)
    spot_of = [order.index(owner) for owner in range(count)]
    ring = [
        (owner * slabs + slab, order[(spot_of[owner] + step) % count] * slabs + slab)
        for owner in range(count)
        for slab, step in enumerate((1, -1))
    ]
    turns = (count // 2, (count - 1) // 2)
    hops = hop_order(len(widths), turns)

    firsts = [2 * sum(widths[:piece]) for piece in range(len(widths))]
    held, arrived, crossed, edges = {}, [], {}, []
    for piece, width in enumerate(widths):
        own_strips, border = cut(out_weight, key_value, width, firsts[piece], total, piece == 0)
        edges = border or edges
        for strip, own in enumerate(own_strips):
            held[piece, strip, 0] = own

    def hop(slot, *others):
        if slot >= len(hops):
            return
        piece, strip, turn = hops[slot]
        waits = list(others)
        if slot >= FLIGHT:
            waits.append(arrived[slot - FLIGHT])
        if slot > 2 * FLIGHT:
            waits.append(crossed[hops[slot - 2 * FLIGHT - 1]])
        value = held[piece, strip, turn - 1]
        if waits:
            value = after(value, *waits)
        value = lax.ppermute(value, ("owner", "slab"), ring)
        held[hops[slot]] = value
        arrived.append(value)

    def cross(slot, *others):
        value = arrived[slot]
        crossed[hops[slot]] = swap(after(value, *others) if others else value, ("slab",))

    first_done = max(slot for slot, at in enumerate(hops) if at[0] == 0) if hops else 0
    halos = [swap(edge, ("slab",)) for edge in edges]
    for slot in range(FLIGHT):
        hop(slot)

    query_rows = queries.reshape(rows, features)
    key_value_rows = key_value.reshape(2, rows, features)
    waits, attended = {FLIGHT + 2: [held[piece, 0, 0] for piece in range(1, len(widths))]}, None
    for part in range(PARTS):
        attended = attend(query_rows, key_value_rows, halos[part], windows, spots, part, attended)
    a_blocks = (attended, swap(attended, ("groups",)))
    near_gate = scale_gate(after(keep, attended), gate)
    gates = (near_gate, swap(near_gate, ("groups",)))
    waits.setdefault(first_done, []).append(a_blocks[1])
    waits.setdefault(first_done + 1, []).append(gates[1])

    def project_strip(piece, strip, *others):
        chunks, sources = [], []
        for turn in range(turns[strip] + 1):
            chunks.append(held[piece, strip, turn])
            sources.append((-turn, turn))
        for turn in range(1, turns[1 - strip] + 1):
            chunks.append(crossed[piece, 1 - strip, turn])
            sources.append((turn, -turn))
        table = np.zeros((slabs, count, len(chunks)), np.int32)
        for slab in range(slabs):
            for owner in range(count):
                table[slab, owner] = [order[(spot_of[owner] + source[slab]) % count] for source in sources]
        if others:
            chunks[0] = after(chunks[0], *others)
        own, away = project(jnp.asarray(table), a_blocks, chunks, gates, strip, firsts[piece], total)
        return [own, swap(away, ("groups",))]

    results = {}
    for slot in range(FLIGHT, len(hops)):
        cross(slot - FLIGHT, *([arrived[slot - FLIGHT + 1]] if slot - FLIGHT == first_done - 2 else []))
        strip = slot - first_done - 2
        if 0 <= strip < 2:
            results[0, strip] = project_strip(0, strip)
            waits.setdefault(slot, []).append(results[0, strip][0])
            waits.setdefault(min(slot + 3, len(hops) - 1), []).append(results[0, strip][1])
        hop(slot, *waits.get(slot, []))
    for slot in range(max(len(hops) - FLIGHT, 0), len(hops)):
        cross(slot)
    for piece in range(len(widths)):
        for strip in range(2):
            if (piece, strip) not in results:
                results[piece, strip] = project_strip(piece, strip)
    out = None
    last = (len(widths) - 1, 1)
    for batch in ([key for key in results if key != last], [last]):
        blocks = [block for key in batch for block in results[key]]
        out = place(blocks, out, [(firsts[piece], strip) for piece, strip in batch], total, model_width)
    return out.reshape((1, frames_here, spots, model_width))


def solution(mesh):
    placed = (
        P(("groups", "owner"), "slab", None, None),
        P(None, ("groups", "owner"), "slab", None, None),
        P("groups"),
        P("groups", None),
        P("groups", None),
        P("owner", None),
    )
    return jax.shard_map(
        on_device,
        mesh=mesh,
        in_specs=placed,
        out_specs=P(("groups", "owner"), "slab", None, None),
        check_vma=False,
    )
```

```python
import functools
import math

import jax
import jax.numpy as jnp
import numpy as np
from jax import lax
from jax.experimental import pallas as pl
from jax.experimental.pallas import tpu as pltpu
from jax.sharding import PartitionSpec as P

HEAD_DIM = 128
WB = 14
HALO = 1
LANES = 128
NEG_LARGE = -1e30
PARTS = 2
FLIGHT = 2
MIB = 1024 * 1024
ANYWHERE = pl.BlockSpec(memory_space=pl.ANY)
IN_HBM = pl.BlockSpec(memory_space=pltpu.HBM)
IN_VMEM = pl.BlockSpec(memory_space=pltpu.VMEM)
IN_SMEM = pl.BlockSpec(memory_space=pltpu.SMEM)


def ring_order(count):
    width = max(w for w in range(1, count + 1) if count % w == 0 and w * w <= count)
    height = count // width
    if width == 1 or height % 2:
        return list(range(count))
    order = []
    for row in range(height):
        columns = range(1, width) if row % 2 == 0 else range(width - 1, 0, -1)
        order += [row * width + column for column in columns]
    return order + [row * width for row in range(height - 1, -1, -1)]


def piece_widths(half_width):
    tiles = half_width // (2 * LANES)
    late = 2 * tiles // 5
    return [count * LANES for count in (tiles - late, late) if count]


def swap(value, axes):
    count = math.prod(lax.axis_size(axis) for axis in axes)
    return lax.ppermute(value, axes, [(i, count - 1 - i) for i in range(count)])


def after(value, *others):
    return lax.optimization_barrier((value,) + others)[0]


def run_copies(copies):
    for copy in copies:
        copy.start()
    for copy in copies:
        copy.wait()


def through(sources, buffers, targets, arrived, left):
    first = [pltpu.make_async_copy(s, b, arrived.at[i]) for i, (s, b) in enumerate(zip(sources, buffers))]
    second = [pltpu.make_async_copy(b, t, left.at[i]) for i, (b, t) in enumerate(zip(buffers, targets))]
    for copy in first:
        copy.start()
    for before, copy in zip(first, second):
        before.wait()
        copy.start()
    for copy in second:
        copy.wait()


def cut_kernel(first, total, with_border, weight_ref, key_value_ref, *refs):
    count = len(refs) // 2 - 1
    out_refs, buffers, (arrived, left) = refs[:count], refs[count : 2 * count], refs[2 * count :]
    slab = lax.axis_index("slab")
    width = out_refs[0].shape[1]
    sources = []
    for strip in range(2):
        column = lax.axis_index("groups") * total + first + (1 - slab if strip else slab) * width
        sources.append(weight_ref.at[:, pl.ds(pl.multiple_of(column, LANES), width)])
    if with_border:
        frames_here = key_value_ref.shape[2]
        frame = jnp.where(slab == 0, frames_here - HALO, 0)
        width = out_refs[-1].shape[3]
        for part in range(PARTS):
            sources.append(key_value_ref.at[:, 0, pl.ds(frame, HALO), :, part * width : (part + 1) * width])
    through(sources, buffers, out_refs, arrived, left)


def cut(out_weight, key_value, width, first, total, with_border):
    depth = out_weight.shape[0]
    kinds, _, _, spots, features = key_value.shape
    shapes = [(depth, width)] * 2
    shapes += [(kinds, HALO, spots, features // PARTS)] * PARTS if with_border else []
    out_weight = pltpu.with_memory_space_constraint(out_weight, pltpu.HBM)
    key_value = pltpu.with_memory_space_constraint(key_value, pltpu.HBM)
    outs = pl.pallas_call(
        functools.partial(cut_kernel, first, total, with_border),
        out_shape=[jax.ShapeDtypeStruct(shape, jnp.bfloat16) for shape in shapes],
        in_specs=[IN_HBM] * 2,
        out_specs=[ANYWHERE] * len(shapes),
        scratch_shapes=[pltpu.VMEM(shape, jnp.bfloat16) for shape in shapes]
        + [pltpu.SemaphoreType.DMA((len(shapes),))] * 2,
        compiler_params=pltpu.CompilerParams(vmem_limit_bytes=4 * MIB),
        cost_estimate=pl.CostEstimate(flops=0, bytes_accessed=8 * depth * width, transcendentals=0),
        name="cut",
    )(out_weight, key_value)
    return outs[:2], [edge.reshape(kinds, HALO * spots, features // PARTS) for edge in outs[2:]]


def scale_kernel(keep_ref, gate_ref, out_ref):
    owner = lax.axis_index("owner")
    factor = jnp.where(owner % 2 == 1, keep_ref[owner // 2], 1).astype(jnp.float32)
    out_ref[...] = gate_ref[pl.ds(owner // 2, 1), :] * factor


def scale_gate(keep, gate):
    return pl.pallas_call(
        scale_kernel,
        out_shape=jax.ShapeDtypeStruct((1, gate.shape[1]), jnp.float32),
        in_specs=[IN_SMEM, IN_VMEM],
        out_specs=IN_VMEM,
        compiler_params=pltpu.CompilerParams(vmem_limit_bytes=MIB),
        name="scale_gate",
    )(keep, gate)


def token_place(count, dim, spots, first_frame):
    shape = (count, 1) if dim == 0 else (1, count)
    token = lax.broadcasted_iota(jnp.int32, shape, dim).astype(jnp.float32)
    frame = jnp.floor((token + 0.5) * (1.0 / spots))
    spot = token - frame * spots
    row = jnp.floor((spot + 0.5) * (1.0 / WB))
    return frame + first_frame, row, spot - row * WB


def attend_kernel(spots, windows_ref, q_ref, k_ref, v_ref, k_halo_ref, v_halo_ref, *refs):
    out_ref, bias = refs[-2:]
    rows = q_ref.shape[0]
    halo_rows = k_halo_ref.shape[0]
    keys = bias.shape[1]
    frames_here = rows // spots

    @pl.when(pl.program_id(0) == 0)
    def _():
        request = lax.axis_index("owner") // 2
        halo_frame = jnp.where(lax.axis_index("slab") == 0, 0, -HALO - frames_here).astype(jnp.float32)
        query = token_place(rows, 0, spots, 0.0)
        key = token_place(keys, 1, spots, 0.0)
        index = lax.broadcasted_iota(jnp.int32, (1, keys), 1)
        frame = jnp.where(index < rows, key[0], key[0] + halo_frame)
        frame = jnp.where(index < rows + halo_rows, frame, -NEG_LARGE)
        allowed = None
        for part, place in enumerate((frame, key[1], key[2])):
            near = jnp.abs(query[part] - place) <= windows_ref[request, part].astype(jnp.float32)
            allowed = near if allowed is None else allowed & near
        bias[...] = jnp.where(allowed, 0.0, NEG_LARGE)

    scale = math.log2(math.e) / math.sqrt(HEAD_DIM)
    pad = jnp.zeros((keys - rows - halo_rows, HEAD_DIM), jnp.bfloat16)
    ones = jnp.ones((keys, HEAD_DIM), jnp.bfloat16)
    for head in range(q_ref.shape[1] // HEAD_DIM):
        at = slice(head * HEAD_DIM, (head + 1) * HEAD_DIM)
        key = jnp.concatenate([k_ref[:, at], k_halo_ref[:, at], pad], axis=0)
        value = jnp.concatenate([v_ref[:, at], v_halo_ref[:, at], pad], axis=0)
        value = jnp.concatenate([value, ones], axis=1)
        score = lax.dot_general(q_ref[:, at], key, (((1,), (1,)), ((), ())), preferred_element_type=jnp.float32)
        score = score * scale + bias[...]
        weight = jnp.exp2(score - jnp.max(score, axis=1, keepdims=True)).astype(jnp.bfloat16)
        mixture = jnp.dot(weight, value, preferred_element_type=jnp.float32)
        out_ref[:, at] = (mixture[:, :HEAD_DIM] / mixture[:, HEAD_DIM:]).astype(jnp.bfloat16)


def attend(query_rows, key_value_rows, halo, windows, spots, part, attended):
    before = [] if attended is None else [attended]
    rows, features = query_rows.shape
    query_rows = pltpu.with_memory_space_constraint(query_rows, pltpu.HBM)
    width = features // PARTS
    heads = width // HEAD_DIM
    steps = 2 if heads % 2 == 0 else 1
    block = width // steps
    halo_rows = halo.shape[1]
    first = part * steps
    keys = pl.cdiv(rows + halo_rows, LANES) * LANES
    return pl.pallas_call(
        functools.partial(attend_kernel, spots),
        grid=(steps,),
        out_shape=jax.ShapeDtypeStruct((rows, features), jnp.bfloat16),
        in_specs=[
            IN_SMEM,
            pl.BlockSpec((rows, block), lambda i: (0, first + i)),
            pl.BlockSpec((None, rows, block), lambda i: (0, 0, first + i)),
            pl.BlockSpec((None, rows, block), lambda i: (1, 0, first + i)),
            pl.BlockSpec((None, halo_rows, block), lambda i: (0, 0, i)),
            pl.BlockSpec((None, halo_rows, block), lambda i: (1, 0, i)),
        ]
        + [ANYWHERE] * len(before),
        out_specs=pl.BlockSpec((rows, block), lambda i: (0, first + i)),
        input_output_aliases={6: 0} if before else {},
        scratch_shapes=[pltpu.VMEM((rows, keys), jnp.float32)],
        compiler_params=pltpu.CompilerParams(vmem_limit_bytes=10 * MIB),
        cost_estimate=pl.CostEstimate(
            flops=32 * rows * keys * width, bytes_accessed=2 * width * (2 * rows + 2 * keys), transcendentals=heads * rows * keys
        ),
        name="attend",
    )(windows, query_rows, key_value_rows, key_value_rows, halo, halo, *before)


def arrange_kernel(near_ref, far_ref, out_ref):
    rows = near_ref.shape[0]
    depth = out_ref.shape[2]
    for owner in range(out_ref.shape[0]):
        at = slice(owner * depth, (owner + 1) * depth)
        out_ref[owner, :rows] = near_ref[:, at]
        out_ref[owner, rows:] = far_ref[:, at]


def arrange(near, far, count):
    rows, features = near.shape
    return pl.pallas_call(
        arrange_kernel,
        out_shape=jax.ShapeDtypeStruct((count, 2 * rows, features // count), near.dtype),
        in_specs=[IN_VMEM] * 2,
        out_specs=IN_VMEM,
        compiler_params=pltpu.CompilerParams(vmem_limit_bytes=8 * MIB),
        cost_estimate=pl.CostEstimate(flops=0, bytes_accessed=8 * near.size, transcendentals=0),
        name="arrange",
    )(near, far)


def project_kernel(strip, column, total, tables_ref, rows_ref, *refs):
    count = tables_ref.shape[2]
    w_refs, gate_refs, out_refs = refs[:count], refs[count : count + 2], refs[count + 2 :]
    owner, slab = lax.axis_index("owner"), lax.axis_index("slab")
    rows, width = out_refs[0].shape
    sources = [tables_ref[slab, owner, index] for index in range(count)]
    place = lax.axis_index("groups") * total + column + (1 - slab if strip else slab) * width
    for first in range(0, width, 2 * LANES):
        tile = min(2 * LANES, width - first)
        product = None
        for source, w_ref in zip(sources, w_refs):
            term = jnp.dot(rows_ref[source], w_ref[:, first : first + tile], preferred_element_type=jnp.float32)
            product = term if product is None else product + term
        here = pl.ds(pl.multiple_of(place + first, LANES), tile)
        for block in range(2):
            gate = gate_refs[block][:, here]
            result = product[block * rows : (block + 1) * rows] * gate
            out_refs[block][:, first : first + tile] = result.astype(jnp.bfloat16)


def project(table, arranged, chunks, gates, strip, column, total):
    count, rows, depth = arranged.shape
    width = chunks[0].shape[1]
    return pl.pallas_call(
        functools.partial(project_kernel, strip, column, total),
        out_shape=[jax.ShapeDtypeStruct((rows // 2, width), jnp.bfloat16)] * 2,
        in_specs=[IN_SMEM] + [IN_VMEM] * (1 + count + 2),
        out_specs=[IN_VMEM] * 2,
        compiler_params=pltpu.CompilerParams(vmem_limit_bytes=16 * MIB),
        cost_estimate=pl.CostEstimate(
            flops=3 * rows * width * depth * count,
            bytes_accessed=2 * (rows * (depth * count + width) + count * depth * width),
            transcendentals=0,
        ),
        name="project",
    )(table, arranged, *chunks, *gates)


def place_kernel(count, columns, total, *refs):
    in_refs, (out_ref, done) = refs[:count], refs[-2:]
    group, slab = lax.axis_index("groups"), lax.axis_index("slab")
    copies = []
    for index, in_ref in enumerate(in_refs):
        strip, away = divmod(index, 2)
        width = in_ref.shape[1]
        start = (1 - group if away else group) * total + columns[strip][0] + (1 - slab if columns[strip][1] else slab) * width
        at = pl.ds(pl.multiple_of(start, LANES), width)
        copies.append(pltpu.make_async_copy(in_ref, out_ref.at[:, at], done.at[index]))
    run_copies(copies)


def place(blocks, out, columns, total, model_width):
    rows = blocks[0].shape[0]
    held = [] if out is None else [out]
    return pl.pallas_call(
        functools.partial(place_kernel, len(blocks), columns, total),
        out_shape=jax.ShapeDtypeStruct((rows, model_width), jnp.bfloat16),
        in_specs=[IN_VMEM] * len(blocks) + [ANYWHERE] * len(held),
        out_specs=ANYWHERE,
        scratch_shapes=[pltpu.SemaphoreType.DMA((len(blocks),))],
        input_output_aliases={len(blocks): 0} if held else {},
        compiler_params=pltpu.CompilerParams(vmem_limit_bytes=4 * MIB),
        cost_estimate=pl.CostEstimate(flops=0, bytes_accessed=4 * sum(block.size for block in blocks), transcendentals=0),
        name="place",
    )(*blocks, *held)


def hop_order(pieces, turns):
    order = []
    for piece in range(pieces):
        hops = [(piece, strip, turn) for turn in range(1, turns[0] + 1) for strip in range(2) if turn <= turns[strip]]
        order = order[:-1] + hops[:1] + order[-1:] + hops[1:] if order else hops
    return order


def on_device(queries, key_value, keep, windows, gate, out_weight):
    frames_here, spots, features = queries.shape[1:]
    model_width = gate.shape[1]
    rows = frames_here * spots
    slabs = lax.axis_size("slab")
    total = model_width // lax.axis_size("groups")
    widths = piece_widths(total)

    count = lax.axis_size("owner")
    order = ring_order(count)
    spot_of = [order.index(owner) for owner in range(count)]
    ring = [
        (owner * slabs + slab, order[(spot_of[owner] + step) % count] * slabs + slab)
        for owner in range(count)
        for slab, step in enumerate((1, -1))
    ]
    turns = (count // 2, (count - 1) // 2)
    hops = hop_order(len(widths), turns)

    firsts = [2 * sum(widths[:piece]) for piece in range(len(widths))]
    held, arrived, crossed, edges = {}, [], {}, []
    for piece, width in enumerate(widths):
        own_strips, border = cut(out_weight, key_value, width, firsts[piece], total, piece == 0)
        edges = border or edges
        for strip, own in enumerate(own_strips):
            held[piece, strip, 0] = own

    def hop(slot, *others):
        if slot >= len(hops):
            return
        piece, strip, turn = hops[slot]
        waits = list(others)
        if slot >= FLIGHT:
            waits.append(arrived[slot - FLIGHT])
        if slot > 2 * FLIGHT:
            waits.append(crossed[hops[slot - 2 * FLIGHT - 1]])
        value = held[piece, strip, turn - 1]
        if waits:
            value = after(value, *waits)
        value = lax.ppermute(value, ("owner", "slab"), ring)
        held[hops[slot]] = value
        arrived.append(value)

    def cross(slot, *others):
        value = arrived[slot]
        crossed[hops[slot]] = swap(after(value, *others) if others else value, ("slab",))

    first_done = max(slot for slot, at in enumerate(hops) if at[0] == 0) if hops else 0
    halos = [swap(edge, ("slab",)) for edge in edges]
    for slot in range(FLIGHT):
        hop(slot, *halos[:slot])

    query_rows = queries.reshape(rows, features)
    key_value_rows = key_value.reshape(2, rows, features)
    waits, attended = {FLIGHT + 2: [held[piece, 0, 0] for piece in range(1, len(widths))]}, None
    for part in range(PARTS):
        attended = attend(query_rows, key_value_rows, halos[part], windows, spots, part, attended)
    a_blocks = (attended, swap(attended, ("groups",)))
    near_gate = scale_gate(after(keep, attended), gate)
    gates = (near_gate, swap(near_gate, ("groups",)))
    waits.setdefault(first_done, []).append(a_blocks[1])

    arranged = arrange(*a_blocks, count)

    def project_strip(piece, strip, *others):
        chunks, sources = [], []
        for turn in range(turns[strip] + 1):
            chunks.append(held[piece, strip, turn])
            sources.append((-turn, turn))
        for turn in range(1, turns[1 - strip] + 1):
            chunks.append(crossed[piece, 1 - strip, turn])
            sources.append((turn, -turn))
        table = np.zeros((slabs, count, len(chunks)), np.int32)
        for slab in range(slabs):
            for owner in range(count):
                table[slab, owner] = [order[(spot_of[owner] + source[slab]) % count] for source in sources]
        if others:
            chunks[0] = after(chunks[0], *others)
        own, away = project(jnp.asarray(table), arranged, chunks, gates, strip, firsts[piece], total)
        return [own, swap(away, ("groups",))]

    results = {}
    for slot in range(FLIGHT, len(hops)):
        cross(slot - FLIGHT, *([arrived[slot - FLIGHT + 1], gates[1], arranged] if slot - FLIGHT == first_done - 2 else []))
        strip = slot - first_done - 2
        if 0 <= strip < 2:
            results[0, strip] = project_strip(0, strip)
            waits.setdefault(slot, []).append(results[0, strip][0])
            waits.setdefault(min(slot + 3, len(hops) - 1), []).append(results[0, strip][1])
        hop(slot, *waits.get(slot, []))
    for slot in range(max(len(hops) - FLIGHT, 0), len(hops)):
        cross(slot)
    for piece in range(len(widths)):
        for strip in range(2):
            if (piece, strip) not in results:
                results[piece, strip] = project_strip(piece, strip)
    out = None
    last = (len(widths) - 1, 1)
    for batch in ([key for key in results if key != last], [last]):
        blocks = [block for key in batch for block in results[key]]
        out = place(blocks, out, [(firsts[piece], strip) for piece, strip in batch], total, model_width)
    return out.reshape((1, frames_here, spots, model_width))


def solution(mesh):
    placed = (
        P(("groups", "owner"), "slab", None, None),
        P(None, ("groups", "owner"), "slab", None, None),
        P("groups"),
        P("groups", None),
        P("groups", None),
        P("owner", None),
    )
    return jax.shard_map(
        on_device,
        mesh=mesh,
        in_specs=placed,
        out_specs=P(("groups", "owner"), "slab", None, None),
        check_vma=False,
    )
```

```python
import functools
import math

import jax
import jax.numpy as jnp
import numpy as np
from jax import lax
from jax.experimental import pallas as pl
from jax.experimental.pallas import tpu as pltpu
from jax.sharding import PartitionSpec as P

HEAD_DIM = 128
WB = 14
HALO = 1
LANES = 128
NEG_LARGE = -1e30
PARTS = 2
FLIGHT = 2
MIB = 1024 * 1024
ANYWHERE = pl.BlockSpec(memory_space=pl.ANY)
IN_HBM = pl.BlockSpec(memory_space=pltpu.HBM)
IN_VMEM = pl.BlockSpec(memory_space=pltpu.VMEM)
IN_SMEM = pl.BlockSpec(memory_space=pltpu.SMEM)


def ring_order(count):
    width = max(w for w in range(1, count + 1) if count % w == 0 and w * w <= count)
    height = count // width
    if width == 1 or height % 2:
        return list(range(count))
    order = []
    for row in range(height):
        columns = range(1, width) if row % 2 == 0 else range(width - 1, 0, -1)
        order += [row * width + column for column in columns]
    return order + [row * width for row in range(height - 1, -1, -1)]


def piece_widths(half_width):
    tiles = half_width // (2 * LANES)
    late = 2 * tiles // 5
    return [count * LANES for count in (tiles - late, late) if count]


def swap(value, axes):
    count = math.prod(lax.axis_size(axis) for axis in axes)
    return lax.ppermute(value, axes, [(i, count - 1 - i) for i in range(count)])


def after(value, *others):
    return lax.optimization_barrier((value,) + others)[0]


def run_copies(copies):
    for copy in copies:
        copy.start()
    for copy in copies:
        copy.wait()


def through(sources, buffers, targets, arrived, left):
    first = [pltpu.make_async_copy(s, b, arrived.at[i]) for i, (s, b) in enumerate(zip(sources, buffers))]
    second = [pltpu.make_async_copy(b, t, left.at[i]) for i, (b, t) in enumerate(zip(buffers, targets))]
    for copy in first:
        copy.start()
    for before, copy in zip(first, second):
        before.wait()
        copy.start()
    for copy in second:
        copy.wait()


def cut_kernel(first, total, with_border, weight_ref, key_value_ref, *refs):
    count = len(refs) // 2 - 1
    out_refs, buffers, (arrived, left) = refs[:count], refs[count : 2 * count], refs[2 * count :]
    slab = lax.axis_index("slab")
    width = out_refs[0].shape[1]
    sources = []
    for strip in range(2):
        column = lax.axis_index("groups") * total + first + (1 - slab if strip else slab) * width
        sources.append(weight_ref.at[:, pl.ds(pl.multiple_of(column, LANES), width)])
    if with_border:
        frames_here = key_value_ref.shape[2]
        frame = jnp.where(slab == 0, frames_here - HALO, 0)
        width = out_refs[-1].shape[3]
        for part in range(PARTS):
            sources.append(key_value_ref.at[:, 0, pl.ds(frame, HALO), :, part * width : (part + 1) * width])
    through(sources, buffers, out_refs, arrived, left)


def cut(out_weight, key_value, width, first, total, with_border):
    depth = out_weight.shape[0]
    kinds, _, _, spots, features = key_value.shape
    shapes = [(depth, width)] * 2
    shapes += [(kinds, HALO, spots, features // PARTS)] * PARTS if with_border else []
    out_weight = pltpu.with_memory_space_constraint(out_weight, pltpu.HBM)
    key_value = pltpu.with_memory_space_constraint(key_value, pltpu.HBM)
    outs = pl.pallas_call(
        functools.partial(cut_kernel, first, total, with_border),
        out_shape=[jax.ShapeDtypeStruct(shape, jnp.bfloat16) for shape in shapes],
        in_specs=[IN_HBM] * 2,
        out_specs=[ANYWHERE] * len(shapes),
        scratch_shapes=[pltpu.VMEM(shape, jnp.bfloat16) for shape in shapes]
        + [pltpu.SemaphoreType.DMA((len(shapes),))] * 2,
        compiler_params=pltpu.CompilerParams(vmem_limit_bytes=4 * MIB),
        cost_estimate=pl.CostEstimate(flops=0, bytes_accessed=8 * depth * width, transcendentals=0),
        name="cut",
    )(out_weight, key_value)
    return outs[:2], [edge.reshape(kinds, HALO * spots, features // PARTS) for edge in outs[2:]]


def scale_kernel(keep_ref, gate_ref, out_ref):
    owner = lax.axis_index("owner")
    factor = jnp.where(owner % 2 == 1, keep_ref[owner // 2], 1).astype(jnp.float32)
    out_ref[...] = gate_ref[pl.ds(owner // 2, 1), :] * factor


def scale_gate(keep, gate):
    return pl.pallas_call(
        scale_kernel,
        out_shape=jax.ShapeDtypeStruct((1, gate.shape[1]), jnp.float32),
        in_specs=[IN_SMEM, IN_VMEM],
        out_specs=IN_VMEM,
        compiler_params=pltpu.CompilerParams(vmem_limit_bytes=MIB),
        name="scale_gate",
    )(keep, gate)


def token_place(count, dim, spots, first_frame):
    shape = (count, 1) if dim == 0 else (1, count)
    token = lax.broadcasted_iota(jnp.int32, shape, dim).astype(jnp.float32)
    frame = jnp.floor((token + 0.5) * (1.0 / spots))
    spot = token - frame * spots
    row = jnp.floor((spot + 0.5) * (1.0 / WB))
    return frame + first_frame, row, spot - row * WB


def attend_kernel(spots, windows_ref, q_ref, k_ref, v_ref, k_halo_ref, v_halo_ref, *refs):
    out_ref, bias = refs[-2:]
    rows = q_ref.shape[0]
    halo_rows = k_halo_ref.shape[0]
    keys = bias.shape[1]
    frames_here = rows // spots

    @pl.when(pl.program_id(0) == 0)
    def _():
        request = lax.axis_index("owner") // 2
        halo_frame = jnp.where(lax.axis_index("slab") == 0, 0, -HALO - frames_here).astype(jnp.float32)
        query = token_place(rows, 0, spots, 0.0)
        key = token_place(keys, 1, spots, 0.0)
        index = lax.broadcasted_iota(jnp.int32, (1, keys), 1)
        frame = jnp.where(index < rows, key[0], key[0] + halo_frame)
        frame = jnp.where(index < rows + halo_rows, frame, -NEG_LARGE)
        allowed = None
        for part, place in enumerate((frame, key[1], key[2])):
            near = jnp.abs(query[part] - place) <= windows_ref[request, part].astype(jnp.float32)
            allowed = near if allowed is None else allowed & near
        bias[...] = jnp.where(allowed, 0.0, NEG_LARGE)

    scale = math.log2(math.e) / math.sqrt(HEAD_DIM)
    pad = jnp.zeros((keys - rows - halo_rows, HEAD_DIM), jnp.bfloat16)
    ones = jnp.ones((keys, HEAD_DIM), jnp.bfloat16)
    for head in range(q_ref.shape[1] // HEAD_DIM):
        at = slice(head * HEAD_DIM, (head + 1) * HEAD_DIM)
        key = jnp.concatenate([k_ref[:, at], k_halo_ref[:, at], pad], axis=0)
        value = jnp.concatenate([v_ref[:, at], v_halo_ref[:, at], pad], axis=0)
        value = jnp.concatenate([value, ones], axis=1)
        score = lax.dot_general(q_ref[:, at], key, (((1,), (1,)), ((), ())), preferred_element_type=jnp.float32)
        score = score * scale + bias[...]
        weight = jnp.exp2(score - jnp.max(score, axis=1, keepdims=True)).astype(jnp.bfloat16)
        mixture = jnp.dot(weight, value, preferred_element_type=jnp.float32)
        out_ref[:, at] = (mixture[:, :HEAD_DIM] / mixture[:, HEAD_DIM:]).astype(jnp.bfloat16)


def attend(query_rows, key_value_rows, halo, windows, spots, part, attended):
    before = [] if attended is None else [attended]
    rows, features = query_rows.shape
    query_rows = pltpu.with_memory_space_constraint(query_rows, pltpu.HBM)
    width = features // PARTS
    heads = width // HEAD_DIM
    steps = 2 if heads % 2 == 0 else 1
    block = width // steps
    halo_rows = halo.shape[1]
    first = part * steps
    keys = pl.cdiv(rows + halo_rows, LANES) * LANES
    return pl.pallas_call(
        functools.partial(attend_kernel, spots),
        grid=(steps,),
        out_shape=jax.ShapeDtypeStruct((rows, features), jnp.bfloat16),
        in_specs=[
            IN_SMEM,
            pl.BlockSpec((rows, block), lambda i: (0, first + i)),
            pl.BlockSpec((None, rows, block), lambda i: (0, 0, first + i)),
            pl.BlockSpec((None, rows, block), lambda i: (1, 0, first + i)),
            pl.BlockSpec((None, halo_rows, block), lambda i: (0, 0, i)),
            pl.BlockSpec((None, halo_rows, block), lambda i: (1, 0, i)),
        ]
        + [ANYWHERE] * len(before),
        out_specs=pl.BlockSpec((rows, block), lambda i: (0, first + i)),
        input_output_aliases={6: 0} if before else {},
        scratch_shapes=[pltpu.VMEM((rows, keys), jnp.float32)],
        compiler_params=pltpu.CompilerParams(vmem_limit_bytes=10 * MIB),
        cost_estimate=pl.CostEstimate(
            flops=32 * rows * keys * width, bytes_accessed=2 * width * (2 * rows + 2 * keys), transcendentals=heads * rows * keys
        ),
        name="attend",
    )(windows, query_rows, key_value_rows, key_value_rows, halo, halo, *before)


def arrange_kernel(near_ref, far_ref, out_ref):
    rows = near_ref.shape[0]
    depth = out_ref.shape[2]
    for owner in range(out_ref.shape[0]):
        at = slice(owner * depth, (owner + 1) * depth)
        out_ref[owner, :rows] = near_ref[:, at]
        out_ref[owner, rows:] = far_ref[:, at]


def arrange(near, far, count):
    rows, features = near.shape
    return pl.pallas_call(
        arrange_kernel,
        out_shape=jax.ShapeDtypeStruct((count, 2 * rows, features // count), near.dtype),
        in_specs=[IN_VMEM] * 2,
        out_specs=IN_VMEM,
        compiler_params=pltpu.CompilerParams(vmem_limit_bytes=8 * MIB),
        cost_estimate=pl.CostEstimate(flops=0, bytes_accessed=8 * near.size, transcendentals=0),
        name="arrange",
    )(near, far)


def project_kernel(strip, column, total, tables_ref, rows_ref, *refs):
    count = tables_ref.shape[2]
    w_refs, gate_refs, out_refs = refs[:count], refs[count : count + 2], refs[count + 2 :]
    owner, slab = lax.axis_index("owner"), lax.axis_index("slab")
    rows, width = out_refs[0].shape
    sources = [tables_ref[slab, owner, index] for index in range(count)]
    place = lax.axis_index("groups") * total + column + (1 - slab if strip else slab) * width
    for first in range(0, width, 2 * LANES):
        tile = min(2 * LANES, width - first)
        product = None
        for source, w_ref in zip(sources, w_refs):
            term = jnp.dot(rows_ref[source], w_ref[:, first : first + tile], preferred_element_type=jnp.float32)
            product = term if product is None else product + term
        here = pl.ds(pl.multiple_of(place + first, LANES), tile)
        for block in range(2):
            gate = gate_refs[block][:, here]
            result = product[block * rows : (block + 1) * rows] * gate
            out_refs[block][:, first : first + tile] = result.astype(jnp.bfloat16)


def project(table, arranged, chunks, gates, strip, column, total):
    count, rows, depth = arranged.shape
    width = chunks[0].shape[1]
    return pl.pallas_call(
        functools.partial(project_kernel, strip, column, total),
        out_shape=[jax.ShapeDtypeStruct((rows // 2, width), jnp.bfloat16)] * 2,
        in_specs=[IN_SMEM] + [IN_VMEM] * (1 + count + 2),
        out_specs=[IN_VMEM] * 2,
        compiler_params=pltpu.CompilerParams(vmem_limit_bytes=16 * MIB),
        cost_estimate=pl.CostEstimate(
            flops=3 * rows * width * depth * count,
            bytes_accessed=2 * (rows * (depth * count + width) + count * depth * width),
            transcendentals=0,
        ),
        name="project",
    )(table, arranged, *chunks, *gates)


def place_kernel(count, columns, total, *refs):
    in_refs, (out_ref, done) = refs[:count], refs[-2:]
    group, slab = lax.axis_index("groups"), lax.axis_index("slab")
    copies = []
    for index, in_ref in enumerate(in_refs):
        strip, away = divmod(index, 2)
        width = in_ref.shape[1]
        start = (1 - group if away else group) * total + columns[strip][0] + (1 - slab if columns[strip][1] else slab) * width
        at = pl.ds(pl.multiple_of(start, LANES), width)
        copies.append(pltpu.make_async_copy(in_ref, out_ref.at[:, at], done.at[index]))
    run_copies(copies)


def place(blocks, out, columns, total, model_width):
    rows = blocks[0].shape[0]
    held = [] if out is None else [out]
    return pl.pallas_call(
        functools.partial(place_kernel, len(blocks), columns, total),
        out_shape=jax.ShapeDtypeStruct((rows, model_width), jnp.bfloat16),
        in_specs=[IN_VMEM] * len(blocks) + [ANYWHERE] * len(held),
        out_specs=ANYWHERE,
        scratch_shapes=[pltpu.SemaphoreType.DMA((len(blocks),))],
        input_output_aliases={len(blocks): 0} if held else {},
        compiler_params=pltpu.CompilerParams(vmem_limit_bytes=4 * MIB),
        cost_estimate=pl.CostEstimate(flops=0, bytes_accessed=4 * sum(block.size for block in blocks), transcendentals=0),
        name="place",
    )(*blocks, *held)


def hop_order(pieces, turns):
    order = []
    for piece in range(pieces):
        hops = [(piece, strip, turn) for turn in range(1, turns[0] + 1) for strip in range(2) if turn <= turns[strip]]
        order = order[:-1] + hops[:1] + order[-1:] + hops[1:] if order else hops
    return order


def on_device(queries, key_value, keep, windows, gate, out_weight):
    frames_here, spots, features = queries.shape[1:]
    model_width = gate.shape[1]
    rows = frames_here * spots
    slabs = lax.axis_size("slab")
    total = model_width // lax.axis_size("groups")
    widths = piece_widths(total)

    count = lax.axis_size("owner")
    order = ring_order(count)
    spot_of = [order.index(owner) for owner in range(count)]
    ring = [
        (owner * slabs + slab, order[(spot_of[owner] + step) % count] * slabs + slab)
        for owner in range(count)
        for slab, step in enumerate((1, -1))
    ]
    turns = (count // 2, (count - 1) // 2)
    hops = hop_order(len(widths), turns)

    firsts = [2 * sum(widths[:piece]) for piece in range(len(widths))]
    held, arrived, crossed, edges = {}, [], {}, []
    for piece, width in enumerate(widths):
        own_strips, border = cut(out_weight, key_value, width, firsts[piece], total, piece == 0)
        edges = border or edges
        for strip, own in enumerate(own_strips):
            held[piece, strip, 0] = own

    def hop(slot, *others):
        if slot >= len(hops):
            return
        piece, strip, turn = hops[slot]
        waits = list(others)
        if slot >= FLIGHT:
            waits.append(arrived[slot - FLIGHT])
        if slot > 2 * FLIGHT:
            waits.append(crossed[hops[slot - 2 * FLIGHT - 1]])
        value = held[piece, strip, turn - 1]
        if waits:
            value = after(value, *waits)
        value = lax.ppermute(value, ("owner", "slab"), ring)
        held[hops[slot]] = value
        arrived.append(value)

    def cross(slot, *others):
        value = arrived[slot]
        crossed[hops[slot]] = swap(after(value, *others) if others else value, ("slab",))

    first_done = max(slot for slot, at in enumerate(hops) if at[0] == 0) if hops else 0
    halos = [swap(edge, ("slab",)) for edge in edges]
    for slot in range(FLIGHT):
        hop(slot, *halos[:slot])

    query_rows = queries.reshape(rows, features)
    key_value_rows = key_value.reshape(2, rows, features)
    waits, attended = {FLIGHT + 2: [held[piece, 0, 0] for piece in range(1, len(widths))]}, None
    for part in range(PARTS):
        attended = attend(query_rows, key_value_rows, halos[part], windows, spots, part, attended)
    a_blocks = (attended, swap(attended, ("groups",)))
    near_gate = scale_gate(after(keep, attended), gate)
    gates = (near_gate, swap(near_gate, ("groups",)))
    waits.setdefault(first_done, []).append(a_blocks[1])

    arranged = arrange(*a_blocks, count)

    def project_strip(piece, strip, *others):
        chunks, sources = [], []
        for turn in range(turns[strip] + 1):
            chunks.append(held[piece, strip, turn])
            sources.append((-turn, turn))
        for turn in range(1, turns[1 - strip] + 1):
            chunks.append(crossed[piece, 1 - strip, turn])
            sources.append((turn, -turn))
        table = np.zeros((slabs, count, len(chunks)), np.int32)
        for slab in range(slabs):
            for owner in range(count):
                table[slab, owner] = [order[(spot_of[owner] + source[slab]) % count] for source in sources]
        if others:
            chunks[0] = after(chunks[0], *others)
        own, away = project(jnp.asarray(table), arranged, chunks, gates, strip, firsts[piece], total)
        return [own, swap(away, ("groups",))]

    results, needs = {}, {}
    if first_done >= 2 and first_done + 1 < len(hops):
        needs[first_done - 2] = [first_done - 1, gates[1], arranged]
        needs[first_done] = [first_done + 1]
    for slot in range(FLIGHT, len(hops)):
        others = needs.get(slot - FLIGHT, [])
        cross(slot - FLIGHT, *(arrived[other] if isinstance(other, int) else other for other in others))
        strip = slot - first_done - 3
        if 0 <= strip < 2:
            results[0, strip] = project_strip(0, strip)
            waits.setdefault(slot, []).append(results[0, strip][0])
            if strip:
                needs[len(hops) - 2] = [results[0, strip][1]]
            else:
                waits.setdefault(len(hops) - 2, []).append(results[0, strip][1])
        hop(slot, *waits.get(slot, []))
    for slot in range(max(len(hops) - FLIGHT, 0), len(hops)):
        cross(slot, *needs.get(slot, []))
    for piece in range(len(widths)):
        for strip in range(2):
            if (piece, strip) not in results:
                results[piece, strip] = project_strip(piece, strip)
    out = None
    last = (len(widths) - 1, 1)
    for batch in ([key for key in results if key != last], [last]):
        blocks = [block for key in batch for block in results[key]]
        out = place(blocks, out, [(firsts[piece], strip) for piece, strip in batch], total, model_width)
    return out.reshape((1, frames_here, spots, model_width))


def solution(mesh):
    placed = (
        P(("groups", "owner"), "slab", None, None),
        P(None, ("groups", "owner"), "slab", None, None),
        P("groups"),
        P("groups", None),
        P("groups", None),
        P("owner", None),
    )
    return jax.shard_map(
        on_device,
        mesh=mesh,
        in_specs=placed,
        out_specs=P(("groups", "owner"), "slab", None, None),
        check_vma=False,
    )
```

```python
import functools
import math

import jax
import jax.numpy as jnp
import numpy as np
from jax import lax
from jax.experimental import pallas as pl
from jax.experimental.pallas import tpu as pltpu
from jax.sharding import PartitionSpec as P

HEAD_DIM = 128
WB = 14
HALO = 1
LANES = 128
NEG_LARGE = -1e30
PARTS = 2
FLIGHT = 2
MIB = 1024 * 1024
ANYWHERE = pl.BlockSpec(memory_space=pl.ANY)
IN_HBM = pl.BlockSpec(memory_space=pltpu.HBM)
IN_VMEM = pl.BlockSpec(memory_space=pltpu.VMEM)
IN_SMEM = pl.BlockSpec(memory_space=pltpu.SMEM)


def ring_order(count):
    width = max(w for w in range(1, count + 1) if count % w == 0 and w * w <= count)
    height = count // width
    if width == 1 or height % 2:
        return list(range(count))
    order = []
    for row in range(height):
        columns = range(1, width) if row % 2 == 0 else range(width - 1, 0, -1)
        order += [row * width + column for column in columns]
    return order + [row * width for row in range(height - 1, -1, -1)]


def piece_widths(half_width):
    tiles = half_width // (2 * LANES)
    late = 2 * tiles // 5
    return [count * LANES for count in (tiles - late, late) if count]


def swap(value, axes):
    count = math.prod(lax.axis_size(axis) for axis in axes)
    return lax.ppermute(value, axes, [(i, count - 1 - i) for i in range(count)])


def after(value, *others):
    return lax.optimization_barrier((value,) + others)[0]


def run_copies(copies):
    for copy in copies:
        copy.start()
    for copy in copies:
        copy.wait()


def through(sources, buffers, targets, arrived, left):
    first = [pltpu.make_async_copy(s, b, arrived.at[i]) for i, (s, b) in enumerate(zip(sources, buffers))]
    second = [pltpu.make_async_copy(b, t, left.at[i]) for i, (b, t) in enumerate(zip(buffers, targets))]
    for copy in first:
        copy.start()
    for before, copy in zip(first, second):
        before.wait()
        copy.start()
    for copy in second:
        copy.wait()


def cut_kernel(first, total, with_border, weight_ref, key_value_ref, *refs):
    count = len(refs) // 2 - 1
    out_refs, buffers, (arrived, left) = refs[:count], refs[count : 2 * count], refs[2 * count :]
    slab = lax.axis_index("slab")
    width = out_refs[0].shape[1]
    sources = []
    for strip in range(2):
        column = lax.axis_index("groups") * total + first + (1 - slab if strip else slab) * width
        sources.append(weight_ref.at[:, pl.ds(pl.multiple_of(column, LANES), width)])
    if with_border:
        frames_here = key_value_ref.shape[2]
        frame = jnp.where(slab == 0, frames_here - HALO, 0)
        width = out_refs[-1].shape[3]
        for part in range(PARTS):
            sources.append(key_value_ref.at[:, 0, pl.ds(frame, HALO), :, part * width : (part + 1) * width])
    through(sources, buffers, out_refs, arrived, left)


def cut(out_weight, key_value, width, first, total, with_border):
    depth = out_weight.shape[0]
    kinds, _, _, spots, features = key_value.shape
    shapes = [(depth, width)] * 2
    shapes += [(kinds, HALO, spots, features // PARTS)] * PARTS if with_border else []
    out_weight = pltpu.with_memory_space_constraint(out_weight, pltpu.HBM)
    key_value = pltpu.with_memory_space_constraint(key_value, pltpu.HBM)
    outs = pl.pallas_call(
        functools.partial(cut_kernel, first, total, with_border),
        out_shape=[jax.ShapeDtypeStruct(shape, jnp.bfloat16) for shape in shapes],
        in_specs=[IN_HBM] * 2,
        out_specs=[ANYWHERE] * len(shapes),
        scratch_shapes=[pltpu.VMEM(shape, jnp.bfloat16) for shape in shapes]
        + [pltpu.SemaphoreType.DMA((len(shapes),))] * 2,
        compiler_params=pltpu.CompilerParams(vmem_limit_bytes=4 * MIB),
        cost_estimate=pl.CostEstimate(flops=0, bytes_accessed=8 * depth * width, transcendentals=0),
        name="cut",
    )(out_weight, key_value)
    return outs[:2], [edge.reshape(kinds, HALO * spots, features // PARTS) for edge in outs[2:]]


def scale_kernel(keep_ref, gate_ref, out_ref):
    owner = lax.axis_index("owner")
    factor = jnp.where(owner % 2 == 1, keep_ref[owner // 2], 1).astype(jnp.float32)
    out_ref[...] = gate_ref[pl.ds(owner // 2, 1), :] * factor


def scale_gate(keep, gate):
    return pl.pallas_call(
        scale_kernel,
        out_shape=jax.ShapeDtypeStruct((1, gate.shape[1]), jnp.float32),
        in_specs=[IN_SMEM, IN_VMEM],
        out_specs=IN_VMEM,
        compiler_params=pltpu.CompilerParams(vmem_limit_bytes=MIB),
        name="scale_gate",
    )(keep, gate)


def token_place(count, dim, spots, first_frame):
    shape = (count, 1) if dim == 0 else (1, count)
    token = lax.broadcasted_iota(jnp.int32, shape, dim).astype(jnp.float32)
    frame = jnp.floor((token + 0.5) * (1.0 / spots))
    spot = token - frame * spots
    row = jnp.floor((spot + 0.5) * (1.0 / WB))
    return frame + first_frame, row, spot - row * WB


def attend_kernel(spots, windows_ref, q_ref, k_ref, v_ref, k_halo_ref, v_halo_ref, *refs):
    out_ref, bias = refs[-2:]
    rows = q_ref.shape[0]
    halo_rows = k_halo_ref.shape[0]
    keys = bias.shape[1]
    frames_here = rows // spots

    @pl.when(pl.program_id(0) == 0)
    def _():
        request = lax.axis_index("owner") // 2
        halo_frame = jnp.where(lax.axis_index("slab") == 0, 0, -HALO - frames_here).astype(jnp.float32)
        query = token_place(rows, 0, spots, 0.0)
        key = token_place(keys, 1, spots, 0.0)
        index = lax.broadcasted_iota(jnp.int32, (1, keys), 1)
        frame = jnp.where(index < rows, key[0], key[0] + halo_frame)
        frame = jnp.where(index < rows + halo_rows, frame, -NEG_LARGE)
        allowed = None
        for part, place in enumerate((frame, key[1], key[2])):
            near = jnp.abs(query[part] - place) <= windows_ref[request, part].astype(jnp.float32)
            allowed = near if allowed is None else allowed & near
        bias[...] = jnp.where(allowed, 0.0, NEG_LARGE)

    scale = math.log2(math.e) / math.sqrt(HEAD_DIM)
    pad = jnp.zeros((keys - rows - halo_rows, HEAD_DIM), jnp.bfloat16)
    ones = jnp.ones((keys, HEAD_DIM), jnp.bfloat16)
    for head in range(q_ref.shape[1] // HEAD_DIM):
        at = slice(head * HEAD_DIM, (head + 1) * HEAD_DIM)
        key = jnp.concatenate([k_ref[:, at], k_halo_ref[:, at], pad], axis=0)
        value = jnp.concatenate([v_ref[:, at], v_halo_ref[:, at], pad], axis=0)
        value = jnp.concatenate([value, ones], axis=1)
        score = lax.dot_general(q_ref[:, at], key, (((1,), (1,)), ((), ())), preferred_element_type=jnp.float32)
        score = score * scale + bias[...]
        weight = jnp.exp2(score - jnp.max(score, axis=1, keepdims=True)).astype(jnp.bfloat16)
        mixture = jnp.dot(weight, value, preferred_element_type=jnp.float32)
        out_ref[:, at] = (mixture[:, :HEAD_DIM] / mixture[:, HEAD_DIM:]).astype(jnp.bfloat16)


def attend(query_rows, key_value_rows, halo, windows, spots, part, attended):
    before = [] if attended is None else [attended]
    rows, features = query_rows.shape
    query_rows = pltpu.with_memory_space_constraint(query_rows, pltpu.HBM)
    width = features // PARTS
    heads = width // HEAD_DIM
    steps = 2 if heads % 2 == 0 else 1
    block = width // steps
    halo_rows = halo.shape[1]
    first = part * steps
    keys = pl.cdiv(rows + halo_rows, LANES) * LANES
    return pl.pallas_call(
        functools.partial(attend_kernel, spots),
        grid=(steps,),
        out_shape=jax.ShapeDtypeStruct((rows, features), jnp.bfloat16),
        in_specs=[
            IN_SMEM,
            pl.BlockSpec((rows, block), lambda i: (0, first + i)),
            pl.BlockSpec((None, rows, block), lambda i: (0, 0, first + i)),
            pl.BlockSpec((None, rows, block), lambda i: (1, 0, first + i)),
            pl.BlockSpec((None, halo_rows, block), lambda i: (0, 0, i)),
            pl.BlockSpec((None, halo_rows, block), lambda i: (1, 0, i)),
        ]
        + [ANYWHERE] * len(before),
        out_specs=pl.BlockSpec((rows, block), lambda i: (0, first + i)),
        input_output_aliases={6: 0} if before else {},
        scratch_shapes=[pltpu.VMEM((rows, keys), jnp.float32)],
        compiler_params=pltpu.CompilerParams(vmem_limit_bytes=10 * MIB),
        cost_estimate=pl.CostEstimate(
            flops=32 * rows * keys * width, bytes_accessed=2 * width * (2 * rows + 2 * keys), transcendentals=heads * rows * keys
        ),
        name="attend",
    )(windows, query_rows, key_value_rows, key_value_rows, halo, halo, *before)


def arrange_kernel(near_ref, far_ref, out_ref):
    rows = near_ref.shape[0]
    depth = out_ref.shape[2]
    for owner in range(out_ref.shape[0]):
        at = slice(owner * depth, (owner + 1) * depth)
        out_ref[owner, :rows] = near_ref[:, at]
        out_ref[owner, rows:] = far_ref[:, at]


def arrange(near, far, count):
    rows, features = near.shape
    return pl.pallas_call(
        arrange_kernel,
        out_shape=jax.ShapeDtypeStruct((count, 2 * rows, features // count), near.dtype),
        in_specs=[IN_VMEM] * 2,
        out_specs=IN_VMEM,
        compiler_params=pltpu.CompilerParams(vmem_limit_bytes=8 * MIB),
        cost_estimate=pl.CostEstimate(flops=0, bytes_accessed=8 * near.size, transcendentals=0),
        name="arrange",
    )(near, far)


def project_kernel(strip, column, total, tables_ref, rows_ref, *refs):
    count = tables_ref.shape[2]
    w_refs, gate_refs, out_refs = refs[:count], refs[count : count + 2], refs[count + 2 :]
    owner, slab = lax.axis_index("owner"), lax.axis_index("slab")
    rows, width = out_refs[0].shape
    sources = [tables_ref[slab, owner, index] for index in range(count)]
    place = lax.axis_index("groups") * total + column + (1 - slab if strip else slab) * width
    for first in range(0, width, 2 * LANES):
        tile = min(2 * LANES, width - first)
        product = None
        for source, w_ref in zip(sources, w_refs):
            term = jnp.dot(rows_ref[source], w_ref[:, first : first + tile], preferred_element_type=jnp.float32)
            product = term if product is None else product + term
        here = pl.ds(pl.multiple_of(place + first, LANES), tile)
        for block in range(2):
            gate = gate_refs[block][:, here]
            result = product[block * rows : (block + 1) * rows] * gate
            out_refs[block][:, first : first + tile] = result.astype(jnp.bfloat16)


def project(table, arranged, chunks, gates, strip, column, total):
    count, rows, depth = arranged.shape
    width = chunks[0].shape[1]
    return pl.pallas_call(
        functools.partial(project_kernel, strip, column, total),
        out_shape=[jax.ShapeDtypeStruct((rows // 2, width), jnp.bfloat16)] * 2,
        in_specs=[IN_SMEM] + [IN_VMEM] * (1 + count + 2),
        out_specs=[IN_VMEM] * 2,
        compiler_params=pltpu.CompilerParams(vmem_limit_bytes=16 * MIB),
        cost_estimate=pl.CostEstimate(
            flops=3 * rows * width * depth * count,
            bytes_accessed=2 * (rows * (depth * count + width) + count * depth * width),
            transcendentals=0,
        ),
        name="project",
    )(table, arranged, *chunks, *gates)


def place_kernel(count, columns, total, *refs):
    in_refs, (out_ref, done) = refs[:count], refs[-2:]
    group, slab = lax.axis_index("groups"), lax.axis_index("slab")
    copies = []
    for index, in_ref in enumerate(in_refs):
        strip, away = divmod(index, 2)
        width = in_ref.shape[1]
        start = (1 - group if away else group) * total + columns[strip][0] + (1 - slab if columns[strip][1] else slab) * width
        at = pl.ds(pl.multiple_of(start, LANES), width)
        copies.append(pltpu.make_async_copy(in_ref, out_ref.at[:, at], done.at[index]))
    run_copies(copies)


def place(blocks, out, columns, total, model_width):
    rows = blocks[0].shape[0]
    held = [] if out is None else [out]
    return pl.pallas_call(
        functools.partial(place_kernel, len(blocks), columns, total),
        out_shape=jax.ShapeDtypeStruct((rows, model_width), jnp.bfloat16),
        in_specs=[IN_VMEM] * len(blocks) + [ANYWHERE] * len(held),
        out_specs=ANYWHERE,
        scratch_shapes=[pltpu.SemaphoreType.DMA((len(blocks),))],
        input_output_aliases={len(blocks): 0} if held else {},
        compiler_params=pltpu.CompilerParams(vmem_limit_bytes=4 * MIB),
        cost_estimate=pl.CostEstimate(flops=0, bytes_accessed=4 * sum(block.size for block in blocks), transcendentals=0),
        name="place",
    )(*blocks, *held)


def hop_order(pieces, turns):
    order = []
    for piece in range(pieces):
        hops = [(piece, strip, turn) for turn in range(1, turns[0] + 1) for strip in range(2) if turn <= turns[strip]]
        order = order[:-1] + hops[:1] + order[-1:] + hops[1:] if order else hops
    return order


def on_device(queries, key_value, keep, windows, gate, out_weight):
    frames_here, spots, features = queries.shape[1:]
    model_width = gate.shape[1]
    rows = frames_here * spots
    slabs = lax.axis_size("slab")
    total = model_width // lax.axis_size("groups")
    widths = piece_widths(total)

    count = lax.axis_size("owner")
    order = ring_order(count)
    spot_of = [order.index(owner) for owner in range(count)]
    ring = [
        (owner * slabs + slab, order[(spot_of[owner] + step) % count] * slabs + slab)
        for owner in range(count)
        for slab, step in enumerate((1, -1))
    ]
    turns = (count // 2, (count - 1) // 2)
    hops = hop_order(len(widths), turns)

    firsts = [2 * sum(widths[:piece]) for piece in range(len(widths))]
    held, arrived, crossed, edges = {}, [], {}, []
    for piece, width in enumerate(widths):
        own_strips, border = cut(out_weight, key_value, width, firsts[piece], total, piece == 0)
        edges = border or edges
        for strip, own in enumerate(own_strips):
            held[piece, strip, 0] = own

    def hop(slot, *others):
        if slot >= len(hops):
            return
        piece, strip, turn = hops[slot]
        waits = list(others)
        if slot >= FLIGHT:
            waits.append(arrived[slot - FLIGHT])
        if slot > 2 * FLIGHT:
            waits.append(crossed[hops[slot - 2 * FLIGHT - 1]])
        value = held[piece, strip, turn - 1]
        if waits:
            value = after(value, *waits)
        value = lax.ppermute(value, ("owner", "slab"), ring)
        held[hops[slot]] = value
        arrived.append(value)

    def cross(slot, *others):
        value = arrived[slot]
        crossed[hops[slot]] = swap(after(value, *others) if others else value, ("slab",))

    first_done = max(slot for slot, at in enumerate(hops) if at[0] == 0) if hops else 0
    halos = [swap(edge, ("slab",)) for edge in edges]
    for slot in range(FLIGHT):
        hop(slot)

    query_rows = queries.reshape(rows, features)
    key_value_rows = key_value.reshape(2, rows, features)
    waits, attended = {FLIGHT + 2: [held[piece, 0, 0] for piece in range(1, len(widths))]}, None
    for part in range(PARTS):
        attended = attend(query_rows, key_value_rows, halos[part], windows, spots, part, attended)
    a_blocks = (attended, swap(attended, ("groups",)))
    near_gate = scale_gate(after(keep, attended), gate)
    gates = (near_gate, swap(near_gate, ("groups",)))
    waits.setdefault(FLIGHT, []).append(attended)
    waits.setdefault(first_done, []).append(a_blocks[1])

    arranged = arrange(*a_blocks, count)

    def project_strip(piece, strip, *others):
        chunks, sources = [], []
        for turn in range(turns[strip] + 1):
            chunks.append(held[piece, strip, turn])
            sources.append((-turn, turn))
        for turn in range(1, turns[1 - strip] + 1):
            chunks.append(crossed[piece, 1 - strip, turn])
            sources.append((turn, -turn))
        table = np.zeros((slabs, count, len(chunks)), np.int32)
        for slab in range(slabs):
            for owner in range(count):
                table[slab, owner] = [order[(spot_of[owner] + source[slab]) % count] for source in sources]
        if others:
            chunks[0] = after(chunks[0], *others)
        own, away = project(jnp.asarray(table), arranged, chunks, gates, strip, firsts[piece], total)
        return [own, swap(away, ("groups",))]

    results, needs = {}, {}
    if first_done >= 2 and first_done + 1 < len(hops):
        needs[first_done - 2] = [first_done - 1, gates[1], arranged]
    for slot in range(FLIGHT, len(hops)):
        strip = slot - first_done - 3
        if 0 <= strip < 2:
            results[0, strip] = project_strip(0, strip, *(arrived[first_done + 1 : first_done + 2] if strip else []))
            waits.setdefault(slot, []).append(results[0, strip][0])
            if strip:
                needs[len(hops) - 2] = [results[0, strip][1]]
            else:
                needs[first_done + 1] = [results[0, strip][0]]
                waits.setdefault(len(hops) - 2, []).append(results[0, strip][1])
        others = needs.get(slot - FLIGHT, [])
        cross(slot - FLIGHT, *(arrived[other] if isinstance(other, int) else other for other in others))
        hop(slot, *waits.get(slot, []))
    for slot in range(max(len(hops) - FLIGHT, 0), len(hops)):
        cross(slot, *needs.get(slot, []))
    for piece in range(len(widths)):
        for strip in range(2):
            if (piece, strip) not in results:
                results[piece, strip] = project_strip(piece, strip)
    out = None
    last = (len(widths) - 1, 1)
    for batch in ([key for key in results if key != last], [last]):
        blocks = [block for key in batch for block in results[key]]
        out = place(blocks, out, [(firsts[piece], strip) for piece, strip in batch], total, model_width)
    return out.reshape((1, frames_here, spots, model_width))


def solution(mesh):
    placed = (
        P(("groups", "owner"), "slab", None, None),
        P(None, ("groups", "owner"), "slab", None, None),
        P("groups"),
        P("groups", None),
        P("groups", None),
        P("owner", None),
    )
    return jax.shard_map(
        on_device,
        mesh=mesh,
        in_specs=placed,
        out_specs=P(("groups", "owner"), "slab", None, None),
        check_vma=False,
    )
```

```python
import functools
import math

import jax
import jax.numpy as jnp
import numpy as np
from jax import lax
from jax.experimental import pallas as pl
from jax.experimental.pallas import tpu as pltpu
from jax.sharding import PartitionSpec as P

HEAD_DIM = 128
WB = 14
HALO = 1
LANES = 128
NEG_LARGE = -1e30
PARTS = 2
FLIGHT = 2
MIB = 1024 * 1024
ANYWHERE = pl.BlockSpec(memory_space=pl.ANY)
IN_HBM = pl.BlockSpec(memory_space=pltpu.HBM)
IN_VMEM = pl.BlockSpec(memory_space=pltpu.VMEM)
IN_SMEM = pl.BlockSpec(memory_space=pltpu.SMEM)


def ring_order(count):
    width = max(w for w in range(1, count + 1) if count % w == 0 and w * w <= count)
    height = count // width
    if width == 1 or height % 2:
        return list(range(count))
    order = []
    for row in range(height):
        columns = range(1, width) if row % 2 == 0 else range(width - 1, 0, -1)
        order += [row * width + column for column in columns]
    return order + [row * width for row in range(height - 1, -1, -1)]


def piece_widths(half_width):
    tiles = half_width // (2 * LANES)
    late = 3 * tiles // 10
    return [count * LANES for count in (tiles - late, late) if count]


def swap(value, axes):
    count = math.prod(lax.axis_size(axis) for axis in axes)
    return lax.ppermute(value, axes, [(i, count - 1 - i) for i in range(count)])


def after(value, *others):
    return lax.optimization_barrier((value,) + others)[0]


def run_copies(copies):
    for copy in copies:
        copy.start()
    for copy in copies:
        copy.wait()


def cut_kernel(first, total, with_border, weight_ref, key_value_ref, *refs):
    out_refs, done = refs[:-1], refs[-1]
    slab = lax.axis_index("slab")
    width = out_refs[0].shape[1]
    sources = []
    for strip in range(2):
        column = lax.axis_index("groups") * total + first + (1 - slab if strip else slab) * width
        sources.append(weight_ref.at[:, pl.ds(pl.multiple_of(column, LANES), width)])
    if with_border:
        frames_here = key_value_ref.shape[2]
        frame = jnp.where(slab == 0, frames_here - HALO, 0)
        width = out_refs[-1].shape[3]
        for part in range(PARTS):
            sources.append(key_value_ref.at[:, 0, pl.ds(frame, HALO), :, part * width : (part + 1) * width])
    run_copies([pltpu.make_async_copy(s, t, done.at[i]) for i, (s, t) in enumerate(zip(sources, out_refs))])


def cut(out_weight, key_value, width, first, total, with_border):
    depth = out_weight.shape[0]
    kinds, _, _, spots, features = key_value.shape
    shapes = [(depth, width)] * 2
    shapes += [(kinds, HALO, spots, features // PARTS)] * PARTS if with_border else []
    out_weight = pltpu.with_memory_space_constraint(out_weight, pltpu.HBM)
    key_value = pltpu.with_memory_space_constraint(key_value, pltpu.HBM)
    outs = pl.pallas_call(
        functools.partial(cut_kernel, first, total, with_border),
        out_shape=[jax.ShapeDtypeStruct(shape, jnp.bfloat16) for shape in shapes],
        in_specs=[IN_HBM] * 2,
        out_specs=[IN_VMEM] * len(shapes),
        scratch_shapes=[pltpu.SemaphoreType.DMA((len(shapes),))],
        compiler_params=pltpu.CompilerParams(vmem_limit_bytes=4 * MIB),
        cost_estimate=pl.CostEstimate(flops=0, bytes_accessed=8 * depth * width, transcendentals=0),
        name="cut",
    )(out_weight, key_value)
    return outs[:2], [edge.reshape(kinds, HALO * spots, features // PARTS) for edge in outs[2:]]


def scale_kernel(keep_ref, gate_ref, out_ref):
    owner = lax.axis_index("owner")
    factor = jnp.where(owner % 2 == 1, keep_ref[owner // 2], 1).astype(jnp.float32)
    out_ref[...] = gate_ref[pl.ds(owner // 2, 1), :] * factor


def scale_gate(keep, gate):
    return pl.pallas_call(
        scale_kernel,
        out_shape=jax.ShapeDtypeStruct((1, gate.shape[1]), jnp.float32),
        in_specs=[IN_SMEM, IN_VMEM],
        out_specs=IN_VMEM,
        compiler_params=pltpu.CompilerParams(vmem_limit_bytes=MIB),
        name="scale_gate",
    )(keep, gate)


def token_place(count, dim, spots, first_frame):
    shape = (count, 1) if dim == 0 else (1, count)
    token = lax.broadcasted_iota(jnp.int32, shape, dim).astype(jnp.float32)
    frame = jnp.floor((token + 0.5) * (1.0 / spots))
    spot = token - frame * spots
    row = jnp.floor((spot + 0.5) * (1.0 / WB))
    return frame + first_frame, row, spot - row * WB


def attend_kernel(spots, windows_ref, q_ref, k_ref, v_ref, k_halo_ref, v_halo_ref, *refs):
    out_ref, bias = refs[-2:]
    rows = q_ref.shape[0]
    halo_rows = k_halo_ref.shape[0]
    keys = bias.shape[1]
    frames_here = rows // spots

    @pl.when(pl.program_id(0) == 0)
    def _():
        request = lax.axis_index("owner") // 2
        halo_frame = jnp.where(lax.axis_index("slab") == 0, 0, -HALO - frames_here).astype(jnp.float32)
        query = token_place(rows, 0, spots, 0.0)
        key = token_place(keys, 1, spots, 0.0)
        index = lax.broadcasted_iota(jnp.int32, (1, keys), 1)
        frame = jnp.where(index < rows, key[0], key[0] + halo_frame)
        frame = jnp.where(index < rows + halo_rows, frame, -NEG_LARGE)
        allowed = None
        for part, place in enumerate((frame, key[1], key[2])):
            near = jnp.abs(query[part] - place) <= windows_ref[request, part].astype(jnp.float32)
            allowed = near if allowed is None else allowed & near
        bias[...] = jnp.where(allowed, 0.0, NEG_LARGE)

    scale = math.log2(math.e) / math.sqrt(HEAD_DIM)
    pad = jnp.zeros((keys - rows - halo_rows, HEAD_DIM), jnp.bfloat16)
    ones = jnp.ones((keys, HEAD_DIM), jnp.bfloat16)
    for head in range(q_ref.shape[1] // HEAD_DIM):
        at = slice(head * HEAD_DIM, (head + 1) * HEAD_DIM)
        key = jnp.concatenate([k_ref[:, at], k_halo_ref[:, at], pad], axis=0)
        value = jnp.concatenate([v_ref[:, at], v_halo_ref[:, at], pad], axis=0)
        value = jnp.concatenate([value, ones], axis=1)
        score = lax.dot_general(q_ref[:, at], key, (((1,), (1,)), ((), ())), preferred_element_type=jnp.float32)
        score = score * scale + bias[...]
        weight = jnp.exp2(score - jnp.max(score, axis=1, keepdims=True)).astype(jnp.bfloat16)
        mixture = jnp.dot(weight, value, preferred_element_type=jnp.float32)
        out_ref[:, at] = (mixture[:, :HEAD_DIM] / mixture[:, HEAD_DIM:]).astype(jnp.bfloat16)


def attend(query_rows, key_value_rows, halo, windows, spots, part, attended):
    before = [] if attended is None else [attended]
    rows, features = query_rows.shape
    query_rows = pltpu.with_memory_space_constraint(query_rows, pltpu.HBM)
    width = features // PARTS
    heads = width // HEAD_DIM
    steps = 2 if heads % 2 == 0 else 1
    block = width // steps
    halo_rows = halo.shape[1]
    first = part * steps
    keys = pl.cdiv(rows + halo_rows, LANES) * LANES
    return pl.pallas_call(
        functools.partial(attend_kernel, spots),
        grid=(steps,),
        out_shape=jax.ShapeDtypeStruct((rows, features), jnp.bfloat16),
        in_specs=[
            IN_SMEM,
            pl.BlockSpec((rows, block), lambda i: (0, first + i)),
            pl.BlockSpec((None, rows, block), lambda i: (0, 0, first + i)),
            pl.BlockSpec((None, rows, block), lambda i: (1, 0, first + i)),
            pl.BlockSpec((None, halo_rows, block), lambda i: (0, 0, i)),
            pl.BlockSpec((None, halo_rows, block), lambda i: (1, 0, i)),
        ]
        + [ANYWHERE] * len(before),
        out_specs=pl.BlockSpec((rows, block), lambda i: (0, first + i)),
        input_output_aliases={6: 0} if before else {},
        scratch_shapes=[pltpu.VMEM((rows, keys), jnp.float32)],
        compiler_params=pltpu.CompilerParams(vmem_limit_bytes=10 * MIB),
        cost_estimate=pl.CostEstimate(
            flops=32 * rows * keys * width, bytes_accessed=2 * width * (2 * rows + 2 * keys), transcendentals=heads * rows * keys
        ),
        name="attend",
    )(windows, query_rows, key_value_rows, key_value_rows, halo, halo, *before)


def arrange_kernel(near_ref, far_ref, out_ref):
    rows = near_ref.shape[0]
    depth = out_ref.shape[2]
    for owner in range(out_ref.shape[0]):
        at = slice(owner * depth, (owner + 1) * depth)
        out_ref[owner, :rows] = near_ref[:, at]
        out_ref[owner, rows:] = far_ref[:, at]


def arrange(near, far, count):
    rows, features = near.shape
    return pl.pallas_call(
        arrange_kernel,
        out_shape=jax.ShapeDtypeStruct((count, 2 * rows, features // count), near.dtype),
        in_specs=[IN_VMEM] * 2,
        out_specs=IN_VMEM,
        compiler_params=pltpu.CompilerParams(vmem_limit_bytes=8 * MIB),
        cost_estimate=pl.CostEstimate(flops=0, bytes_accessed=8 * near.size, transcendentals=0),
        name="arrange",
    )(near, far)


def project_kernel(strip, column, total, tables_ref, rows_ref, *refs):
    count = tables_ref.shape[2]
    w_refs, gate_refs, out_refs = refs[:count], refs[count : count + 2], refs[count + 2 :]
    owner, slab = lax.axis_index("owner"), lax.axis_index("slab")
    rows, width = out_refs[0].shape
    sources = [tables_ref[slab, owner, index] for index in range(count)]
    place = lax.axis_index("groups") * total + column + (1 - slab if strip else slab) * width
    for first in range(0, width, 2 * LANES):
        tile = min(2 * LANES, width - first)
        product = None
        for source, w_ref in zip(sources, w_refs):
            term = jnp.dot(rows_ref[source], w_ref[:, first : first + tile], preferred_element_type=jnp.float32)
            product = term if product is None else product + term
        here = pl.ds(pl.multiple_of(place + first, LANES), tile)
        for block in range(2):
            gate = gate_refs[block][:, here]
            result = product[block * rows : (block + 1) * rows] * gate
            out_refs[block][:, first : first + tile] = result.astype(jnp.bfloat16)


def project(table, arranged, chunks, gates, strip, column, total):
    count, rows, depth = arranged.shape
    width = chunks[0].shape[1]
    return pl.pallas_call(
        functools.partial(project_kernel, strip, column, total),
        out_shape=[jax.ShapeDtypeStruct((rows // 2, width), jnp.bfloat16)] * 2,
        in_specs=[IN_SMEM] + [IN_VMEM] * (1 + count + 2),
        out_specs=[IN_VMEM] * 2,
        compiler_params=pltpu.CompilerParams(vmem_limit_bytes=16 * MIB),
        cost_estimate=pl.CostEstimate(
            flops=3 * rows * width * depth * count,
            bytes_accessed=2 * (rows * (depth * count + width) + count * depth * width),
            transcendentals=0,
        ),
        name="project",
    )(table, arranged, *chunks, *gates)


def place_kernel(count, columns, total, *refs):
    in_refs, (out_ref, done) = refs[:count], refs[-2:]
    group, slab = lax.axis_index("groups"), lax.axis_index("slab")
    copies = []
    for index, in_ref in enumerate(in_refs):
        strip, away = divmod(index, 2)
        width = in_ref.shape[1]
        start = (1 - group if away else group) * total + columns[strip][0] + (1 - slab if columns[strip][1] else slab) * width
        at = pl.ds(pl.multiple_of(start, LANES), width)
        copies.append(pltpu.make_async_copy(in_ref, out_ref.at[:, at], done.at[index]))
    run_copies(copies)


def place(blocks, out, columns, total, model_width):
    rows = blocks[0].shape[0]
    held = [] if out is None else [out]
    return pl.pallas_call(
        functools.partial(place_kernel, len(blocks), columns, total),
        out_shape=jax.ShapeDtypeStruct((rows, model_width), jnp.bfloat16),
        in_specs=[IN_VMEM] * len(blocks) + [ANYWHERE] * len(held),
        out_specs=ANYWHERE,
        scratch_shapes=[pltpu.SemaphoreType.DMA((len(blocks),))],
        input_output_aliases={len(blocks): 0} if held else {},
        compiler_params=pltpu.CompilerParams(vmem_limit_bytes=4 * MIB),
        cost_estimate=pl.CostEstimate(flops=0, bytes_accessed=4 * sum(block.size for block in blocks), transcendentals=0),
        name="place",
    )(*blocks, *held)


def hop_order(pieces, turns):
    order = []
    for piece in range(pieces):
        hops = [(piece, strip, turn) for turn in range(1, turns[0] + 1) for strip in range(2) if turn <= turns[strip]]
        order = order[:-1] + hops[:1] + order[-1:] + hops[1:] if order else hops
    return order


def on_device(queries, key_value, keep, windows, gate, out_weight):
    frames_here, spots, features = queries.shape[1:]
    model_width = gate.shape[1]
    rows = frames_here * spots
    slabs = lax.axis_size("slab")
    total = model_width // lax.axis_size("groups")
    widths = piece_widths(total)

    count = lax.axis_size("owner")
    order = ring_order(count)
    spot_of = [order.index(owner) for owner in range(count)]
    ring = [
        (owner * slabs + slab, order[(spot_of[owner] + step) % count] * slabs + slab)
        for owner in range(count)
        for slab, step in enumerate((1, -1))
    ]
    turns = (count // 2, (count - 1) // 2)
    hops = hop_order(len(widths), turns)

    firsts = [2 * sum(widths[:piece]) for piece in range(len(widths))]
    held, arrived, crossed, edges = {}, [], {}, []
    for piece, width in enumerate(widths):
        own_strips, border = cut(out_weight, key_value, width, firsts[piece], total, piece == 0)
        edges = border or edges
        for strip, own in enumerate(own_strips):
            held[piece, strip, 0] = own

    def hop(slot, *others):
        if slot >= len(hops):
            return
        piece, strip, turn = hops[slot]
        waits = list(others)
        if slot >= FLIGHT:
            waits.append(arrived[slot - FLIGHT])
        if slot > 2 * FLIGHT:
            waits.append(crossed[hops[slot - 2 * FLIGHT - 1]])
        value = held[piece, strip, turn - 1]
        if waits:
            value = after(value, *waits)
        value = lax.ppermute(value, ("owner", "slab"), ring)
        held[hops[slot]] = value
        arrived.append(value)

    def cross(slot, *others):
        value = arrived[slot]
        crossed[hops[slot]] = swap(after(value, *others) if others else value, ("slab",))

    first_done = max(slot for slot, at in enumerate(hops) if at[0] == 0) if hops else 0
    halos = [swap(edge, ("slab",)) for edge in edges]
    for slot in range(FLIGHT):
        hop(slot)

    query_rows = queries.reshape(rows, features)
    key_value_rows = key_value.reshape(2, rows, features)
    waits, attended = {FLIGHT + 2: [held[piece, 0, 0] for piece in range(1, len(widths))]}, None
    for part in range(PARTS):
        attended = attend(query_rows, key_value_rows, halos[part], windows, spots, part, attended)
    a_blocks = (attended, swap(attended, ("groups",)))
    near_gate = scale_gate(after(keep, attended), gate)
    gates = (near_gate, swap(near_gate, ("groups",)))
    waits.setdefault(FLIGHT, []).append(attended)
    waits.setdefault(first_done - 1, []).append(a_blocks[1])

    arranged = arrange(*a_blocks, count)

    def project_strip(piece, strip, *others):
        chunks, sources = [], []
        for turn in range(turns[strip] + 1):
            chunks.append(held[piece, strip, turn])
            sources.append((-turn, turn))
        for turn in range(1, turns[1 - strip] + 1):
            chunks.append(crossed[piece, 1 - strip, turn])
            sources.append((turn, -turn))
        table = np.zeros((slabs, count, len(chunks)), np.int32)
        for slab in range(slabs):
            for owner in range(count):
                table[slab, owner] = [order[(spot_of[owner] + source[slab]) % count] for source in sources]
        if others:
            chunks[0] = after(chunks[0], *others)
        own, away = project(jnp.asarray(table), arranged, chunks, gates, strip, firsts[piece], total)
        return [own, swap(away, ("groups",))]

    results, needs = {}, {}
    if first_done >= 2 and first_done + 1 < len(hops):
        needs[first_done - 2] = [first_done - 1, gates[1], arranged]
    for slot in range(FLIGHT, len(hops)):
        strip = slot - first_done - 3
        if 0 <= strip < 2:
            results[0, strip] = project_strip(0, strip, *(arrived[first_done + 1 : first_done + 2] if strip else []))
            waits.setdefault(slot, []).append(results[0, strip][0])
            if strip:
                needs[len(hops) - 2] = [results[0, strip][1]]
            else:
                needs[first_done + 1] = [results[0, strip][0]]
                waits.setdefault(len(hops) - 1, []).append(results[0, strip][1])
        others = needs.get(slot - FLIGHT, [])
        cross(slot - FLIGHT, *(arrived[other] if isinstance(other, int) else other for other in others))
        hop(slot, *waits.get(slot, []))
    for slot in range(max(len(hops) - FLIGHT, 0), len(hops)):
        cross(slot, *needs.get(slot, []))
    for piece in range(len(widths)):
        for strip in range(2):
            if (piece, strip) not in results:
                results[piece, strip] = project_strip(piece, strip)
    out = None
    last = (len(widths) - 1, 1)
    for batch in ([key for key in results if key != last], [last]):
        blocks = [block for key in batch for block in results[key]]
        out = place(blocks, out, [(firsts[piece], strip) for piece, strip in batch], total, model_width)
    return out.reshape((1, frames_here, spots, model_width))


def solution(mesh):
    placed = (
        P(("groups", "owner"), "slab", None, None),
        P(None, ("groups", "owner"), "slab", None, None),
        P("groups"),
        P("groups", None),
        P("groups", None),
        P("owner", None),
    )
    return jax.shard_map(
        on_device,
        mesh=mesh,
        in_specs=placed,
        out_specs=P(("groups", "owner"), "slab", None, None),
        check_vma=False,
    )
```

```python
import functools
import math

import jax
import jax.numpy as jnp
import numpy as np
from jax import lax
from jax.experimental import pallas as pl
from jax.experimental.pallas import tpu as pltpu
from jax.sharding import PartitionSpec as P

HEAD_DIM = 128
WB = 14
HALO = 1
LANES = 128
NEG_LARGE = -1e30
PARTS = 2
FLIGHT = 2
MIB = 1024 * 1024
ANYWHERE = pl.BlockSpec(memory_space=pl.ANY)
IN_HBM = pl.BlockSpec(memory_space=pltpu.HBM)
IN_VMEM = pl.BlockSpec(memory_space=pltpu.VMEM)
IN_SMEM = pl.BlockSpec(memory_space=pltpu.SMEM)


def ring_order(count):
    width = max(w for w in range(1, count + 1) if count % w == 0 and w * w <= count)
    height = count // width
    if width == 1 or height % 2:
        return list(range(count))
    order = []
    for row in range(height):
        columns = range(1, width) if row % 2 == 0 else range(width - 1, 0, -1)
        order += [row * width + column for column in columns]
    return order + [row * width for row in range(height - 1, -1, -1)]


def piece_widths(half_width):
    tiles = half_width // (2 * LANES)
    late = 2 * tiles // 5
    return [count * LANES for count in (tiles - late, late) if count]


def swap(value, axes):
    count = math.prod(lax.axis_size(axis) for axis in axes)
    return lax.ppermute(value, axes, [(i, count - 1 - i) for i in range(count)])


def after(value, *others):
    return lax.optimization_barrier((value,) + others)[0]


def run_copies(copies):
    for copy in copies:
        copy.start()
    for copy in copies:
        copy.wait()


def cut_kernel(first, total, with_border, weight_ref, key_value_ref, *refs):
    out_refs, done = refs[:-1], refs[-1]
    slab = lax.axis_index("slab")
    width = out_refs[0].shape[1]
    sources = []
    for strip in range(2):
        column = lax.axis_index("groups") * total + first + (1 - slab if strip else slab) * width
        sources.append(weight_ref.at[:, pl.ds(pl.multiple_of(column, LANES), width)])
    if with_border:
        frames_here = key_value_ref.shape[2]
        frame = jnp.where(slab == 0, frames_here - HALO, 0)
        width = out_refs[-1].shape[3]
        for part in range(PARTS):
            sources.append(key_value_ref.at[:, 0, pl.ds(frame, HALO), :, part * width : (part + 1) * width])
    run_copies([pltpu.make_async_copy(s, t, done.at[i]) for i, (s, t) in enumerate(zip(sources, out_refs))])


def cut(out_weight, key_value, width, first, total, with_border):
    depth = out_weight.shape[0]
    kinds, _, _, spots, features = key_value.shape
    shapes = [(depth, width)] * 2
    shapes += [(kinds, HALO, spots, features // PARTS)] * PARTS if with_border else []
    out_weight = pltpu.with_memory_space_constraint(out_weight, pltpu.HBM)
    key_value = pltpu.with_memory_space_constraint(key_value, pltpu.HBM)
    outs = pl.pallas_call(
        functools.partial(cut_kernel, first, total, with_border),
        out_shape=[jax.ShapeDtypeStruct(shape, jnp.bfloat16) for shape in shapes],
        in_specs=[IN_HBM] * 2,
        out_specs=[IN_VMEM] * len(shapes),
        scratch_shapes=[pltpu.SemaphoreType.DMA((len(shapes),))],
        compiler_params=pltpu.CompilerParams(vmem_limit_bytes=4 * MIB),
        cost_estimate=pl.CostEstimate(flops=0, bytes_accessed=8 * depth * width, transcendentals=0),
        name="cut",
    )(out_weight, key_value)
    return outs[:2], [edge.reshape(kinds, HALO * spots, features // PARTS) for edge in outs[2:]]


def scale_kernel(keep_ref, gate_ref, out_ref):
    owner = lax.axis_index("owner")
    factor = jnp.where(owner % 2 == 1, keep_ref[owner // 2], 1).astype(jnp.float32)
    out_ref[...] = gate_ref[pl.ds(owner // 2, 1), :] * factor


def scale_gate(keep, gate):
    return pl.pallas_call(
        scale_kernel,
        out_shape=jax.ShapeDtypeStruct((1, gate.shape[1]), jnp.float32),
        in_specs=[IN_SMEM, IN_VMEM],
        out_specs=IN_VMEM,
        compiler_params=pltpu.CompilerParams(vmem_limit_bytes=MIB),
        name="scale_gate",
    )(keep, gate)


def token_place(count, dim, spots, first_frame):
    shape = (count, 1) if dim == 0 else (1, count)
    token = lax.broadcasted_iota(jnp.int32, shape, dim).astype(jnp.float32)
    frame = jnp.floor((token + 0.5) * (1.0 / spots))
    spot = token - frame * spots
    row = jnp.floor((spot + 0.5) * (1.0 / WB))
    return frame + first_frame, row, spot - row * WB


def attend_kernel(spots, windows_ref, q_ref, k_ref, v_ref, k_halo_ref, v_halo_ref, *refs):
    out_ref, bias = refs[-2:]
    rows = q_ref.shape[0]
    halo_rows = k_halo_ref.shape[0]
    keys = bias.shape[1]
    frames_here = rows // spots

    @pl.when(pl.program_id(0) == 0)
    def _():
        request = lax.axis_index("owner") // 2
        halo_frame = jnp.where(lax.axis_index("slab") == 0, 0, -HALO - frames_here).astype(jnp.float32)
        query = token_place(rows, 0, spots, 0.0)
        key = token_place(keys, 1, spots, 0.0)
        index = lax.broadcasted_iota(jnp.int32, (1, keys), 1)
        frame = jnp.where(index < rows, key[0], key[0] + halo_frame)
        frame = jnp.where(index < rows + halo_rows, frame, -NEG_LARGE)
        allowed = None
        for part, place in enumerate((frame, key[1], key[2])):
            near = jnp.abs(query[part] - place) <= windows_ref[request, part].astype(jnp.float32)
            allowed = near if allowed is None else allowed & near
        bias[...] = jnp.where(allowed, 0.0, NEG_LARGE)

    scale = math.log2(math.e) / math.sqrt(HEAD_DIM)
    pad = jnp.zeros((keys - rows - halo_rows, HEAD_DIM), jnp.bfloat16)
    ones = jnp.ones((keys, HEAD_DIM), jnp.bfloat16)
    for head in range(q_ref.shape[1] // HEAD_DIM):
        at = slice(head * HEAD_DIM, (head + 1) * HEAD_DIM)
        key = jnp.concatenate([k_ref[:, at], k_halo_ref[:, at], pad], axis=0)
        value = jnp.concatenate([v_ref[:, at], v_halo_ref[:, at], pad], axis=0)
        value = jnp.concatenate([value, ones], axis=1)
        score = lax.dot_general(q_ref[:, at], key, (((1,), (1,)), ((), ())), preferred_element_type=jnp.float32)
        score = score * scale + bias[...]
        weight = jnp.exp2(score - jnp.max(score, axis=1, keepdims=True)).astype(jnp.bfloat16)
        mixture = jnp.dot(weight, value, preferred_element_type=jnp.float32)
        out_ref[:, at] = (mixture[:, :HEAD_DIM] / mixture[:, HEAD_DIM:]).astype(jnp.bfloat16)


def attend(query_rows, key_value_rows, halo, windows, spots, part, attended):
    before = [] if attended is None else [attended]
    rows, features = query_rows.shape
    query_rows = pltpu.with_memory_space_constraint(query_rows, pltpu.HBM)
    width = features // PARTS
    heads = width // HEAD_DIM
    steps = 2 if heads % 2 == 0 else 1
    block = width // steps
    halo_rows = halo.shape[1]
    first = part * steps
    keys = pl.cdiv(rows + halo_rows, LANES) * LANES
    return pl.pallas_call(
        functools.partial(attend_kernel, spots),
        grid=(steps,),
        out_shape=jax.ShapeDtypeStruct((rows, features), jnp.bfloat16),
        in_specs=[
            IN_SMEM,
            pl.BlockSpec((rows, block), lambda i: (0, first + i)),
            pl.BlockSpec((None, rows, block), lambda i: (0, 0, first + i)),
            pl.BlockSpec((None, rows, block), lambda i: (1, 0, first + i)),
            pl.BlockSpec((None, halo_rows, block), lambda i: (0, 0, i)),
            pl.BlockSpec((None, halo_rows, block), lambda i: (1, 0, i)),
        ]
        + [ANYWHERE] * len(before),
        out_specs=pl.BlockSpec((rows, block), lambda i: (0, first + i)),
        input_output_aliases={6: 0} if before else {},
        scratch_shapes=[pltpu.VMEM((rows, keys), jnp.float32)],
        compiler_params=pltpu.CompilerParams(vmem_limit_bytes=10 * MIB),
        cost_estimate=pl.CostEstimate(
            flops=32 * rows * keys * width, bytes_accessed=2 * width * (2 * rows + 2 * keys), transcendentals=heads * rows * keys
        ),
        name="attend",
    )(windows, query_rows, key_value_rows, key_value_rows, halo, halo, *before)


def arrange_kernel(near_ref, far_ref, out_ref):
    rows = near_ref.shape[0]
    depth = out_ref.shape[2]
    for owner in range(out_ref.shape[0]):
        at = slice(owner * depth, (owner + 1) * depth)
        out_ref[owner, :rows] = near_ref[:, at]
        out_ref[owner, rows:] = far_ref[:, at]


def arrange(near, far, count):
    rows, features = near.shape
    return pl.pallas_call(
        arrange_kernel,
        out_shape=jax.ShapeDtypeStruct((count, 2 * rows, features // count), near.dtype),
        in_specs=[IN_VMEM] * 2,
        out_specs=IN_VMEM,
        compiler_params=pltpu.CompilerParams(vmem_limit_bytes=8 * MIB),
        cost_estimate=pl.CostEstimate(flops=0, bytes_accessed=8 * near.size, transcendentals=0),
        name="arrange",
    )(near, far)


def project_kernel(strip, column, total, tables_ref, rows_ref, *refs):
    count = tables_ref.shape[2]
    w_refs, gate_refs, out_refs = refs[:count], refs[count : count + 2], refs[count + 2 :]
    owner, slab = lax.axis_index("owner"), lax.axis_index("slab")
    rows, width = out_refs[0].shape
    sources = [tables_ref[slab, owner, index] for index in range(count)]
    place = lax.axis_index("groups") * total + column + (1 - slab if strip else slab) * width
    for first in range(0, width, 2 * LANES):
        tile = min(2 * LANES, width - first)
        product = None
        for source, w_ref in zip(sources, w_refs):
            term = jnp.dot(rows_ref[source], w_ref[:, first : first + tile], preferred_element_type=jnp.float32)
            product = term if product is None else product + term
        here = pl.ds(pl.multiple_of(place + first, LANES), tile)
        for block in range(2):
            gate = gate_refs[block][:, here]
            result = product[block * rows : (block + 1) * rows] * gate
            out_refs[block][:, first : first + tile] = result.astype(jnp.bfloat16)


def project(table, arranged, chunks, gates, strip, column, total):
    count, rows, depth = arranged.shape
    width = chunks[0].shape[1]
    return pl.pallas_call(
        functools.partial(project_kernel, strip, column, total),
        out_shape=[jax.ShapeDtypeStruct((rows // 2, width), jnp.bfloat16)] * 2,
        in_specs=[IN_SMEM] + [IN_VMEM] * (1 + count + 2),
        out_specs=[IN_VMEM] * 2,
        compiler_params=pltpu.CompilerParams(vmem_limit_bytes=16 * MIB),
        cost_estimate=pl.CostEstimate(
            flops=3 * rows * width * depth * count,
            bytes_accessed=2 * (rows * (depth * count + width) + count * depth * width),
            transcendentals=0,
        ),
        name="project",
    )(table, arranged, *chunks, *gates)


def place_kernel(count, columns, total, *refs):
    in_refs, (out_ref, done) = refs[:count], refs[-2:]
    group, slab = lax.axis_index("groups"), lax.axis_index("slab")
    copies = []
    for index, in_ref in enumerate(in_refs):
        strip, away = divmod(index, 2)
        width = in_ref.shape[1]
        start = (1 - group if away else group) * total + columns[strip][0] + (1 - slab if columns[strip][1] else slab) * width
        at = pl.ds(pl.multiple_of(start, LANES), width)
        copies.append(pltpu.make_async_copy(in_ref, out_ref.at[:, at], done.at[index]))
    run_copies(copies)


def place(blocks, out, columns, total, model_width):
    rows = blocks[0].shape[0]
    held = [] if out is None else [out]
    return pl.pallas_call(
        functools.partial(place_kernel, len(blocks), columns, total),
        out_shape=jax.ShapeDtypeStruct((rows, model_width), jnp.bfloat16),
        in_specs=[IN_VMEM] * len(blocks) + [ANYWHERE] * len(held),
        out_specs=ANYWHERE,
        scratch_shapes=[pltpu.SemaphoreType.DMA((len(blocks),))],
        input_output_aliases={len(blocks): 0} if held else {},
        compiler_params=pltpu.CompilerParams(vmem_limit_bytes=4 * MIB),
        cost_estimate=pl.CostEstimate(flops=0, bytes_accessed=4 * sum(block.size for block in blocks), transcendentals=0),
        name="place",
    )(*blocks, *held)


def hop_order(pieces, turns):
    order = []
    for piece in range(pieces):
        hops = [(piece, strip, turn) for turn in range(1, turns[0] + 1) for strip in range(2) if turn <= turns[strip]]
        order = order[:-1] + hops[:1] + order[-1:] + hops[1:] if order else hops
    return order


def on_device(queries, key_value, keep, windows, gate, out_weight):
    frames_here, spots, features = queries.shape[1:]
    model_width = gate.shape[1]
    rows = frames_here * spots
    slabs = lax.axis_size("slab")
    total = model_width // lax.axis_size("groups")
    widths = piece_widths(total)

    count = lax.axis_size("owner")
    order = ring_order(count)
    spot_of = [order.index(owner) for owner in range(count)]
    ring = [
        (owner * slabs + slab, order[(spot_of[owner] + step) % count] * slabs + slab)
        for owner in range(count)
        for slab, step in enumerate((1, -1))
    ]
    turns = (count // 2, (count - 1) // 2)
    hops = hop_order(len(widths), turns)

    firsts = [2 * sum(widths[:piece]) for piece in range(len(widths))]
    held, arrived, crossed, edges = {}, [], {}, []
    for piece, width in enumerate(widths):
        own_strips, border = cut(out_weight, key_value, width, firsts[piece], total, piece == 0)
        edges = border or edges
        for strip, own in enumerate(own_strips):
            held[piece, strip, 0] = own

    def hop(slot, *others):
        if slot >= len(hops):
            return
        piece, strip, turn = hops[slot]
        waits = list(others)
        if slot >= FLIGHT:
            waits.append(arrived[slot - FLIGHT])
        if slot > 2 * FLIGHT:
            waits.append(crossed[hops[slot - 2 * FLIGHT - 1]])
        value = held[piece, strip, turn - 1]
        if waits:
            value = after(value, *waits)
        value = lax.ppermute(value, ("owner", "slab"), ring)
        held[hops[slot]] = value
        arrived.append(value)

    def cross(slot, *others):
        value = arrived[slot]
        crossed[hops[slot]] = swap(after(value, *others) if others else value, ("slab",))

    first_done = max(slot for slot, at in enumerate(hops) if at[0] == 0) if hops else 0
    halos = [swap(edge, ("slab",)) for edge in edges]
    for slot in range(FLIGHT):
        hop(slot)

    query_rows = queries.reshape(rows, features)
    key_value_rows = key_value.reshape(2, rows, features)
    waits, attended = {FLIGHT + 2: [held[piece, 0, 0] for piece in range(1, len(widths))]}, None
    for part in range(PARTS):
        attended = attend(query_rows, key_value_rows, halos[part], windows, spots, part, attended)
    a_blocks = (attended, swap(attended, ("groups",)))
    near_gate = scale_gate(after(keep, attended), gate)
    gates = (near_gate, swap(near_gate, ("groups",)))
    waits.setdefault(FLIGHT, []).append(attended)
    waits.setdefault(first_done, []).append(a_blocks[1])

    arranged = arrange(*a_blocks, count)

    def project_strip(piece, strip, *others):
        chunks, sources = [], []
        for turn in range(turns[strip] + 1):
            chunks.append(held[piece, strip, turn])
            sources.append((-turn, turn))
        for turn in range(1, turns[1 - strip] + 1):
            chunks.append(crossed[piece, 1 - strip, turn])
            sources.append((turn, -turn))
        table = np.zeros((slabs, count, len(chunks)), np.int32)
        for slab in range(slabs):
            for owner in range(count):
                table[slab, owner] = [order[(spot_of[owner] + source[slab]) % count] for source in sources]
        if others:
            chunks[0] = after(chunks[0], *others)
        own, away = project(jnp.asarray(table), arranged, chunks, gates, strip, firsts[piece], total)
        return [own, swap(away, ("groups",))]

    results, needs = {}, {}
    if first_done >= 2 and first_done + 1 < len(hops):
        needs[first_done - 2] = [first_done - 1, gates[1], arranged]
    for slot in range(FLIGHT, len(hops)):
        strip = {first_done + 3: 0, first_done + 5: 1}.get(slot)
        if strip is not None:
            results[0, strip] = project_strip(0, strip, *(arrived[first_done + 1 : first_done + 2] if strip else []))
            waits.setdefault(slot, []).append(results[0, strip][0])
            if strip:
                needs[len(hops) - 2] = [results[0, strip][1]]
                waits[slot].append(arrived[slot - 1])
            else:
                needs[first_done + 1] = [results[0, strip][0]]
                waits.setdefault(len(hops) - 1, []).append(results[0, strip][1])
        others = needs.get(slot - FLIGHT, [])
        cross(slot - FLIGHT, *(arrived[other] if isinstance(other, int) else other for other in others))
        hop(slot, *waits.get(slot, []))
    for slot in range(max(len(hops) - FLIGHT, 0), len(hops)):
        cross(slot, *needs.get(slot, []))
    for piece in range(len(widths)):
        for strip in range(2):
            if (piece, strip) not in results:
                results[piece, strip] = project_strip(piece, strip)
    out = None
    last = (len(widths) - 1, 1)
    for batch in ([key for key in results if key != last], [last]):
        blocks = [block for key in batch for block in results[key]]
        out = place(blocks, out, [(firsts[piece], strip) for piece, strip in batch], total, model_width)
    return out.reshape((1, frames_here, spots, model_width))


def solution(mesh):
    placed = (
        P(("groups", "owner"), "slab", None, None),
        P(None, ("groups", "owner"), "slab", None, None),
        P("groups"),
        P("groups", None),
        P("groups", None),
        P("owner", None),
    )
    return jax.shard_map(
        on_device,
        mesh=mesh,
        in_specs=placed,
        out_specs=P(("groups", "owner"), "slab", None, None),
        check_vma=False,
    )
```

```python
import functools
import math

import jax
import jax.numpy as jnp
import numpy as np
from jax import lax
from jax.experimental import pallas as pl
from jax.experimental.pallas import tpu as pltpu
from jax.sharding import PartitionSpec as P

HEAD_DIM = 128
WB = 14
HALO = 1
LANES = 128
NEG_LARGE = -1e30
PARTS = 2
FLIGHT = 2
MIB = 1024 * 1024
ANYWHERE = pl.BlockSpec(memory_space=pl.ANY)
IN_HBM = pl.BlockSpec(memory_space=pltpu.HBM)
IN_VMEM = pl.BlockSpec(memory_space=pltpu.VMEM)
IN_SMEM = pl.BlockSpec(memory_space=pltpu.SMEM)


def ring_order(count):
    width = max(w for w in range(1, count + 1) if count % w == 0 and w * w <= count)
    height = count // width
    if width == 1 or height % 2:
        return list(range(count))
    order = []
    for row in range(height):
        columns = range(1, width) if row % 2 == 0 else range(width - 1, 0, -1)
        order += [row * width + column for column in columns]
    return order + [row * width for row in range(height - 1, -1, -1)]


def piece_widths(half_width):
    tiles = half_width // (2 * LANES)
    late = 2 * tiles // 5
    return [count * LANES for count in (tiles - late, late) if count]


def swap(value, axes):
    count = math.prod(lax.axis_size(axis) for axis in axes)
    return lax.ppermute(value, axes, [(i, count - 1 - i) for i in range(count)])


def after(value, *others):
    return lax.optimization_barrier((value,) + others)[0]


def run_copies(copies):
    for copy in copies:
        copy.start()
    for copy in copies:
        copy.wait()


def cut_kernel(first, total, with_border, weight_ref, key_value_ref, *refs):
    out_refs, done = refs[:-1], refs[-1]
    slab = lax.axis_index("slab")
    width = out_refs[0].shape[1]
    sources = []
    for strip in range(2):
        column = lax.axis_index("groups") * total + first + (1 - slab if strip else slab) * width
        sources.append(weight_ref.at[:, pl.ds(pl.multiple_of(column, LANES), width)])
    if with_border:
        frames_here = key_value_ref.shape[2]
        frame = jnp.where(slab == 0, frames_here - HALO, 0)
        width = out_refs[-1].shape[3]
        for part in range(PARTS):
            sources.append(key_value_ref.at[:, 0, pl.ds(frame, HALO), :, part * width : (part + 1) * width])
    run_copies([pltpu.make_async_copy(s, t, done.at[i]) for i, (s, t) in enumerate(zip(sources, out_refs))])


def cut(out_weight, key_value, width, first, total, with_border):
    depth = out_weight.shape[0]
    kinds, _, _, spots, features = key_value.shape
    shapes = [(depth, width)] * 2
    shapes += [(kinds, HALO, spots, features // PARTS)] * PARTS if with_border else []
    out_weight = pltpu.with_memory_space_constraint(out_weight, pltpu.HBM)
    key_value = pltpu.with_memory_space_constraint(key_value, pltpu.HBM)
    outs = pl.pallas_call(
        functools.partial(cut_kernel, first, total, with_border),
        out_shape=[jax.ShapeDtypeStruct(shape, jnp.bfloat16) for shape in shapes],
        in_specs=[IN_HBM] * 2,
        out_specs=[IN_VMEM] * len(shapes),
        scratch_shapes=[pltpu.SemaphoreType.DMA((len(shapes),))],
        compiler_params=pltpu.CompilerParams(vmem_limit_bytes=4 * MIB),
        cost_estimate=pl.CostEstimate(flops=0, bytes_accessed=8 * depth * width, transcendentals=0),
        name="cut",
    )(out_weight, key_value)
    return outs[:2], [edge.reshape(kinds, HALO * spots, features // PARTS) for edge in outs[2:]]


def scale_kernel(keep_ref, gate_ref, out_ref):
    owner = lax.axis_index("owner")
    factor = jnp.where(owner % 2 == 1, keep_ref[owner // 2], 1).astype(jnp.float32)
    out_ref[...] = gate_ref[pl.ds(owner // 2, 1), :] * factor


def scale_gate(keep, gate):
    return pl.pallas_call(
        scale_kernel,
        out_shape=jax.ShapeDtypeStruct((1, gate.shape[1]), jnp.float32),
        in_specs=[IN_SMEM, IN_VMEM],
        out_specs=IN_VMEM,
        compiler_params=pltpu.CompilerParams(vmem_limit_bytes=MIB),
        name="scale_gate",
    )(keep, gate)


def token_place(count, dim, spots, first_frame):
    shape = (count, 1) if dim == 0 else (1, count)
    token = lax.broadcasted_iota(jnp.int32, shape, dim).astype(jnp.float32)
    frame = jnp.floor((token + 0.5) * (1.0 / spots))
    spot = token - frame * spots
    row = jnp.floor((spot + 0.5) * (1.0 / WB))
    return frame + first_frame, row, spot - row * WB


def attend_kernel(spots, windows_ref, q_ref, k_ref, v_ref, k_halo_ref, v_halo_ref, *refs):
    out_ref, bias = refs[-2:]
    rows = q_ref.shape[0]
    halo_rows = k_halo_ref.shape[0]
    keys = bias.shape[1]
    frames_here = rows // spots

    @pl.when(pl.program_id(0) == 0)
    def _():
        request = lax.axis_index("owner") // 2
        halo_frame = jnp.where(lax.axis_index("slab") == 0, 0, -HALO - frames_here).astype(jnp.float32)
        query = token_place(rows, 0, spots, 0.0)
        key = token_place(keys, 1, spots, 0.0)
        index = lax.broadcasted_iota(jnp.int32, (1, keys), 1)
        frame = jnp.where(index < rows, key[0], key[0] + halo_frame)
        frame = jnp.where(index < rows + halo_rows, frame, -NEG_LARGE)
        allowed = None
        for part, place in enumerate((frame, key[1], key[2])):
            near = jnp.abs(query[part] - place) <= windows_ref[request, part].astype(jnp.float32)
            allowed = near if allowed is None else allowed & near
        bias[...] = jnp.where(allowed, 0.0, NEG_LARGE)

    scale = math.log2(math.e) / math.sqrt(HEAD_DIM)
    pad = jnp.zeros((keys - rows - halo_rows, HEAD_DIM), jnp.bfloat16)
    ones = jnp.ones((keys, HEAD_DIM), jnp.bfloat16)
    for head in range(q_ref.shape[1] // HEAD_DIM):
        at = slice(head * HEAD_DIM, (head + 1) * HEAD_DIM)
        key = jnp.concatenate([k_ref[:, at], k_halo_ref[:, at], pad], axis=0)
        value = jnp.concatenate([v_ref[:, at], v_halo_ref[:, at], pad], axis=0)
        value = jnp.concatenate([value, ones], axis=1)
        score = lax.dot_general(q_ref[:, at], key, (((1,), (1,)), ((), ())), preferred_element_type=jnp.float32)
        score = score * scale + bias[...]
        weight = jnp.exp2(score - jnp.max(score, axis=1, keepdims=True)).astype(jnp.bfloat16)
        mixture = jnp.dot(weight, value, preferred_element_type=jnp.float32)
        out_ref[:, at] = (mixture[:, :HEAD_DIM] / mixture[:, HEAD_DIM:]).astype(jnp.bfloat16)


def attend(query_rows, key_value_rows, halo, windows, spots, part, attended):
    before = [] if attended is None else [attended]
    rows, features = query_rows.shape
    query_rows = pltpu.with_memory_space_constraint(query_rows, pltpu.HBM)
    width = features // PARTS
    heads = width // HEAD_DIM
    steps = 2 if heads % 2 == 0 else 1
    block = width // steps
    halo_rows = halo.shape[1]
    first = part * steps
    keys = pl.cdiv(rows + halo_rows, LANES) * LANES
    return pl.pallas_call(
        functools.partial(attend_kernel, spots),
        grid=(steps,),
        out_shape=jax.ShapeDtypeStruct((rows, features), jnp.bfloat16),
        in_specs=[
            IN_SMEM,
            pl.BlockSpec((rows, block), lambda i: (0, first + i)),
            pl.BlockSpec((None, rows, block), lambda i: (0, 0, first + i)),
            pl.BlockSpec((None, rows, block), lambda i: (1, 0, first + i)),
            pl.BlockSpec((None, halo_rows, block), lambda i: (0, 0, i)),
            pl.BlockSpec((None, halo_rows, block), lambda i: (1, 0, i)),
        ]
        + [ANYWHERE] * len(before),
        out_specs=pl.BlockSpec((rows, block), lambda i: (0, first + i)),
        input_output_aliases={6: 0} if before else {},
        scratch_shapes=[pltpu.VMEM((rows, keys), jnp.float32)],
        compiler_params=pltpu.CompilerParams(vmem_limit_bytes=10 * MIB),
        cost_estimate=pl.CostEstimate(
            flops=32 * rows * keys * width, bytes_accessed=2 * width * (2 * rows + 2 * keys), transcendentals=heads * rows * keys
        ),
        name="attend",
    )(windows, query_rows, key_value_rows, key_value_rows, halo, halo, *before)


def arrange_kernel(near_ref, far_ref, out_ref):
    rows = near_ref.shape[0]
    depth = out_ref.shape[2]
    for owner in range(out_ref.shape[0]):
        at = slice(owner * depth, (owner + 1) * depth)
        out_ref[owner, :rows] = near_ref[:, at]
        out_ref[owner, rows:] = far_ref[:, at]


def arrange(near, far, count):
    rows, features = near.shape
    return pl.pallas_call(
        arrange_kernel,
        out_shape=jax.ShapeDtypeStruct((count, 2 * rows, features // count), near.dtype),
        in_specs=[IN_VMEM] * 2,
        out_specs=IN_VMEM,
        compiler_params=pltpu.CompilerParams(vmem_limit_bytes=8 * MIB),
        cost_estimate=pl.CostEstimate(flops=0, bytes_accessed=8 * near.size, transcendentals=0),
        name="arrange",
    )(near, far)


def project_kernel(strip, column, total, tables_ref, rows_ref, *refs):
    count = tables_ref.shape[2]
    w_refs, gate_refs, out_refs = refs[:count], refs[count : count + 2], refs[count + 2 :]
    owner, slab = lax.axis_index("owner"), lax.axis_index("slab")
    rows, width = out_refs[0].shape
    sources = [tables_ref[slab, owner, index] for index in range(count)]
    place = lax.axis_index("groups") * total + column + (1 - slab if strip else slab) * width
    for first in range(0, width, 2 * LANES):
        tile = min(2 * LANES, width - first)
        product = None
        for source, w_ref in zip(sources, w_refs):
            term = jnp.dot(rows_ref[source], w_ref[:, first : first + tile], preferred_element_type=jnp.float32)
            product = term if product is None else product + term
        here = pl.ds(pl.multiple_of(place + first, LANES), tile)
        for block in range(2):
            gate = gate_refs[block][:, here]
            result = product[block * rows : (block + 1) * rows] * gate
            out_refs[block][:, first : first + tile] = result.astype(jnp.bfloat16)


def project(table, arranged, chunks, gates, strip, column, total):
    count, rows, depth = arranged.shape
    width = chunks[0].shape[1]
    return pl.pallas_call(
        functools.partial(project_kernel, strip, column, total),
        out_shape=[jax.ShapeDtypeStruct((rows // 2, width), jnp.bfloat16)] * 2,
        in_specs=[IN_SMEM] + [IN_VMEM] * (1 + count + 2),
        out_specs=[IN_VMEM] * 2,
        compiler_params=pltpu.CompilerParams(vmem_limit_bytes=16 * MIB),
        cost_estimate=pl.CostEstimate(
            flops=3 * rows * width * depth * count,
            bytes_accessed=2 * (rows * (depth * count + width) + count * depth * width),
            transcendentals=0,
        ),
        name="project",
    )(table, arranged, *chunks, *gates)


def place_kernel(count, columns, total, *refs):
    in_refs, (out_ref, done) = refs[:count], refs[-2:]
    group, slab = lax.axis_index("groups"), lax.axis_index("slab")
    copies = []
    for index, in_ref in enumerate(in_refs):
        strip, away = divmod(index, 2)
        width = in_ref.shape[1]
        start = (1 - group if away else group) * total + columns[strip][0] + (1 - slab if columns[strip][1] else slab) * width
        at = pl.ds(pl.multiple_of(start, LANES), width)
        copies.append(pltpu.make_async_copy(in_ref, out_ref.at[:, at], done.at[index]))
    run_copies(copies)


def place(blocks, out, columns, total, model_width):
    rows = blocks[0].shape[0]
    held = [] if out is None else [out]
    return pl.pallas_call(
        functools.partial(place_kernel, len(blocks), columns, total),
        out_shape=jax.ShapeDtypeStruct((rows, model_width), jnp.bfloat16),
        in_specs=[IN_VMEM] * len(blocks) + [ANYWHERE] * len(held),
        out_specs=ANYWHERE,
        scratch_shapes=[pltpu.SemaphoreType.DMA((len(blocks),))],
        input_output_aliases={len(blocks): 0} if held else {},
        compiler_params=pltpu.CompilerParams(vmem_limit_bytes=4 * MIB),
        cost_estimate=pl.CostEstimate(flops=0, bytes_accessed=4 * sum(block.size for block in blocks), transcendentals=0),
        name="place",
    )(*blocks, *held)


def hop_order(pieces, turns):
    order = []
    for piece in range(pieces):
        hops = [(piece, strip, turn) for turn in range(1, turns[0] + 1) for strip in range(2) if turn <= turns[strip]]
        order = order[:-1] + hops[:1] + order[-1:] + hops[1:] if order else hops
    return order


def on_device(queries, key_value, keep, windows, gate, out_weight):
    frames_here, spots, features = queries.shape[1:]
    model_width = gate.shape[1]
    rows = frames_here * spots
    slabs = lax.axis_size("slab")
    total = model_width // lax.axis_size("groups")
    widths = piece_widths(total)

    count = lax.axis_size("owner")
    order = ring_order(count)
    spot_of = [order.index(owner) for owner in range(count)]
    ring = [
        (owner * slabs + slab, order[(spot_of[owner] + step) % count] * slabs + slab)
        for owner in range(count)
        for slab, step in enumerate((1, -1))
    ]
    turns = (count // 2, (count - 1) // 2)
    hops = hop_order(len(widths), turns)

    firsts = [2 * sum(widths[:piece]) for piece in range(len(widths))]
    held, arrived, crossed, edges = {}, [], {}, []
    for piece, width in enumerate(widths):
        own_strips, border = cut(out_weight, key_value, width, firsts[piece], total, piece == 0)
        edges = border or edges
        for strip, own in enumerate(own_strips):
            held[piece, strip, 0] = own

    def hop(slot, *others):
        if slot >= len(hops):
            return
        piece, strip, turn = hops[slot]
        waits = list(others)
        if slot >= FLIGHT:
            waits.append(arrived[slot - FLIGHT])
        if slot > 2 * FLIGHT:
            waits.append(crossed[hops[slot - 2 * FLIGHT - 1]])
        value = held[piece, strip, turn - 1]
        if waits:
            value = after(value, *waits)
        value = lax.ppermute(value, ("owner", "slab"), ring)
        held[hops[slot]] = value
        arrived.append(value)

    def cross(slot, *others):
        value = arrived[slot]
        crossed[hops[slot]] = swap(after(value, *others) if others else value, ("slab",))

    first_done = max(slot for slot, at in enumerate(hops) if at[0] == 0) if hops else 0
    halos = [swap(edge, ("slab",)) for edge in edges]
    for slot in range(FLIGHT):
        hop(slot)

    query_rows = queries.reshape(rows, features)
    key_value_rows = key_value.reshape(2, rows, features)
    waits, attended = {FLIGHT + 2: [held[piece, 0, 0] for piece in range(1, len(widths))]}, None
    for part in range(PARTS):
        attended = attend(query_rows, key_value_rows, halos[part], windows, spots, part, attended)
    a_blocks = (attended, swap(attended, ("groups",)))
    near_gate = scale_gate(after(keep, attended), gate)
    gates = (near_gate, swap(near_gate, ("groups",)))
    waits.setdefault(FLIGHT, []).append(attended)
    waits.setdefault(first_done, []).append(a_blocks[1])

    arranged = arrange(*a_blocks, count)

    def project_strip(piece, strip, *others):
        chunks, sources = [], []
        for turn in range(turns[strip] + 1):
            chunks.append(held[piece, strip, turn])
            sources.append((-turn, turn))
        for turn in range(1, turns[1 - strip] + 1):
            chunks.append(crossed[piece, 1 - strip, turn])
            sources.append((turn, -turn))
        table = np.zeros((slabs, count, len(chunks)), np.int32)
        for slab in range(slabs):
            for owner in range(count):
                table[slab, owner] = [order[(spot_of[owner] + source[slab]) % count] for source in sources]
        if others:
            chunks[0] = after(chunks[0], *others)
        own, away = project(jnp.asarray(table), arranged, chunks, gates, strip, firsts[piece], total)
        return [own, swap(away, ("groups",))]

    results, needs = {}, {}
    if first_done >= 2 and first_done + 1 < len(hops):
        needs[first_done - 2] = [first_done - 1, gates[1], arranged]
    for slot in range(FLIGHT, len(hops)):
        strip = {first_done + 3: 0, first_done + 5: 1}.get(slot)
        if strip is not None:
            results[0, strip] = project_strip(0, strip, *(arrived[first_done + 1 : first_done + 2] if strip else []))
            waits.setdefault(slot, []).append(results[0, strip][0])
            if strip:
                needs[len(hops) - 2] = [results[0, strip][1]]
                waits[slot].append(arrived[slot - 1])
            else:
                needs[first_done + 1] = [results[0, strip][0]]
                waits.setdefault(len(hops) - 2, []).append(results[0, strip][1])
        others = needs.get(slot - FLIGHT, [])
        cross(slot - FLIGHT, *(arrived[other] if isinstance(other, int) else other for other in others))
        hop(slot, *waits.get(slot, []))
    for slot in range(max(len(hops) - FLIGHT, 0), len(hops)):
        cross(slot, *needs.get(slot, []))
    for piece in range(len(widths)):
        for strip in range(2):
            if (piece, strip) not in results:
                results[piece, strip] = project_strip(piece, strip)
    out = None
    last = (len(widths) - 1, 1)
    for batch in ([key for key in results if key != last], [last]):
        blocks = [block for key in batch for block in results[key]]
        out = place(blocks, out, [(firsts[piece], strip) for piece, strip in batch], total, model_width)
    return out.reshape((1, frames_here, spots, model_width))


def solution(mesh):
    placed = (
        P(("groups", "owner"), "slab", None, None),
        P(None, ("groups", "owner"), "slab", None, None),
        P("groups"),
        P("groups", None),
        P("groups", None),
        P("owner", None),
    )
    return jax.shard_map(
        on_device,
        mesh=mesh,
        in_specs=placed,
        out_specs=P(("groups", "owner"), "slab", None, None),
        check_vma=False,
    )
```

```python
import functools
import math

import jax
import jax.numpy as jnp
import numpy as np
from jax import lax
from jax.experimental import pallas as pl
from jax.experimental.pallas import tpu as pltpu
from jax.sharding import PartitionSpec as P

HEAD_DIM = 128
WB = 14
HALO = 1
LANES = 128
NEG_LARGE = -1e30
PARTS = 2
FLIGHT = 2
MIB = 1024 * 1024
ANYWHERE = pl.BlockSpec(memory_space=pl.ANY)
IN_HBM = pl.BlockSpec(memory_space=pltpu.HBM)
IN_VMEM = pl.BlockSpec(memory_space=pltpu.VMEM)
IN_SMEM = pl.BlockSpec(memory_space=pltpu.SMEM)


def ring_order(count):
    width = max(w for w in range(1, count + 1) if count % w == 0 and w * w <= count)
    height = count // width
    if width == 1 or height % 2:
        return list(range(count))
    order = []
    for row in range(height):
        columns = range(1, width) if row % 2 == 0 else range(width - 1, 0, -1)
        order += [row * width + column for column in columns]
    return order + [row * width for row in range(height - 1, -1, -1)]


def piece_widths(half_width):
    tiles = half_width // (2 * LANES)
    late = 2 * tiles // 5
    return [count * LANES for count in (tiles - late, late) if count]


def swap(value, axes):
    count = math.prod(lax.axis_size(axis) for axis in axes)
    return lax.ppermute(value, axes, [(i, count - 1 - i) for i in range(count)])


def after(value, *others):
    return lax.optimization_barrier((value,) + others)[0]


def run_copies(copies):
    for copy in copies:
        copy.start()
    for copy in copies:
        copy.wait()


def cut_kernel(first, total, with_border, weight_ref, key_value_ref, *refs):
    out_refs, done = refs[:-1], refs[-1]
    slab = lax.axis_index("slab")
    width = out_refs[0].shape[1]
    sources = []
    for strip in range(2):
        column = lax.axis_index("groups") * total + first + (1 - slab if strip else slab) * width
        sources.append(weight_ref.at[:, pl.ds(pl.multiple_of(column, LANES), width)])
    if with_border:
        frames_here = key_value_ref.shape[2]
        frame = jnp.where(slab == 0, frames_here - HALO, 0)
        width = out_refs[-1].shape[3]
        for part in range(PARTS):
            sources.append(key_value_ref.at[:, 0, pl.ds(frame, HALO), :, part * width : (part + 1) * width])
    run_copies([pltpu.make_async_copy(s, t, done.at[i]) for i, (s, t) in enumerate(zip(sources, out_refs))])


def cut(out_weight, key_value, width, first, total, with_border):
    depth = out_weight.shape[0]
    kinds, _, _, spots, features = key_value.shape
    shapes = [(depth, width)] * 2
    shapes += [(kinds, HALO, spots, features // PARTS)] * PARTS if with_border else []
    out_weight = pltpu.with_memory_space_constraint(out_weight, pltpu.HBM)
    key_value = pltpu.with_memory_space_constraint(key_value, pltpu.HBM)
    outs = pl.pallas_call(
        functools.partial(cut_kernel, first, total, with_border),
        out_shape=[jax.ShapeDtypeStruct(shape, jnp.bfloat16) for shape in shapes],
        in_specs=[IN_HBM] * 2,
        out_specs=[IN_VMEM] * len(shapes),
        scratch_shapes=[pltpu.SemaphoreType.DMA((len(shapes),))],
        compiler_params=pltpu.CompilerParams(vmem_limit_bytes=4 * MIB),
        cost_estimate=pl.CostEstimate(flops=0, bytes_accessed=8 * depth * width, transcendentals=0),
        name="cut",
    )(out_weight, key_value)
    return outs[:2], [edge.reshape(kinds, HALO * spots, features // PARTS) for edge in outs[2:]]


def scale_kernel(keep_ref, gate_ref, out_ref):
    owner = lax.axis_index("owner")
    factor = jnp.where(owner % 2 == 1, keep_ref[owner // 2], 1).astype(jnp.float32)
    out_ref[...] = gate_ref[pl.ds(owner // 2, 1), :] * factor


def scale_gate(keep, gate):
    return pl.pallas_call(
        scale_kernel,
        out_shape=jax.ShapeDtypeStruct((1, gate.shape[1]), jnp.float32),
        in_specs=[IN_SMEM, IN_VMEM],
        out_specs=IN_VMEM,
        compiler_params=pltpu.CompilerParams(vmem_limit_bytes=MIB),
        name="scale_gate",
    )(keep, gate)


def token_place(count, dim, spots, first_frame):
    shape = (count, 1) if dim == 0 else (1, count)
    token = lax.broadcasted_iota(jnp.int32, shape, dim).astype(jnp.float32)
    frame = jnp.floor((token + 0.5) * (1.0 / spots))
    spot = token - frame * spots
    row = jnp.floor((spot + 0.5) * (1.0 / WB))
    return frame + first_frame, row, spot - row * WB


def attend_kernel(spots, windows_ref, q_ref, k_ref, v_ref, k_halo_ref, v_halo_ref, *refs):
    out_ref, bias = refs[-2:]
    rows = q_ref.shape[0]
    halo_rows = k_halo_ref.shape[0]
    keys = bias.shape[1]
    frames_here = rows // spots

    @pl.when(pl.program_id(0) == 0)
    def _():
        request = lax.axis_index("owner") // 2
        halo_frame = jnp.where(lax.axis_index("slab") == 0, 0, -HALO - frames_here).astype(jnp.float32)
        query = token_place(rows, 0, spots, 0.0)
        key = token_place(keys, 1, spots, 0.0)
        index = lax.broadcasted_iota(jnp.int32, (1, keys), 1)
        frame = jnp.where(index < rows, key[0], key[0] + halo_frame)
        frame = jnp.where(index < rows + halo_rows, frame, -NEG_LARGE)
        allowed = None
        for part, place in enumerate((frame, key[1], key[2])):
            near = jnp.abs(query[part] - place) <= windows_ref[request, part].astype(jnp.float32)
            allowed = near if allowed is None else allowed & near
        bias[...] = jnp.where(allowed, 0.0, NEG_LARGE)

    scale = math.log2(math.e) / math.sqrt(HEAD_DIM)
    pad = jnp.zeros((keys - rows - halo_rows, HEAD_DIM), jnp.bfloat16)
    ones = jnp.ones((keys, HEAD_DIM), jnp.bfloat16)
    for head in range(q_ref.shape[1] // HEAD_DIM):
        at = slice(head * HEAD_DIM, (head + 1) * HEAD_DIM)
        key = jnp.concatenate([k_ref[:, at], k_halo_ref[:, at], pad], axis=0)
        value = jnp.concatenate([v_ref[:, at], v_halo_ref[:, at], pad], axis=0)
        value = jnp.concatenate([value, ones], axis=1)
        score = lax.dot_general(q_ref[:, at], key, (((1,), (1,)), ((), ())), preferred_element_type=jnp.float32)
        score = score * scale + bias[...]
        weight = jnp.exp2(score - jnp.max(score, axis=1, keepdims=True)).astype(jnp.bfloat16)
        mixture = jnp.dot(weight, value, preferred_element_type=jnp.float32)
        out_ref[:, at] = (mixture[:, :HEAD_DIM] / mixture[:, HEAD_DIM:]).astype(jnp.bfloat16)


def attend(query_rows, key_value_rows, halo, windows, spots, part, attended):
    before = [] if attended is None else [attended]
    rows, features = query_rows.shape
    query_rows = pltpu.with_memory_space_constraint(query_rows, pltpu.HBM)
    width = features // PARTS
    heads = width // HEAD_DIM
    steps = 2 if heads % 2 == 0 else 1
    block = width // steps
    halo_rows = halo.shape[1]
    first = part * steps
    keys = pl.cdiv(rows + halo_rows, LANES) * LANES
    return pl.pallas_call(
        functools.partial(attend_kernel, spots),
        grid=(steps,),
        out_shape=jax.ShapeDtypeStruct((rows, features), jnp.bfloat16),
        in_specs=[
            IN_SMEM,
            pl.BlockSpec((rows, block), lambda i: (0, first + i)),
            pl.BlockSpec((None, rows, block), lambda i: (0, 0, first + i)),
            pl.BlockSpec((None, rows, block), lambda i: (1, 0, first + i)),
            pl.BlockSpec((None, halo_rows, block), lambda i: (0, 0, i)),
            pl.BlockSpec((None, halo_rows, block), lambda i: (1, 0, i)),
        ]
        + [ANYWHERE] * len(before),
        out_specs=pl.BlockSpec((rows, block), lambda i: (0, first + i)),
        input_output_aliases={6: 0} if before else {},
        scratch_shapes=[pltpu.VMEM((rows, keys), jnp.float32)],
        compiler_params=pltpu.CompilerParams(vmem_limit_bytes=10 * MIB),
        cost_estimate=pl.CostEstimate(
            flops=32 * rows * keys * width, bytes_accessed=2 * width * (2 * rows + 2 * keys), transcendentals=heads * rows * keys
        ),
        name="attend",
    )(windows, query_rows, key_value_rows, key_value_rows, halo, halo, *before)


def arrange_kernel(near_ref, far_ref, out_ref):
    rows = near_ref.shape[0]
    depth = out_ref.shape[2]
    for owner in range(out_ref.shape[0]):
        at = slice(owner * depth, (owner + 1) * depth)
        out_ref[owner, :rows] = near_ref[:, at]
        out_ref[owner, rows:] = far_ref[:, at]


def arrange(near, far, count):
    rows, features = near.shape
    return pl.pallas_call(
        arrange_kernel,
        out_shape=jax.ShapeDtypeStruct((count, 2 * rows, features // count), near.dtype),
        in_specs=[IN_VMEM] * 2,
        out_specs=IN_VMEM,
        compiler_params=pltpu.CompilerParams(vmem_limit_bytes=8 * MIB),
        cost_estimate=pl.CostEstimate(flops=0, bytes_accessed=8 * near.size, transcendentals=0),
        name="arrange",
    )(near, far)


def project_kernel(strip, column, total, begun, tables_ref, rows_ref, *refs):
    count = tables_ref.shape[2]
    w_refs, refs = refs[:count], refs[count:]
    sum_ref, refs = (refs[0], refs[1:]) if begun else (None, refs)
    owner, slab = lax.axis_index("owner"), lax.axis_index("slab")
    width = w_refs[0].shape[1]
    sources = [tables_ref[slab, owner, index] for index in range(count)]
    place = lax.axis_index("groups") * total + column + (1 - slab if strip else slab) * width
    for first in range(0, width, 2 * LANES):
        tile = min(2 * LANES, width - first)
        at = slice(first, first + tile)
        product = sum_ref[:, at] if begun else None
        for source, w_ref in zip(sources, w_refs):
            term = jnp.dot(rows_ref[source], w_ref[:, at], preferred_element_type=jnp.float32)
            product = term if product is None else product + term
        if len(refs) == 1:
            refs[0][:, at] = product
            continue
        here = pl.ds(pl.multiple_of(place + first, LANES), tile)
        rows = refs[2].shape[0]
        for block in range(2):
            gate = refs[block][:, here]
            result = product[block * rows : (block + 1) * rows] * gate
            refs[2 + block][:, at] = result.astype(jnp.bfloat16)


def project(table, arranged, chunks, begun, gates, strip, column, total):
    rows, depth = arranged.shape[1:]
    count, width = len(chunks), chunks[0].shape[1]
    begun = [] if begun is None else [begun]
    out_shape = jax.ShapeDtypeStruct((rows, width), jnp.float32)
    if gates:
        out_shape = [jax.ShapeDtypeStruct((rows // 2, width), jnp.bfloat16)] * 2
    return pl.pallas_call(
        functools.partial(project_kernel, strip, column, total, bool(begun)),
        out_shape=out_shape,
        in_specs=[IN_SMEM] + [IN_VMEM] * (1 + count + len(begun) + len(gates)),
        out_specs=[IN_VMEM] * 2 if gates else IN_VMEM,
        compiler_params=pltpu.CompilerParams(vmem_limit_bytes=16 * MIB),
        cost_estimate=pl.CostEstimate(
            flops=3 * rows * width * depth * count,
            bytes_accessed=2 * (rows * (depth * count + width) + count * depth * width),
            transcendentals=0,
        ),
        name="project",
    )(table, arranged, *chunks, *begun, *gates)


def place_kernel(count, columns, total, *refs):
    in_refs, (out_ref, done) = refs[:count], refs[-2:]
    group, slab = lax.axis_index("groups"), lax.axis_index("slab")
    copies = []
    for index, in_ref in enumerate(in_refs):
        strip, away = divmod(index, 2)
        width = in_ref.shape[1]
        start = (1 - group if away else group) * total + columns[strip][0] + (1 - slab if columns[strip][1] else slab) * width
        at = pl.ds(pl.multiple_of(start, LANES), width)
        copies.append(pltpu.make_async_copy(in_ref, out_ref.at[:, at], done.at[index]))
    run_copies(copies)


def place(blocks, out, columns, total, model_width):
    rows = blocks[0].shape[0]
    held = [] if out is None else [out]
    return pl.pallas_call(
        functools.partial(place_kernel, len(blocks), columns, total),
        out_shape=jax.ShapeDtypeStruct((rows, model_width), jnp.bfloat16),
        in_specs=[IN_VMEM] * len(blocks) + [ANYWHERE] * len(held),
        out_specs=ANYWHERE,
        scratch_shapes=[pltpu.SemaphoreType.DMA((len(blocks),))],
        input_output_aliases={len(blocks): 0} if held else {},
        compiler_params=pltpu.CompilerParams(vmem_limit_bytes=4 * MIB),
        cost_estimate=pl.CostEstimate(flops=0, bytes_accessed=4 * sum(block.size for block in blocks), transcendentals=0),
        name="place",
    )(*blocks, *held)


def hop_order(pieces, turns):
    order = []
    for piece in range(pieces):
        hops = [(piece, strip, turn) for turn in range(1, turns[0] + 1) for strip in range(2) if turn <= turns[strip]]
        order = order[:-1] + hops[:1] + order[-1:] + hops[1:] if order else hops
    return order


def on_device(queries, key_value, keep, windows, gate, out_weight):
    frames_here, spots, features = queries.shape[1:]
    model_width = gate.shape[1]
    rows = frames_here * spots
    slabs = lax.axis_size("slab")
    total = model_width // lax.axis_size("groups")
    widths = piece_widths(total)

    count = lax.axis_size("owner")
    order = ring_order(count)
    spot_of = [order.index(owner) for owner in range(count)]
    ring = [
        (owner * slabs + slab, order[(spot_of[owner] + step) % count] * slabs + slab)
        for owner in range(count)
        for slab, step in enumerate((1, -1))
    ]
    turns = (count // 2, (count - 1) // 2)
    hops = hop_order(len(widths), turns)

    firsts = [2 * sum(widths[:piece]) for piece in range(len(widths))]
    held, arrived, crossed, edges = {}, [], {}, []
    for piece, width in enumerate(widths):
        own_strips, border = cut(out_weight, key_value, width, firsts[piece], total, piece == 0)
        edges = border or edges
        for strip, own in enumerate(own_strips):
            held[piece, strip, 0] = own

    def hop(slot, *others):
        if slot >= len(hops):
            return
        piece, strip, turn = hops[slot]
        waits = list(others)
        if slot >= FLIGHT:
            waits.append(arrived[slot - FLIGHT])
        if slot > 2 * FLIGHT:
            waits.append(crossed[hops[slot - 2 * FLIGHT - 1]])
        value = held[piece, strip, turn - 1]
        if waits:
            value = after(value, *waits)
        value = lax.ppermute(value, ("owner", "slab"), ring)
        held[hops[slot]] = value
        arrived.append(value)

    def cross(slot, *others):
        value = arrived[slot]
        crossed[hops[slot]] = swap(after(value, *others) if others else value, ("slab",))

    first_done = max(slot for slot, at in enumerate(hops) if at[0] == 0) if hops else 0
    halos = [swap(edge, ("slab",)) for edge in edges]
    for slot in range(FLIGHT):
        hop(slot)

    query_rows = queries.reshape(rows, features)
    key_value_rows = key_value.reshape(2, rows, features)
    waits, attended = {FLIGHT + 2: [held[piece, 0, 0] for piece in range(1, len(widths))]}, None
    for part in range(PARTS):
        attended = attend(query_rows, key_value_rows, halos[part], windows, spots, part, attended)
    a_blocks = (attended, swap(attended, ("groups",)))
    near_gate = scale_gate(after(keep, attended), gate)
    gates = (near_gate, swap(near_gate, ("groups",)))
    waits.setdefault(FLIGHT, []).append(attended)
    waits.setdefault(first_done, []).append(a_blocks[1])

    arranged = arrange(*a_blocks, count)

    begun = {}

    def project_strip(piece, strip, *others, final=True):
        sources = [(-turn, turn) for turn in range(turns[strip] + 1)]
        sources += [(turn, -turn) for turn in range(1, turns[1 - strip] + 1)]
        late = {len(sources) - 1, turns[strip]} if strip == 0 else {len(sources) - 1}
        batch = sorted(late if final else set(range(len(sources))) - late)
        if final and (piece, strip) not in begun:
            project_strip(piece, strip, final=False)
        if not batch:
            begun[piece, strip] = None
            return None
        chunks = [
            held[piece, strip, index] if index <= turns[strip] else crossed[piece, 1 - strip, index - turns[strip]]
            for index in batch
        ]
        table = np.zeros((slabs, count, len(batch)), np.int32)
        for slab in range(slabs):
            for owner in range(count):
                table[slab, owner] = [order[(spot_of[owner] + sources[index][slab]) % count] for index in batch]
        if others:
            chunks[0] = after(chunks[0], *others)
        before, gates_here = (begun[piece, strip], gates) if final else (None, ())
        result = project(jnp.asarray(table), arranged, chunks, before, gates_here, strip, firsts[piece], total)
        if not final:
            begun[piece, strip] = result
            return result
        return [result[0], swap(result[1], ("groups",))]

    results, needs = {}, {}
    if first_done >= 2 and first_done + 1 < len(hops):
        needs[first_done - 2] = [first_done - 1, gates[1], arranged]
    for slot in range(FLIGHT, len(hops)):
        strip = {first_done + 3: 0, first_done + 5: 1}.get(slot)
        if strip is not None:
            results[0, strip] = project_strip(0, strip, *(arrived[first_done + 1 : first_done + 2] if strip else []))
            waits.setdefault(slot, []).append(results[0, strip][0])
            if strip:
                needs[len(hops) - 2] = [results[0, strip][1]]
                waits[slot].append(arrived[slot - 1])
            else:
                needs[first_done + 1] = [results[0, strip][0]]
                waits.setdefault(len(hops) - 2, []).append(results[0, strip][1])
        others = needs.get(slot - FLIGHT, [])
        cross(slot - FLIGHT, *(arrived[other] if isinstance(other, int) else other for other in others))
        hop(slot, *waits.get(slot, []))
    if len(hops) > 2 * FLIGHT and len(widths) > 1:
        needs[len(hops) - 1] = [project_strip(len(widths) - 1, strip, final=False) for strip in range(2)]
    for slot in range(max(len(hops) - FLIGHT, 0), len(hops)):
        cross(slot, *needs.get(slot, []))
    for piece in range(len(widths)):
        for strip in range(2):
            if (piece, strip) not in results:
                results[piece, strip] = project_strip(piece, strip)
    out = None
    last = (len(widths) - 1, 1)
    for batch in ([key for key in results if key != last], [last]):
        blocks = [block for key in batch for block in results[key]]
        out = place(blocks, out, [(firsts[piece], strip) for piece, strip in batch], total, model_width)
    return out.reshape((1, frames_here, spots, model_width))


def solution(mesh):
    placed = (
        P(("groups", "owner"), "slab", None, None),
        P(None, ("groups", "owner"), "slab", None, None),
        P("groups"),
        P("groups", None),
        P("groups", None),
        P("owner", None),
    )
    return jax.shard_map(
        on_device,
        mesh=mesh,
        in_specs=placed,
        out_specs=P(("groups", "owner"), "slab", None, None),
        check_vma=False,
    )
```

```python
import functools
import math

import jax
import jax.numpy as jnp
import numpy as np
from jax import lax
from jax.experimental import pallas as pl
from jax.experimental.pallas import tpu as pltpu
from jax.sharding import PartitionSpec as P

HEAD_DIM = 128
WB = 14
HALO = 1
LANES = 128
NEG_LARGE = -1e30
PARTS = 2
FLIGHT = 2
MIB = 1024 * 1024
ANYWHERE = pl.BlockSpec(memory_space=pl.ANY)
IN_HBM = pl.BlockSpec(memory_space=pltpu.HBM)
IN_VMEM = pl.BlockSpec(memory_space=pltpu.VMEM)
IN_SMEM = pl.BlockSpec(memory_space=pltpu.SMEM)


def ring_order(count):
    width = max(w for w in range(1, count + 1) if count % w == 0 and w * w <= count)
    height = count // width
    if width == 1 or height % 2:
        return list(range(count))
    order = []
    for row in range(height):
        columns = range(1, width) if row % 2 == 0 else range(width - 1, 0, -1)
        order += [row * width + column for column in columns]
    return order + [row * width for row in range(height - 1, -1, -1)]


def piece_widths(half_width):
    tiles = half_width // (2 * LANES)
    late = 2 * tiles // 5
    return [count * LANES for count in (tiles - late, late) if count]


def swap(value, axes):
    count = math.prod(lax.axis_size(axis) for axis in axes)
    return lax.ppermute(value, axes, [(i, count - 1 - i) for i in range(count)])


def after(value, *others):
    return lax.optimization_barrier((value,) + others)[0]


def run_copies(copies):
    for copy in copies:
        copy.start()
    for copy in copies:
        copy.wait()


def cut_kernel(first, total, with_border, weight_ref, key_value_ref, *refs):
    out_refs, done = refs[:-1], refs[-1]
    slab = lax.axis_index("slab")
    width = out_refs[0].shape[1]
    sources = []
    for strip in range(2):
        column = lax.axis_index("groups") * total + first + (1 - slab if strip else slab) * width
        sources.append(weight_ref.at[:, pl.ds(pl.multiple_of(column, LANES), width)])
    if with_border:
        frames_here = key_value_ref.shape[2]
        frame = jnp.where(slab == 0, frames_here - HALO, 0)
        width = out_refs[-1].shape[3]
        for part in range(PARTS):
            sources.append(key_value_ref.at[:, 0, pl.ds(frame, HALO), :, part * width : (part + 1) * width])
    run_copies([pltpu.make_async_copy(s, t, done.at[i]) for i, (s, t) in enumerate(zip(sources, out_refs))])


def cut(out_weight, key_value, width, first, total, with_border):
    depth = out_weight.shape[0]
    kinds, _, _, spots, features = key_value.shape
    shapes = [(depth, width)] * 2
    shapes += [(kinds, HALO, spots, features // PARTS)] * PARTS if with_border else []
    out_weight = pltpu.with_memory_space_constraint(out_weight, pltpu.HBM)
    key_value = pltpu.with_memory_space_constraint(key_value, pltpu.HBM)
    outs = pl.pallas_call(
        functools.partial(cut_kernel, first, total, with_border),
        out_shape=[jax.ShapeDtypeStruct(shape, jnp.bfloat16) for shape in shapes],
        in_specs=[IN_HBM] * 2,
        out_specs=[IN_VMEM] * len(shapes),
        scratch_shapes=[pltpu.SemaphoreType.DMA((len(shapes),))],
        compiler_params=pltpu.CompilerParams(vmem_limit_bytes=4 * MIB),
        cost_estimate=pl.CostEstimate(flops=0, bytes_accessed=8 * depth * width, transcendentals=0),
        name="cut",
    )(out_weight, key_value)
    return outs[:2], [edge.reshape(kinds, HALO * spots, features // PARTS) for edge in outs[2:]]


def scale_kernel(keep_ref, gate_ref, out_ref):
    owner = lax.axis_index("owner")
    factor = jnp.where(owner % 2 == 1, keep_ref[owner // 2], 1).astype(jnp.float32)
    out_ref[...] = gate_ref[pl.ds(owner // 2, 1), :] * factor


def scale_gate(keep, gate):
    return pl.pallas_call(
        scale_kernel,
        out_shape=jax.ShapeDtypeStruct((1, gate.shape[1]), jnp.float32),
        in_specs=[IN_SMEM, IN_VMEM],
        out_specs=IN_VMEM,
        compiler_params=pltpu.CompilerParams(vmem_limit_bytes=MIB),
        name="scale_gate",
    )(keep, gate)


def token_place(count, dim, spots, first_frame):
    shape = (count, 1) if dim == 0 else (1, count)
    token = lax.broadcasted_iota(jnp.int32, shape, dim).astype(jnp.float32)
    frame = jnp.floor((token + 0.5) * (1.0 / spots))
    spot = token - frame * spots
    row = jnp.floor((spot + 0.5) * (1.0 / WB))
    return frame + first_frame, row, spot - row * WB


def attend_kernel(spots, windows_ref, q_ref, k_ref, v_ref, k_halo_ref, v_halo_ref, *refs):
    out_ref, bias = refs[-2:]
    rows = q_ref.shape[0]
    halo_rows = k_halo_ref.shape[0]
    keys = bias.shape[1]
    frames_here = rows // spots

    @pl.when(pl.program_id(0) == 0)
    def _():
        request = lax.axis_index("owner") // 2
        halo_frame = jnp.where(lax.axis_index("slab") == 0, 0, -HALO - frames_here).astype(jnp.float32)
        query = token_place(rows, 0, spots, 0.0)
        key = token_place(keys, 1, spots, 0.0)
        index = lax.broadcasted_iota(jnp.int32, (1, keys), 1)
        frame = jnp.where(index < rows, key[0], key[0] + halo_frame)
        frame = jnp.where(index < rows + halo_rows, frame, -NEG_LARGE)
        allowed = None
        for part, place in enumerate((frame, key[1], key[2])):
            near = jnp.abs(query[part] - place) <= windows_ref[request, part].astype(jnp.float32)
            allowed = near if allowed is None else allowed & near
        bias[...] = jnp.where(allowed, 0.0, NEG_LARGE)

    scale = math.log2(math.e) / math.sqrt(HEAD_DIM)
    pad = jnp.zeros((keys - rows - halo_rows, HEAD_DIM), jnp.bfloat16)
    ones = jnp.ones((keys, HEAD_DIM), jnp.bfloat16)
    for head in range(q_ref.shape[1] // HEAD_DIM):
        at = slice(head * HEAD_DIM, (head + 1) * HEAD_DIM)
        key = jnp.concatenate([k_ref[:, at], k_halo_ref[:, at], pad], axis=0)
        value = jnp.concatenate([v_ref[:, at], v_halo_ref[:, at], pad], axis=0)
        value = jnp.concatenate([value, ones], axis=1)
        score = lax.dot_general(q_ref[:, at], key, (((1,), (1,)), ((), ())), preferred_element_type=jnp.float32)
        score = score * scale + bias[...]
        weight = jnp.exp2(score - jnp.max(score, axis=1, keepdims=True)).astype(jnp.bfloat16)
        mixture = jnp.dot(weight, value, preferred_element_type=jnp.float32)
        out_ref[:, at] = (mixture[:, :HEAD_DIM] / mixture[:, HEAD_DIM:]).astype(jnp.bfloat16)


def attend(query_rows, key_value_rows, halo, windows, spots, part, attended):
    before = [] if attended is None else [attended]
    rows, features = query_rows.shape
    query_rows = pltpu.with_memory_space_constraint(query_rows, pltpu.HBM)
    width = features // PARTS
    heads = width // HEAD_DIM
    steps = 2 if heads % 2 == 0 else 1
    block = width // steps
    halo_rows = halo.shape[1]
    first = part * steps
    keys = pl.cdiv(rows + halo_rows, LANES) * LANES
    return pl.pallas_call(
        functools.partial(attend_kernel, spots),
        grid=(steps,),
        out_shape=jax.ShapeDtypeStruct((rows, features), jnp.bfloat16),
        in_specs=[
            IN_SMEM,
            pl.BlockSpec((rows, block), lambda i: (0, first + i)),
            pl.BlockSpec((None, rows, block), lambda i: (0, 0, first + i)),
            pl.BlockSpec((None, rows, block), lambda i: (1, 0, first + i)),
            pl.BlockSpec((None, halo_rows, block), lambda i: (0, 0, i)),
            pl.BlockSpec((None, halo_rows, block), lambda i: (1, 0, i)),
        ]
        + [ANYWHERE] * len(before),
        out_specs=pl.BlockSpec((rows, block), lambda i: (0, first + i)),
        input_output_aliases={6: 0} if before else {},
        scratch_shapes=[pltpu.VMEM((rows, keys), jnp.float32)],
        compiler_params=pltpu.CompilerParams(vmem_limit_bytes=10 * MIB),
        cost_estimate=pl.CostEstimate(
            flops=32 * rows * keys * width, bytes_accessed=2 * width * (2 * rows + 2 * keys), transcendentals=heads * rows * keys
        ),
        name="attend",
    )(windows, query_rows, key_value_rows, key_value_rows, halo, halo, *before)


def arrange_kernel(near_ref, far_ref, out_ref):
    rows = near_ref.shape[0]
    depth = out_ref.shape[2]
    for owner in range(out_ref.shape[0]):
        at = slice(owner * depth, (owner + 1) * depth)
        out_ref[owner, :rows] = near_ref[:, at]
        out_ref[owner, rows:] = far_ref[:, at]


def arrange(near, far, count):
    rows, features = near.shape
    return pl.pallas_call(
        arrange_kernel,
        out_shape=jax.ShapeDtypeStruct((count, 2 * rows, features // count), near.dtype),
        in_specs=[IN_VMEM] * 2,
        out_specs=IN_VMEM,
        compiler_params=pltpu.CompilerParams(vmem_limit_bytes=8 * MIB),
        cost_estimate=pl.CostEstimate(flops=0, bytes_accessed=8 * near.size, transcendentals=0),
        name="arrange",
    )(near, far)


def project_kernel(strip, column, total, begun, tables_ref, rows_ref, *refs):
    count = tables_ref.shape[2]
    w_refs, refs = refs[:count], refs[count:]
    sum_ref, refs = (refs[0], refs[1:]) if begun else (None, refs)
    owner, slab = lax.axis_index("owner"), lax.axis_index("slab")
    width = w_refs[0].shape[1]
    sources = [tables_ref[slab, owner, index] for index in range(count)]
    place = lax.axis_index("groups") * total + column + (1 - slab if strip else slab) * width
    for first in range(0, width, 2 * LANES):
        tile = min(2 * LANES, width - first)
        at = slice(first, first + tile)
        product = sum_ref[:, at] if begun else None
        for source, w_ref in zip(sources, w_refs):
            term = jnp.dot(rows_ref[source], w_ref[:, at], preferred_element_type=jnp.float32)
            product = term if product is None else product + term
        if len(refs) == 1:
            refs[0][:, at] = product
            continue
        here = pl.ds(pl.multiple_of(place + first, LANES), tile)
        rows = refs[2].shape[0]
        for block in range(2):
            gate = refs[block][:, here]
            result = product[block * rows : (block + 1) * rows] * gate
            refs[2 + block][:, at] = result.astype(jnp.bfloat16)


def project(table, arranged, chunks, begun, gates, strip, column, total):
    rows, depth = arranged.shape[1:]
    count, width = len(chunks), chunks[0].shape[1]
    begun = [] if begun is None else [begun]
    out_shape = jax.ShapeDtypeStruct((rows, width), jnp.float32)
    if gates:
        out_shape = [jax.ShapeDtypeStruct((rows // 2, width), jnp.bfloat16)] * 2
    return pl.pallas_call(
        functools.partial(project_kernel, strip, column, total, bool(begun)),
        out_shape=out_shape,
        in_specs=[IN_SMEM] + [IN_VMEM] * (1 + count + len(begun) + len(gates)),
        out_specs=[IN_VMEM] * 2 if gates else IN_VMEM,
        compiler_params=pltpu.CompilerParams(vmem_limit_bytes=16 * MIB),
        cost_estimate=pl.CostEstimate(
            flops=3 * rows * width * depth * count if gates or not column else 0,
            bytes_accessed=2 * (rows * (depth * count + width) + count * depth * width) if gates or not column else 0,
            transcendentals=0,
        ),
        name="project",
    )(table, arranged, *chunks, *begun, *gates)


def place_kernel(count, columns, total, *refs):
    in_refs, (out_ref, done) = refs[:count], refs[-2:]
    group, slab = lax.axis_index("groups"), lax.axis_index("slab")
    copies = []
    for index, in_ref in enumerate(in_refs):
        strip, away = divmod(index, 2)
        width = in_ref.shape[1]
        start = (1 - group if away else group) * total + columns[strip][0] + (1 - slab if columns[strip][1] else slab) * width
        at = pl.ds(pl.multiple_of(start, LANES), width)
        copies.append(pltpu.make_async_copy(in_ref, out_ref.at[:, at], done.at[index]))
    run_copies(copies)


def place(blocks, out, columns, total, model_width):
    rows = blocks[0].shape[0]
    held = [] if out is None else [out]
    return pl.pallas_call(
        functools.partial(place_kernel, len(blocks), columns, total),
        out_shape=jax.ShapeDtypeStruct((rows, model_width), jnp.bfloat16),
        in_specs=[IN_VMEM] * len(blocks) + [ANYWHERE] * len(held),
        out_specs=ANYWHERE,
        scratch_shapes=[pltpu.SemaphoreType.DMA((len(blocks),))],
        input_output_aliases={len(blocks): 0} if held else {},
        compiler_params=pltpu.CompilerParams(vmem_limit_bytes=4 * MIB),
        cost_estimate=pl.CostEstimate(flops=0, bytes_accessed=4 * sum(block.size for block in blocks), transcendentals=0),
        name="place",
    )(*blocks, *held)


def hop_order(pieces, turns):
    order = []
    for piece in range(pieces):
        hops = [(piece, strip, turn) for turn in range(1, turns[0] + 1) for strip in range(2) if turn <= turns[strip]]
        order = order[:-1] + hops[:1] + order[-1:] + hops[1:] if order else hops
    return order


def on_device(queries, key_value, keep, windows, gate, out_weight):
    frames_here, spots, features = queries.shape[1:]
    model_width = gate.shape[1]
    rows = frames_here * spots
    slabs = lax.axis_size("slab")
    total = model_width // lax.axis_size("groups")
    widths = piece_widths(total)

    count = lax.axis_size("owner")
    order = ring_order(count)
    spot_of = [order.index(owner) for owner in range(count)]
    ring = [
        (owner * slabs + slab, order[(spot_of[owner] + step) % count] * slabs + slab)
        for owner in range(count)
        for slab, step in enumerate((1, -1))
    ]
    turns = (count // 2, (count - 1) // 2)
    hops = hop_order(len(widths), turns)

    firsts = [2 * sum(widths[:piece]) for piece in range(len(widths))]
    held, arrived, crossed, edges = {}, [], {}, []
    for piece, width in enumerate(widths):
        own_strips, border = cut(out_weight, key_value, width, firsts[piece], total, piece == 0)
        edges = border or edges
        for strip, own in enumerate(own_strips):
            held[piece, strip, 0] = own

    def hop(slot, *others):
        if slot >= len(hops):
            return
        piece, strip, turn = hops[slot]
        waits = list(others)
        if slot >= FLIGHT:
            waits.append(arrived[slot - FLIGHT])
        if slot > 2 * FLIGHT:
            waits.append(crossed[hops[slot - 2 * FLIGHT - 1]])
        value = held[piece, strip, turn - 1]
        if waits:
            value = after(value, *waits)
        value = lax.ppermute(value, ("owner", "slab"), ring)
        held[hops[slot]] = value
        arrived.append(value)

    def cross(slot, *others):
        value = arrived[slot]
        crossed[hops[slot]] = swap(after(value, *others) if others else value, ("slab",))

    first_done = max(slot for slot, at in enumerate(hops) if at[0] == 0) if hops else 0
    halos = [swap(edge, ("slab",)) for edge in edges]
    for slot in range(FLIGHT):
        hop(slot)

    query_rows = queries.reshape(rows, features)
    key_value_rows = key_value.reshape(2, rows, features)
    waits, attended = {FLIGHT + 2: [held[piece, 0, 0] for piece in range(1, len(widths))]}, None
    for part in range(PARTS):
        attended = attend(query_rows, key_value_rows, halos[part], windows, spots, part, attended)
    a_blocks = (attended, swap(attended, ("groups",)))
    near_gate = scale_gate(after(keep, attended), gate)
    gates = (near_gate, swap(near_gate, ("groups",)))
    waits.setdefault(FLIGHT, []).append(attended)
    waits.setdefault(first_done, []).append(a_blocks[1])

    arranged = arrange(*a_blocks, count)

    begun = {}

    def project_strip(piece, strip, *others, final=True):
        sources = [(-turn, turn) for turn in range(turns[strip] + 1)]
        sources += [(turn, -turn) for turn in range(1, turns[1 - strip] + 1)]
        late = {len(sources) - 1, turns[strip]} if strip == 0 else {len(sources) - 1}
        batch = sorted(late if final else set(range(len(sources))) - late)
        if final and (piece, strip) not in begun:
            project_strip(piece, strip, final=False)
        if not batch:
            begun[piece, strip] = None
            return None
        chunks = [
            held[piece, strip, index] if index <= turns[strip] else crossed[piece, 1 - strip, index - turns[strip]]
            for index in batch
        ]
        table = np.zeros((slabs, count, len(batch)), np.int32)
        for slab in range(slabs):
            for owner in range(count):
                table[slab, owner] = [order[(spot_of[owner] + sources[index][slab]) % count] for index in batch]
        if others:
            chunks[0] = after(chunks[0], *others)
        before, gates_here = (begun[piece, strip], gates) if final else (None, ())
        result = project(jnp.asarray(table), arranged, chunks, before, gates_here, strip, firsts[piece], total)
        if not final:
            begun[piece, strip] = result
            return result
        return [result[0], swap(result[1], ("groups",))]

    results, needs = {}, {}
    if first_done >= 2 and first_done + 1 < len(hops):
        needs[first_done - 2] = [first_done - 1, gates[1], arranged]
    for slot in range(FLIGHT, len(hops)):
        strip = {first_done + 3: 0, first_done + 5: 1}.get(slot)
        if strip is not None:
            results[0, strip] = project_strip(0, strip, *(arrived[first_done + 1 : first_done + 2] if strip else []))
            waits.setdefault(slot, []).append(results[0, strip][0])
            if strip:
                needs[len(hops) - 2] = [results[0, strip][1]]
                waits[slot].append(arrived[slot - 1])
            else:
                needs[first_done + 1] = [results[0, strip][0]]
                waits.setdefault(len(hops) - 2, []).append(results[0, strip][1])
        others = needs.get(slot - FLIGHT, [])
        cross(slot - FLIGHT, *(arrived[other] if isinstance(other, int) else other for other in others))
        hop(slot, *waits.get(slot, []))
    if len(hops) > 2 * FLIGHT and len(widths) > 1:
        sums = [project_strip(len(widths) - 1, strip, final=False) for strip in range(2)]
        needs[len(hops) - 2] = needs.get(len(hops) - 2, []) + sums
    for slot in range(max(len(hops) - FLIGHT, 0), len(hops)):
        cross(slot, *needs.get(slot, []))
    for piece in range(len(widths)):
        for strip in range(2):
            if (piece, strip) not in results:
                results[piece, strip] = project_strip(piece, strip)
    out = None
    last = (len(widths) - 1, 1)
    for batch in ([key for key in results if key != last], [last]):
        blocks = [block for key in batch for block in results[key]]
        out = place(blocks, out, [(firsts[piece], strip) for piece, strip in batch], total, model_width)
    return out.reshape((1, frames_here, spots, model_width))


def solution(mesh):
    placed = (
        P(("groups", "owner"), "slab", None, None),
        P(None, ("groups", "owner"), "slab", None, None),
        P("groups"),
        P("groups", None),
        P("groups", None),
        P("owner", None),
    )
    return jax.shard_map(
        on_device,
        mesh=mesh,
        in_specs=placed,
        out_specs=P(("groups", "owner"), "slab", None, None),
        check_vma=False,
    )
```

```python
import functools
import math

import jax
import jax.numpy as jnp
import numpy as np
from jax import lax
from jax.experimental import pallas as pl
from jax.experimental.pallas import tpu as pltpu
from jax.sharding import PartitionSpec as P

HEAD_DIM = 128
WB = 14
HALO = 1
LANES = 128
NEG_LARGE = -1e30
PARTS = 2
FLIGHT = 2
MIB = 1024 * 1024
ANYWHERE = pl.BlockSpec(memory_space=pl.ANY)
IN_HBM = pl.BlockSpec(memory_space=pltpu.HBM)
IN_VMEM = pl.BlockSpec(memory_space=pltpu.VMEM)
IN_SMEM = pl.BlockSpec(memory_space=pltpu.SMEM)


def ring_order(count):
    width = max(w for w in range(1, count + 1) if count % w == 0 and w * w <= count)
    height = count // width
    if width == 1 or height % 2:
        return list(range(count))
    order = []
    for row in range(height):
        columns = range(1, width) if row % 2 == 0 else range(width - 1, 0, -1)
        order += [row * width + column for column in columns]
    return order + [row * width for row in range(height - 1, -1, -1)]


def piece_widths(half_width):
    tiles = half_width // (2 * LANES)
    late = 2 * tiles // 5
    return [count * LANES for count in (tiles - late, late) if count]


def swap(value, axes):
    count = math.prod(lax.axis_size(axis) for axis in axes)
    return lax.ppermute(value, axes, [(i, count - 1 - i) for i in range(count)])


def after(value, *others):
    return lax.optimization_barrier((value,) + others)[0]


def run_copies(copies):
    for copy in copies:
        copy.start()
    for copy in copies:
        copy.wait()


def cut_kernel(first, total, with_border, weight_ref, key_value_ref, *refs):
    out_refs, done = refs[:-1], refs[-1]
    slab = lax.axis_index("slab")
    width = out_refs[0].shape[1]
    sources = []
    for strip in range(2):
        column = lax.axis_index("groups") * total + first + (1 - slab if strip else slab) * width
        sources.append(weight_ref.at[:, pl.ds(pl.multiple_of(column, LANES), width)])
    if with_border:
        frames_here = key_value_ref.shape[2]
        frame = jnp.where(slab == 0, frames_here - HALO, 0)
        width = out_refs[-1].shape[3]
        for part in range(PARTS):
            sources.append(key_value_ref.at[:, 0, pl.ds(frame, HALO), :, part * width : (part + 1) * width])
    run_copies([pltpu.make_async_copy(s, t, done.at[i]) for i, (s, t) in enumerate(zip(sources, out_refs))])


def cut(out_weight, key_value, width, first, total, with_border):
    depth = out_weight.shape[0]
    kinds, _, _, spots, features = key_value.shape
    shapes = [(depth, width)] * 2
    shapes += [(kinds, HALO, spots, features // PARTS)] * PARTS if with_border else []
    out_weight = pltpu.with_memory_space_constraint(out_weight, pltpu.HBM)
    key_value = pltpu.with_memory_space_constraint(key_value, pltpu.HBM)
    outs = pl.pallas_call(
        functools.partial(cut_kernel, first, total, with_border),
        out_shape=[jax.ShapeDtypeStruct(shape, jnp.bfloat16) for shape in shapes],
        in_specs=[IN_HBM] * 2,
        out_specs=[IN_VMEM] * len(shapes),
        scratch_shapes=[pltpu.SemaphoreType.DMA((len(shapes),))],
        compiler_params=pltpu.CompilerParams(vmem_limit_bytes=4 * MIB),
        cost_estimate=pl.CostEstimate(flops=0, bytes_accessed=8 * depth * width, transcendentals=0),
        name="cut",
    )(out_weight, key_value)
    return outs[:2], [edge.reshape(kinds, HALO * spots, features // PARTS) for edge in outs[2:]]


def scale_kernel(keep_ref, gate_ref, out_ref):
    owner = lax.axis_index("owner")
    factor = jnp.where(owner % 2 == 1, keep_ref[owner // 2], 1).astype(jnp.float32)
    out_ref[...] = gate_ref[pl.ds(owner // 2, 1), :] * factor


def scale_gate(keep, gate):
    return pl.pallas_call(
        scale_kernel,
        out_shape=jax.ShapeDtypeStruct((1, gate.shape[1]), jnp.float32),
        in_specs=[IN_SMEM, IN_VMEM],
        out_specs=IN_VMEM,
        compiler_params=pltpu.CompilerParams(vmem_limit_bytes=MIB),
        name="scale_gate",
    )(keep, gate)


def token_place(count, dim, spots, first_frame):
    shape = (count, 1) if dim == 0 else (1, count)
    token = lax.broadcasted_iota(jnp.int32, shape, dim).astype(jnp.float32)
    frame = jnp.floor((token + 0.5) * (1.0 / spots))
    spot = token - frame * spots
    row = jnp.floor((spot + 0.5) * (1.0 / WB))
    return frame + first_frame, row, spot - row * WB


def attend_kernel(spots, windows_ref, q_ref, k_ref, v_ref, k_halo_ref, v_halo_ref, *refs):
    out_ref, bias = refs[-2:]
    rows = q_ref.shape[0]
    halo_rows = k_halo_ref.shape[0]
    keys = bias.shape[1]
    frames_here = rows // spots

    @pl.when(pl.program_id(0) == 0)
    def _():
        request = lax.axis_index("owner") // 2
        halo_frame = jnp.where(lax.axis_index("slab") == 0, 0, -HALO - frames_here).astype(jnp.float32)
        query = token_place(rows, 0, spots, 0.0)
        key = token_place(keys, 1, spots, 0.0)
        index = lax.broadcasted_iota(jnp.int32, (1, keys), 1)
        frame = jnp.where(index < rows, key[0], key[0] + halo_frame)
        frame = jnp.where(index < rows + halo_rows, frame, -NEG_LARGE)
        allowed = None
        for part, place in enumerate((frame, key[1], key[2])):
            near = jnp.abs(query[part] - place) <= windows_ref[request, part].astype(jnp.float32)
            allowed = near if allowed is None else allowed & near
        bias[...] = jnp.where(allowed, 0.0, NEG_LARGE)

    scale = math.log2(math.e) / math.sqrt(HEAD_DIM)
    pad = jnp.zeros((keys - rows - halo_rows, HEAD_DIM), jnp.bfloat16)
    ones = jnp.ones((keys, HEAD_DIM), jnp.bfloat16)
    for head in range(q_ref.shape[1] // HEAD_DIM):
        at = slice(head * HEAD_DIM, (head + 1) * HEAD_DIM)
        key = jnp.concatenate([k_ref[:, at], k_halo_ref[:, at], pad], axis=0)
        value = jnp.concatenate([v_ref[:, at], v_halo_ref[:, at], pad], axis=0)
        value = jnp.concatenate([value, ones], axis=1)
        score = lax.dot_general(q_ref[:, at], key, (((1,), (1,)), ((), ())), preferred_element_type=jnp.float32)
        score = score * scale + bias[...]
        weight = jnp.exp2(score - jnp.max(score, axis=1, keepdims=True)).astype(jnp.bfloat16)
        mixture = jnp.dot(weight, value, preferred_element_type=jnp.float32)
        out_ref[:, at] = (mixture[:, :HEAD_DIM] / mixture[:, HEAD_DIM:]).astype(jnp.bfloat16)


def attend(query_rows, key_value_rows, halo, windows, spots, part, attended):
    before = [] if attended is None else [attended]
    rows, features = query_rows.shape
    query_rows = pltpu.with_memory_space_constraint(query_rows, pltpu.HBM)
    width = features // PARTS
    heads = width // HEAD_DIM
    steps = 2 if heads % 2 == 0 else 1
    block = width // steps
    halo_rows = halo.shape[1]
    first = part * steps
    keys = pl.cdiv(rows + halo_rows, LANES) * LANES
    return pl.pallas_call(
        functools.partial(attend_kernel, spots),
        grid=(steps,),
        out_shape=jax.ShapeDtypeStruct((rows, features), jnp.bfloat16),
        in_specs=[
            IN_SMEM,
            pl.BlockSpec((rows, block), lambda i: (0, first + i)),
            pl.BlockSpec((None, rows, block), lambda i: (0, 0, first + i)),
            pl.BlockSpec((None, rows, block), lambda i: (1, 0, first + i)),
            pl.BlockSpec((None, halo_rows, block), lambda i: (0, 0, i)),
            pl.BlockSpec((None, halo_rows, block), lambda i: (1, 0, i)),
        ]
        + [ANYWHERE] * len(before),
        out_specs=pl.BlockSpec((rows, block), lambda i: (0, first + i)),
        input_output_aliases={6: 0} if before else {},
        scratch_shapes=[pltpu.VMEM((rows, keys), jnp.float32)],
        compiler_params=pltpu.CompilerParams(vmem_limit_bytes=10 * MIB),
        cost_estimate=pl.CostEstimate(
            flops=32 * rows * keys * width, bytes_accessed=2 * width * (2 * rows + 2 * keys), transcendentals=heads * rows * keys
        ),
        name="attend",
    )(windows, query_rows, key_value_rows, key_value_rows, halo, halo, *before)


def arrange_kernel(near_ref, far_ref, out_ref):
    rows = near_ref.shape[0]
    depth = out_ref.shape[2]
    for owner in range(out_ref.shape[0]):
        at = slice(owner * depth, (owner + 1) * depth)
        out_ref[owner, :rows] = near_ref[:, at]
        out_ref[owner, rows:] = far_ref[:, at]


def arrange(near, far, count):
    rows, features = near.shape
    return pl.pallas_call(
        arrange_kernel,
        out_shape=jax.ShapeDtypeStruct((count, 2 * rows, features // count), near.dtype),
        in_specs=[IN_VMEM] * 2,
        out_specs=IN_VMEM,
        compiler_params=pltpu.CompilerParams(vmem_limit_bytes=8 * MIB),
        cost_estimate=pl.CostEstimate(flops=0, bytes_accessed=8 * near.size, transcendentals=0),
        name="arrange",
    )(near, far)


def project_kernel(strip, column, total, begun, tables_ref, rows_ref, *refs):
    count = tables_ref.shape[2]
    w_refs, refs = refs[:count], refs[count:]
    sum_ref, refs = (refs[0], refs[1:]) if begun else (None, refs)
    owner, slab = lax.axis_index("owner"), lax.axis_index("slab")
    width = w_refs[0].shape[1]
    sources = [tables_ref[slab, owner, index] for index in range(count)]
    place = lax.axis_index("groups") * total + column + (1 - slab if strip else slab) * width
    for first in range(0, width, 2 * LANES):
        tile = min(2 * LANES, width - first)
        at = slice(first, first + tile)
        product = sum_ref[:, at] if begun else None
        for source, w_ref in zip(sources, w_refs):
            term = jnp.dot(rows_ref[source], w_ref[:, at], preferred_element_type=jnp.float32)
            product = term if product is None else product + term
        if len(refs) == 1:
            refs[0][:, at] = product
            continue
        here = pl.ds(pl.multiple_of(place + first, LANES), tile)
        rows = refs[2].shape[0]
        for block in range(2):
            gate = refs[block][:, here]
            result = product[block * rows : (block + 1) * rows] * gate
            refs[2 + block][:, at] = result.astype(jnp.bfloat16)


def project(table, arranged, chunks, begun, gates, strip, column, total):
    rows, depth = arranged.shape[1:]
    count, width = len(chunks), chunks[0].shape[1]
    begun = [] if begun is None else [begun]
    out_shape = jax.ShapeDtypeStruct((rows, width), jnp.float32)
    if gates:
        out_shape = [jax.ShapeDtypeStruct((rows // 2, width), jnp.bfloat16)] * 2
    return pl.pallas_call(
        functools.partial(project_kernel, strip, column, total, bool(begun)),
        out_shape=out_shape,
        in_specs=[IN_SMEM] + [IN_VMEM] * (1 + count + len(begun) + len(gates)),
        out_specs=[IN_VMEM] * 2 if gates else IN_VMEM,
        compiler_params=pltpu.CompilerParams(vmem_limit_bytes=16 * MIB),
        cost_estimate=pl.CostEstimate(
            flops=3 * rows * width * depth * count if gates else 0,
            bytes_accessed=2 * (rows * (depth * count + width) + count * depth * width) if gates else 0,
            transcendentals=0,
        ),
        name="project",
    )(table, arranged, *chunks, *begun, *gates)


def place_kernel(count, columns, total, *refs):
    in_refs, (out_ref, done) = refs[:count], refs[-2:]
    group, slab = lax.axis_index("groups"), lax.axis_index("slab")
    copies = []
    for index, in_ref in enumerate(in_refs):
        strip, away = divmod(index, 2)
        width = in_ref.shape[1]
        start = (1 - group if away else group) * total + columns[strip][0] + (1 - slab if columns[strip][1] else slab) * width
        at = pl.ds(pl.multiple_of(start, LANES), width)
        copies.append(pltpu.make_async_copy(in_ref, out_ref.at[:, at], done.at[index]))
    run_copies(copies)


def place(blocks, out, columns, total, model_width):
    rows = blocks[0].shape[0]
    held = [] if out is None else [out]
    return pl.pallas_call(
        functools.partial(place_kernel, len(blocks), columns, total),
        out_shape=jax.ShapeDtypeStruct((rows, model_width), jnp.bfloat16),
        in_specs=[IN_VMEM] * len(blocks) + [ANYWHERE] * len(held),
        out_specs=ANYWHERE,
        scratch_shapes=[pltpu.SemaphoreType.DMA((len(blocks),))],
        input_output_aliases={len(blocks): 0} if held else {},
        compiler_params=pltpu.CompilerParams(vmem_limit_bytes=4 * MIB),
        cost_estimate=pl.CostEstimate(flops=0, bytes_accessed=4 * sum(block.size for block in blocks), transcendentals=0),
        name="place",
    )(*blocks, *held)


def hop_order(pieces, turns):
    order = []
    for piece in range(pieces):
        hops = [(piece, strip, turn) for turn in range(1, turns[0] + 1) for strip in range(2) if turn <= turns[strip]]
        order = order[:-1] + hops[:1] + order[-1:] + hops[1:] if order else hops
    return order


def on_device(queries, key_value, keep, windows, gate, out_weight):
    frames_here, spots, features = queries.shape[1:]
    model_width = gate.shape[1]
    rows = frames_here * spots
    slabs = lax.axis_size("slab")
    total = model_width // lax.axis_size("groups")
    widths = piece_widths(total)

    count = lax.axis_size("owner")
    order = ring_order(count)
    spot_of = [order.index(owner) for owner in range(count)]
    ring = [
        (owner * slabs + slab, order[(spot_of[owner] + step) % count] * slabs + slab)
        for owner in range(count)
        for slab, step in enumerate((1, -1))
    ]
    turns = (count // 2, (count - 1) // 2)
    hops = hop_order(len(widths), turns)

    firsts = [2 * sum(widths[:piece]) for piece in range(len(widths))]
    held, arrived, crossed, edges = {}, [], {}, []
    for piece, width in enumerate(widths):
        own_strips, border = cut(out_weight, key_value, width, firsts[piece], total, piece == 0)
        edges = border or edges
        for strip, own in enumerate(own_strips):
            held[piece, strip, 0] = own

    def hop(slot, *others):
        if slot >= len(hops):
            return
        piece, strip, turn = hops[slot]
        waits = list(others)
        if slot >= FLIGHT:
            waits.append(arrived[slot - FLIGHT])
        if slot > 2 * FLIGHT:
            waits.append(crossed[hops[slot - 2 * FLIGHT - 1]])
        value = held[piece, strip, turn - 1]
        if waits:
            value = after(value, *waits)
        value = lax.ppermute(value, ("owner", "slab"), ring)
        held[hops[slot]] = value
        arrived.append(value)

    def cross(slot, *others):
        value = arrived[slot]
        crossed[hops[slot]] = swap(after(value, *others) if others else value, ("slab",))

    first_done = max(slot for slot, at in enumerate(hops) if at[0] == 0) if hops else 0
    halos = [swap(edge, ("slab",)) for edge in edges]
    for slot in range(FLIGHT):
        hop(slot)

    query_rows = queries.reshape(rows, features)
    key_value_rows = key_value.reshape(2, rows, features)
    waits, attended = {FLIGHT + 2: [held[piece, 0, 0] for piece in range(1, len(widths))]}, None
    for part in range(PARTS):
        attended = attend(query_rows, key_value_rows, halos[part], windows, spots, part, attended)
    a_blocks = (attended, swap(attended, ("groups",)))
    near_gate = scale_gate(after(keep, attended), gate)
    gates = (near_gate, swap(near_gate, ("groups",)))
    waits.setdefault(FLIGHT, []).append(attended)
    waits.setdefault(first_done, []).append(a_blocks[1])

    arranged = arrange(*a_blocks, count)

    begun = {}

    def project_strip(piece, strip, *others, final=True):
        sources = [(-turn, turn) for turn in range(turns[strip] + 1)]
        sources += [(turn, -turn) for turn in range(1, turns[1 - strip] + 1)]
        late = {len(sources) - 1, turns[strip]} if strip == 0 else {len(sources) - 1}
        batch = sorted(late if final else set(range(len(sources))) - late)
        if final and (piece, strip) not in begun:
            project_strip(piece, strip, final=False)
        if not batch:
            begun[piece, strip] = None
            return None
        chunks = [
            held[piece, strip, index] if index <= turns[strip] else crossed[piece, 1 - strip, index - turns[strip]]
            for index in batch
        ]
        table = np.zeros((slabs, count, len(batch)), np.int32)
        for slab in range(slabs):
            for owner in range(count):
                table[slab, owner] = [order[(spot_of[owner] + sources[index][slab]) % count] for index in batch]
        if others:
            chunks[0] = after(chunks[0], *others)
        before, gates_here = (begun[piece, strip], gates) if final else (None, ())
        result = project(jnp.asarray(table), arranged, chunks, before, gates_here, strip, firsts[piece], total)
        if not final:
            begun[piece, strip] = result
            return result
        return [result[0], swap(result[1], ("groups",))]

    results, needs = {}, {}
    if first_done >= 2 and first_done + 1 < len(hops):
        needs[first_done - 2] = [first_done - 1, gates[1], arranged]
    for slot in range(FLIGHT, len(hops)):
        strip = {first_done + 3: 0, first_done + 5: 1}.get(slot)
        if strip is not None:
            results[0, strip] = project_strip(0, strip, *(arrived[first_done + 1 : first_done + 2] if strip else []))
            waits.setdefault(slot, []).append(results[0, strip][0])
            if strip:
                needs[len(hops) - 2] = [results[0, strip][1]]
                waits[slot].append(arrived[slot - 1])
            else:
                needs[first_done + 1] = [results[0, strip][0]]
                waits.setdefault(len(hops) - 2, []).append(results[0, strip][1])
        if slot == first_done + FLIGHT - 1:
            needs[first_done - 1] = [project_strip(0, 1, final=False)]
        others = needs.get(slot - FLIGHT, [])
        cross(slot - FLIGHT, *(arrived[other] if isinstance(other, int) else other for other in others))
        hop(slot, *waits.get(slot, []))
    if len(hops) > 2 * FLIGHT and len(widths) > 1:
        sums = [project_strip(len(widths) - 1, strip, final=False) for strip in range(2)]
        needs[len(hops) - 2] = needs.get(len(hops) - 2, []) + sums
    for slot in range(max(len(hops) - FLIGHT, 0), len(hops)):
        cross(slot, *needs.get(slot, []))
    for piece in range(len(widths)):
        for strip in range(2):
            if (piece, strip) not in results:
                results[piece, strip] = project_strip(piece, strip)
    out = None
    last = (len(widths) - 1, 1)
    for batch in ([key for key in results if key != last], [last]):
        blocks = [block for key in batch for block in results[key]]
        out = place(blocks, out, [(firsts[piece], strip) for piece, strip in batch], total, model_width)
    return out.reshape((1, frames_here, spots, model_width))


def solution(mesh):
    placed = (
        P(("groups", "owner"), "slab", None, None),
        P(None, ("groups", "owner"), "slab", None, None),
        P("groups"),
        P("groups", None),
        P("groups", None),
        P("owner", None),
    )
    return jax.shard_map(
        on_device,
        mesh=mesh,
        in_specs=placed,
        out_specs=P(("groups", "owner"), "slab", None, None),
        check_vma=False,
    )
```
